128 devices in a mesh: load: 8 (over z_hi, y), space: 16 (over z_lo, x, core).
Axes of the slice: x: 4, y: 4, z: 4 (z_hi: 2, z_lo: 2; z = z_hi * 2 + z_lo), core: 2. Of those that a mesh axis runs over, the one named last changes fastest.
Arguments:
- density: float32 [32, 64, 256], P('space', 'load'), may hold values from 0.2 to 1
- fixed_dofs: int32 [3, 32, 64, 256], P(None, 'space'), may hold values 0 or 1
- body_loads: float32 [8, 3, 32, 64, 256], P('load', None, 'space'), may hold values from -6 to 6
- point_nodes: int32 [8, 128], P('load'), may hold values from 0 to 524287
- point_forces: float32 [8, 3, 128], P('load'), may hold values from -24 to 24
Outputs:
- displacement: float32 [8, 3, 32, 64, 256], P('load', None, 'space')
- filtered: float32 [32, 64, 256], P('space', 'load')
The draws below stay inside these ranges and needn't reach their ends.
All inputs are finite; a program needn't handle non-finite values. No bound on the sum of `fixed_dofs` on one device may be relied on, other than what follows from the above.
Results may differ from the reference program's by a relative error of at most 0.0003.
Values sent between devices are 32-bit elements; how exact they have to be, the bound alone decides.
No kernel may reach another device: no remote copies, remote signals or barrier semaphores. Data moves between devices by JAX's collectives and lax.ppermute only.
A program may use at most 64 MiB of HBM per device.

```python
import math
import jax
import jax.numpy as jnp
import numpy as np
from jax import lax

NY = 64
NZ = 256
POINTS = 128
ITERS = 3
LOADS = 8
NX = 32


def touch_ends(entries, stream_key, low, top_value):
    longest = entries.shape.index(max(entries.shape))
    spots = []
    for shift in (0, 1):
        where = [jax.random.randint(jax.random.fold_in(stream_key, axis), (), 0, length) for axis, length in enumerate(entries.shape)]
        where[longest] = (where[longest] + shift) % entries.shape[longest]
        spots.append(tuple(where))
    return entries.at[spots[0]].set(low).at[spots[1]].set(top_value)


def shard_levels(key, shape, cuts, smallest, top_value):
    level = 1.0
    for axis_at, blocks in cuts:
        heights = jax.random.uniform(jax.random.fold_in(jax.random.fold_in(key, 6), axis_at), (blocks,), jnp.float32, smallest / len(cuts), top_value / len(cuts))
        level = level * jnp.repeat(jnp.exp(heights), shape[axis_at] // blocks).reshape((-1,) + (1,) * (len(shape) - 1 - axis_at))
    return level


def normal_values(own_key, shape, width, limit, cuts=(), kind=jnp.bfloat16):
    entries = width * jax.random.normal(own_key, shape, jnp.float32)
    if cuts:
        entries = entries * shard_levels(own_key, shape, cuts, -0.22, 0.18)
    return jnp.clip(entries, -limit, limit).astype(kind)


def setup_inputs(seed: int = 0) -> dict:
    arg_keys = jax.random.split(jax.random.key(seed), 6)
    return {
        "density": jnp.clip(0.2 + 0.8 * jax.random.uniform(arg_keys[0], (NX, NY, NZ), jnp.float32) ** shard_levels(arg_keys[0], (NX, NY, NZ), ((0, 16), (1, 8)), -0.2, 0.2), 0.2, 1.0),
        "fixed_dofs": touch_ends((jax.random.randint(arg_keys[1], (3, NX, NY, NZ), 0, 16) < 1).astype(jnp.int32), jax.random.fold_in(arg_keys[1], 1), 0, 1),
        "body_loads": normal_values(arg_keys[2], (LOADS, 3, NX, NY, NZ), 1.0, 6.0, ((0, 8), (2, 16)), jnp.float32),
        "point_nodes": touch_ends(jax.random.randint(arg_keys[3], (LOADS, POINTS), 0, NX * NY * NZ), jax.random.fold_in(arg_keys[3], 1), 0, (NX * NY * NZ) - 1).astype(jnp.int32),
        "point_forces": normal_values(arg_keys[4], (LOADS, 3, POINTS), 4.0, 24.0, ((0, 8),), jnp.float32),
    }


EMIN = 0.001
PENALTY = 3.0
RADIUS = 1.5

def element_matrix():
    poisson = 0.3
    lame_first = poisson / ((1.0 + poisson) * (1.0 - 2.0 * poisson))
    shear_mod = 1.0 / (2.0 * (1.0 + poisson))
    elastic = np.zeros((6, 6))
    elastic[:3, :3] = lame_first
    for index in range(3):
        elastic[index, index] += 2.0 * shear_mod
        elastic[index + 3, index + 3] = shear_mod
    points = [0.5 - 0.5 / math.sqrt(3.0), 0.5 + 0.5 / math.sqrt(3.0)]
    stiffness = np.zeros((24, 24))
    for point_x in points:
        for point_y in points:
            for point_z in points:
                strain = np.zeros((6, 24))
                for corner in range(8):
                    along_x = corner & 1
                    along_y = corner >> 1 & 1
                    along_z = corner >> 2 & 1
                    shape_x = point_x if along_x else 1.0 - point_x
                    shape_y = point_y if along_y else 1.0 - point_y
                    shape_z = point_z if along_z else 1.0 - point_z
                    sign_x = 1.0 if along_x else -1.0
                    sign_y = 1.0 if along_y else -1.0
                    sign_z = 1.0 if along_z else -1.0
                    deriv_x = sign_x * shape_y * shape_z
                    deriv_y = shape_x * sign_y * shape_z
                    deriv_z = shape_x * shape_y * sign_z
                    strain[0, corner] = deriv_x
                    strain[1, 8 + corner] = deriv_y
                    strain[2, 16 + corner] = deriv_z
                    strain[3, corner] = deriv_y
                    strain[3, 8 + corner] = deriv_x
                    strain[4, 8 + corner] = deriv_z
                    strain[4, 16 + corner] = deriv_y
                    strain[5, corner] = deriv_z
                    strain[5, 16 + corner] = deriv_x
                stiffness += strain.T @ elastic @ strain / 8.0
    return stiffness

def pad_axis(array, axis_id, before, after):
    widths = [(0, 0)] * array.ndim
    widths[axis_id] = (before, after)
    return jnp.pad(array, widths)

def corners(padded, extent):
    pieces = []
    for component in range(3):
        for along_z in range(2):
            for along_y in range(2):
                for along_x in range(2):
                    pieces.append(padded[component, along_x:along_x + extent[0], along_y:along_y + extent[1], along_z:along_z + extent[2]])
    return jnp.stack(pieces)

def spread(values):
    parts = values.reshape((3, 2, 2, 2) + values.shape[1:])
    summed = pad_axis(parts[:, 0], 5, 0, 1) + pad_axis(parts[:, 1], 5, 1, 0)
    summed = pad_axis(summed[:, 0], 3, 0, 1) + pad_axis(summed[:, 1], 3, 1, 0)
    summed = pad_axis(summed[:, 0], 1, 0, 1) + pad_axis(summed[:, 1], 1, 1, 0)
    return summed

def element_forces(values, modulus, stiffness):
    flat_values = values.reshape(24, -1)
    forces = jnp.dot(stiffness, flat_values, precision=lax.Precision.HIGHEST)
    return forces.reshape(values.shape) * modulus

def smooth(padded, extent):
    result = jnp.zeros(extent, jnp.float32)
    for shift_x in (-1, 0, 1):
        for shift_y in (-1, 0, 1):
            for shift_z in (-1, 0, 1):
                distance = math.sqrt(shift_x * shift_x + shift_y * shift_y + shift_z * shift_z)
                if distance < RADIUS:
                    result = result + (RADIUS - distance) * padded[1 + shift_x:1 + shift_x + extent[0], 1 + shift_y:1 + shift_y + extent[1], 1 + shift_z:1 + shift_z + extent[2]]
    return result

def reference(density, fixed_dofs, body_loads, point_nodes, point_forces):
    stiffness = jnp.asarray(element_matrix(), jnp.float32)
    diag_entries = jnp.diagonal(stiffness)
    modulus = EMIN + (1.0 - EMIN) * density ** 3
    keep = 1.0 - fixed_dofs.astype(jnp.float32)
    extent = (NX, NY, NZ)

    def element_values(field):
        padded = pad_axis(pad_axis(pad_axis(field * keep, 1, 0, 1), 2, 0, 1), 3, 0, 1)
        return corners(padded, extent)

    def apply(field):
        forces = spread(element_forces(element_values(field), modulus, stiffness))[:, :NX, :NY, :NZ]
        return keep * forces + (1.0 - keep) * field
    diagonal = spread(modulus * diag_entries[:, None, None, None])[:, :NX, :NY, :NZ]
    jacobi = keep * diagonal + (1.0 - keep)
    energy = jnp.zeros((NX, NY, NZ), jnp.float32)
    displaced = []
    for load_case in range(LOADS):
        flat_loads = body_loads[load_case].reshape(3, -1).at[:, point_nodes[load_case]].add(point_forces[load_case])
        right_side = flat_loads.reshape(3, NX, NY, NZ) * keep
        iterate = jnp.zeros_like(right_side)
        residual = right_side
        precond = residual / jacobi
        direction = precond
        rz_now = jnp.sum(residual * precond)
        for iteration in range(ITERS):
            image = apply(direction)
            step_len = rz_now / jnp.sum(direction * image)
            iterate = iterate + step_len * direction
            residual = residual - step_len * image
            precond = residual / jacobi
            rz_next = jnp.sum(residual * precond)
            direction = precond + rz_next / rz_now * direction
            rz_now = rz_next
        displaced.append(iterate)
        values = element_values(iterate)
        energy = energy + lax.optimization_barrier(jnp.sum(values * element_forces(values, 1.0, stiffness), axis=0))
    sensitivity = -PENALTY * (1.0 - EMIN) * density ** 2 * energy
    weighted = density * sensitivity
    counts = smooth(jnp.pad(jnp.ones_like(density), 1), extent)
    filtered = smooth(jnp.pad(weighted, 1), extent) / (density * counts)
    return (jnp.stack(displaced), filtered)
```

```python
import math

import jax
import jax.numpy as jnp
from jax import lax
from jax.experimental import pallas as pl
from jax.experimental.pallas import tpu as pltpu
from jax.sharding import PartitionSpec as P

CX = 2
NY = 64
NZ = 256
ROWS = 8
CHUNKS = NY // ROWS
ZBITS = 8
EMIN = 0.001
PENALTY = 3.0
RADIUS = 1.5
POISSON = 0.3
LAME = POISSON / ((1.0 + POISSON) * (1.0 - 2.0 * POISSON))
SHEAR = 1.0 / (2.0 * (1.0 + POISSON))
KDIAG = (LAME + 4.0 * SHEAR) / 9.0
F32 = jnp.float32
VMEM_LIMIT = 56 * 1024 * 1024
PAIRS = ("ss", "sd", "ds", "dd")


def kernel_call(fn, outs, n_smem, n_in, scratch=()):
    vmem = pl.BlockSpec(memory_space=pltpu.VMEM)
    smem = pl.BlockSpec(memory_space=pltpu.SMEM)
    return pl.pallas_call(
        fn,
        out_shape=[jax.ShapeDtypeStruct(shape, F32) for shape in outs],
        in_specs=[smem] * n_smem + [vmem] * n_in,
        out_specs=[vmem] * len(outs),
        scratch_shapes=list(scratch),
        compiler_params=pltpu.CompilerParams(vmem_limit_bytes=VMEM_LIMIT),
    )


def lane_ids(shape):
    return lax.broadcasted_iota(jnp.int32, shape, 1)


def row_ids(shape):
    return lax.broadcasted_iota(jnp.int32, shape, 0)


def from_above(field):
    return jnp.where(lane_ids(field.shape) == NZ - 1, 0.0, pltpu.roll(field, NZ - 1, 1))


def from_below(field):
    return jnp.where(lane_ids(field.shape) == 0, 0.0, pltpu.roll(field, 1, 1))


def rows_at(chunk):
    return pl.ds(pl.multiple_of(chunk * ROWS, ROWS), ROWS)


def store_z_modes(zs_ref, zd_ref, plane, comp, rows, field):
    up = from_above(field)
    zs_ref[plane, comp, rows] = field + up
    zd_ref[plane, comp, rows] = up - field


def y_modes(cur, nxt):
    first = row_ids(cur.shape) == 0
    up = pltpu.roll(jnp.where(first, nxt, cur), ROWS - 1, 0)
    return cur + up, up - cur


def plane_modes(zs_ref, zd_ref, plane, chunk):
    out = []
    for comp in range(3):
        here, after = rows_at(chunk), rows_at(chunk + 1)
        ss, ds = y_modes(zs_ref[plane, comp, here], zs_ref[plane, comp, after])
        sd, dd = y_modes(zd_ref[plane, comp, here], zd_ref[plane, comp, after])
        out.append({"ss": ss, "sd": sd, "ds": ds, "dd": dd})
    return out


def element_modes(low, high):
    modes = []
    for comp in range(3):
        field = {}
        for pair in PAIRS:
            field["d" + pair] = high[comp][pair] - low[comp][pair]
            if pair != "ss":
                field["s" + pair] = high[comp][pair] + low[comp][pair]
        modes.append(field)
    return modes


NORMAL = ((0, "dss"), (1, "sds"), (2, "ssd"))
SHEARS = (((0, "sds"), (1, "dss")), ((0, "ssd"), (2, "dss")), ((1, "ssd"), (2, "sds")))
BENDS = (((0, "dsd"), (1, "sdd")), ((0, "dds"), (2, "sdd")), ((1, "dds"), (2, "dsd")))
TWISTS = ((0, "sdd"), (1, "dsd"), (2, "dds"))


def element_response(modes, modulus):
    k_lame = modulus * (LAME / 16.0)
    k_two = modulus * (SHEAR / 8.0)
    k_shear = modulus * (SHEAR / 16.0)
    k_bend = modulus * (LAME / 48.0)
    k_twist = modulus * (SHEAR / 48.0)
    k_last = modulus * ((LAME + 4.0 * SHEAR) / 144.0)
    force = [{}, {}, {}]
    get = lambda key: modes[key[0]][key[1]]
    trace = k_lame * (get(NORMAL[0]) + get(NORMAL[1]) + get(NORMAL[2]))
    for comp, name in NORMAL:
        force[comp][name] = k_two * modes[comp][name] + trace
    for one, two in SHEARS:
        both = k_shear * (get(one) + get(two))
        force[one[0]][one[1]] = both
        force[two[0]][two[1]] = both
    for one, two in BENDS:
        both = k_bend * (get(one) + get(two))
        force[one[0]][one[1]] = k_shear * get(one) + both
        force[two[0]][two[1]] = k_shear * get(two) + both
    total = get(TWISTS[0]) + get(TWISTS[1]) + get(TWISTS[2])
    for comp, name in TWISTS:
        force[comp][name] = k_twist * (modes[comp][name] + total)
    for comp in range(3):
        force[comp]["ddd"] = k_last * modes[comp]["ddd"]
    return force


def element_energy(modes):
    get = lambda key: modes[key[0]][key[1]]
    square = lambda value: value * value
    normal = [get(key) for key in NORMAL]
    twist = [get(key) for key in TWISTS]
    energy = (LAME / 16.0) * square(normal[0] + normal[1] + normal[2])
    energy += (SHEAR / 8.0) * (square(normal[0]) + square(normal[1]) + square(normal[2]))
    shear = sum(square(get(one) + get(two)) for one, two in SHEARS)
    shear += sum(square(get(one)) + square(get(two)) for one, two in BENDS)
    energy += (SHEAR / 16.0) * shear
    energy += (LAME / 48.0) * sum(square(get(one) + get(two)) for one, two in BENDS)
    twisted = square(twist[0]) + square(twist[1]) + square(twist[2])
    energy += (SHEAR / 48.0) * (twisted + square(twist[0] + twist[1] + twist[2]))
    last = square(modes[0]["ddd"]) + square(modes[1]["ddd"]) + square(modes[2]["ddd"])
    return energy + ((LAME + 4.0 * SHEAR) / 144.0) * last


def split_x(force):
    low, high = [], []
    for comp in range(3):
        lo, hi = {}, {}
        for pair in PAIRS:
            diff = force[comp]["d" + pair]
            if pair == "ss":
                lo[pair], hi[pair] = -diff, diff
            else:
                mean = force[comp]["s" + pair]
                lo[pair], hi[pair] = mean - diff, mean + diff
        low.append(lo)
        high.append(hi)
    return low, high


def node_force(acc, prev):
    sides = []
    for y_mode in ("s", "d"):
        mean, diff = acc[y_mode + "s"], acc[y_mode + "d"]
        sides.append((mean - diff) + from_below(mean + diff))
    low, high = sides[0] - sides[1], sides[0] + sides[1]
    last = row_ids(low.shape) == ROWS - 1
    return low + pltpu.roll(jnp.where(last, prev, high), 1, 0), high


def apply_rows(zs_ref, zd_ref, planes, e_ref, e_first, e_pad, carry_ref, chunk):
    low = plane_modes(zs_ref, zd_ref, 0, chunk)
    partial = None
    for plane in range(planes - 1):
        high = plane_modes(zs_ref, zd_ref, plane + 1, chunk)
        modulus = e_ref[e_first + plane, rows_at(chunk + e_pad)]
        to_low, to_high = split_x(element_response(element_modes(low, high), modulus))
        if partial is not None:
            forces = []
            for comp in range(3):
                acc = {pair: partial[comp][pair] + to_low[comp][pair] for pair in PAIRS}
                force, carry = node_force(acc, carry_ref[plane - 1, comp])
                carry_ref[plane - 1, comp] = carry
                forces.append(force)
            yield plane, forces
        partial, low = to_high, high


def loads_kernel(space_ref, body_ref, fixed_ref, node_ref, force_ref, all_ref, right_ref, far_ref):
    cells = CX * NY * NZ
    local = node_ref[...] - space_ref[0] * cells
    valid = (local >= 0) & (local < cells)
    local = jnp.where(valid, local, -1)
    line = lax.shift_right_arithmetic(local, ZBITS)
    depth = lax.bitwise_and(local, NZ - 1)
    points = local.shape[1]
    on_line = row_ids((CX * NY, points)) == line
    lines = [jnp.where(on_line, force_ref[comp : comp + 1, :], 0.0) for comp in range(3)]
    at_depth = jnp.where(row_ids((NZ, points)) == depth, 1.0, 0.0)
    added = lax.dot_general(
        jnp.concatenate(lines, axis=0),
        at_depth,
        (((1,), (1,)), ((), ())),
        precision=lax.Precision.HIGHEST,
        preferred_element_type=F32,
    )
    for plane in range(CX):
        for comp in range(3):
            keep = 1.0 - fixed_ref[comp, plane].astype(F32)
            first = (comp * CX + plane) * NY
            load = keep * (body_ref[comp, plane] + added[first : first + NY])
            all_ref[plane, comp] = load
            right_ref[plane, comp] = load
            all_ref[3 - plane, comp] = keep
            if plane == 0:
                far_ref[0, comp] = load
            else:
                right_ref[2, comp] = keep


def krylov_kernel(
    space_ref, own_ref, left_ref, right_ref, far_ref, dens_ref,
    v0_ref, v1_ref, v2_ref, edge_ref, mom_ref,
    e_ref, inv_ref, zs0, zd0, zs1, zd1, zs2, zd2, carry1, carry2,
):
    first_x = space_ref[0] * CX
    limit = space_ref[1] * CX
    zero_rows = jnp.zeros((ROWS, NZ), F32)
    for plane in range(8):
        at = first_x - 3 + plane
        scale = jnp.where((at >= 0) & (at < limit), 1.0, 0.0).astype(F32)
        e_ref[plane, 0:ROWS] = zero_rows
        for block in range(CHUNKS):
            dens = dens_ref[block, plane]
            rows = slice((block + 1) * ROWS, (block + 2) * ROWS)
            e_ref[plane, rows] = scale * (EMIN + (1.0 - EMIN) * (dens * dens * dens))
    tail = slice(NY, NY + ROWS)
    for comp in range(3):
        for refs, planes in (((zs0, zd0), 7), ((zs1, zd1), 5), ((zs2, zd2), 3)):
            for ref in refs:
                for plane in range(planes):
                    ref[plane, comp, tail] = zero_rows
        for ref, planes in ((carry1, 5), (carry2, 3)):
            for plane in range(planes):
                ref[plane, comp] = zero_rows

    loads = [left_ref.at[0], left_ref.at[1], own_ref.at[0], own_ref.at[1],
             right_ref.at[0], right_ref.at[1], far_ref.at[0]]
    keeps = [left_ref.at[2], own_ref.at[3], own_ref.at[2], right_ref.at[3], right_ref.at[2]]

    def start(chunk, total):
        here = rows_at(chunk)
        last = row_ids((ROWS, NZ)) == ROWS - 1
        for plane in range(7):
            cur = e_ref[plane, rows_at(chunk + 1)] + e_ref[plane + 1, rows_at(chunk + 1)]
            before = e_ref[plane, rows_at(chunk)] + e_ref[plane + 1, rows_at(chunk)]
            cur = cur + pltpu.roll(jnp.where(last, before, cur), 1, 0)
            diag = KDIAG * (cur + from_below(cur))
            inverse = 1.0 / jnp.where(diag > 0.0, diag, 1.0)
            if 1 <= plane <= 5:
                inv_ref[plane - 1, here] = inverse
            for comp in range(3):
                load = loads[plane][comp, here]
                value = load * inverse
                if 1 <= plane <= 5:
                    v0_ref[plane - 1, comp, here] = value
                if plane in (2, 3):
                    total = total + load * value
                store_z_modes(zs0, zd0, plane, comp, here, value)
        return total

    zero = jnp.zeros((ROWS, NZ), F32)
    mom0 = lax.fori_loop(0, CHUNKS, start, zero)

    def first(chunk, totals):
        here = rows_at(chunk)
        odd, even = totals
        for plane, forces in apply_rows(zs0, zd0, 7, e_ref, 1, 1, carry1, chunk):
            inverse = inv_ref[plane - 1, here]
            for comp in range(3):
                kept = keeps[plane - 1][comp, here] > 0.0
                before = v0_ref[plane - 1, comp, here]
                image = jnp.where(kept, forces[comp], before)
                value = jnp.where(kept, forces[comp] * inverse, before)
                v1_ref[plane - 1, comp, here] = value
                store_z_modes(zs1, zd1, plane - 1, comp, here, value)
                if plane in (2, 3):
                    odd = odd + before * image
                    even = even + value * image
        return odd, even

    mom1, mom2 = lax.fori_loop(0, CHUNKS, first, (zero, zero))

    def second(chunk, totals):
        here = rows_at(chunk)
        odd, even = totals
        for plane, forces in apply_rows(zs1, zd1, 5, e_ref, 2, 1, carry2, chunk):
            inverse = inv_ref[plane, here]
            for comp in range(3):
                kept = keeps[plane][comp, here] > 0.0
                before = v1_ref[plane, comp, here]
                image = jnp.where(kept, forces[comp], before)
                value = jnp.where(kept, forces[comp] * inverse, before)
                v2_ref[plane - 1, comp, here] = value
                if plane == 2:
                    edge_ref[comp, here] = value
                store_z_modes(zs2, zd2, plane - 1, comp, here, value)
                if plane in (1, 2):
                    odd = odd + before * image
                    even = even + value * image
        return odd, even

    mom3, mom4 = lax.fori_loop(0, CHUNKS, second, (zero, zero))

    def third(chunk, total):
        low = plane_modes(zs2, zd2, 0, chunk)
        for plane in range(2):
            high = plane_modes(zs2, zd2, plane + 1, chunk)
            energy = element_energy(element_modes(low, high))
            total = total + e_ref[3 + plane, rows_at(chunk + 1)] * energy
            low = high
        return total

    mom5 = lax.fori_loop(0, CHUNKS, third, zero)
    rows = []
    for value in (mom0, mom1, mom2, mom3, mom4, mom5, zero, zero):
        rows.append(jnp.sum(value[:, :128] + value[:, 128:], axis=0, keepdims=True))
    mom_ref[...] = jnp.concatenate(rows, axis=0)


def energy_kernel(v0_ref, v1_ref, v2_ref, left_ref, right_ref, mom_ref, u_ref, out_ref, zs, zd, e_ref):
    total = mom_ref[0]
    for device in range(1, mom_ref.shape[0]):
        total = total + mom_ref[device]
    total = jnp.broadcast_to(jnp.sum(total, axis=1, keepdims=True), (8, 128))
    m0, m1, m2, m3, m4, m5 = [total[k : k + 1] for k in range(6)]
    low10 = m2 / m1
    low20 = m3 / m1
    piv1 = m3 - low10 * m2
    mix = m4 - low20 * m2
    good1 = piv1 > 1e-7 * m3
    safe1 = jnp.where(good1, piv1, 1.0)
    low21 = jnp.where(good1, mix / safe1, 0.0)
    piv2 = m5 - low20 * m3 - low21 * mix
    good2 = good1 & (piv2 > 1e-7 * m5)
    y1 = m1 - low10 * m0
    y2 = m2 - low20 * m0 - low21 * y1
    c2 = jnp.where(good2, y2 / jnp.where(good2, piv2, 1.0), 0.0)
    c1 = jnp.where(good1, y1 / safe1 - low21 * c2, 0.0)
    c0 = m0 / m1 - low10 * c1 - low20 * c2
    c0, c1, c2 = [jnp.broadcast_to(jnp.concatenate([c, c], axis=1), (ROWS, NZ)) for c in (c0, c1, c2)]

    zero_rows = jnp.zeros((ROWS, NZ), F32)
    for plane in range(5):
        for comp in range(3):
            zs[plane, comp, NY : NY + ROWS] = zero_rows
            zd[plane, comp, NY : NY + ROWS] = zero_rows
    for plane in range(4):
        e_ref[plane, 0:ROWS] = zero_rows
        e_ref[plane, NY + ROWS : NY + 2 * ROWS] = zero_rows
    v2_planes = [left_ref, v2_ref.at[0], v2_ref.at[1], v2_ref.at[2], right_ref]

    def combine(chunk, done):
        here = rows_at(chunk)
        for plane in range(5):
            for comp in range(3):
                value = c0 * v0_ref[plane, comp, here] + c1 * v1_ref[plane, comp, here]
                value = value + c2 * v2_planes[plane][comp, here]
                if plane in (1, 2):
                    u_ref[comp, plane - 1, here] = value
                store_z_modes(zs, zd, plane, comp, here, value)
        return done

    lax.fori_loop(0, CHUNKS, combine, 0)

    def measure(chunk, done):
        low = plane_modes(zs, zd, 0, chunk)
        for plane in range(4):
            high = plane_modes(zs, zd, plane + 1, chunk)
            e_ref[plane, rows_at(chunk + 1)] = element_energy(element_modes(low, high))
            low = high
        return done

    lax.fori_loop(0, CHUNKS, measure, 0)
    span = ROWS + 2
    for block in range(CHUNKS):
        for plane in range(4):
            first = ROWS - 1 + block * ROWS
            out_ref[block, plane * span : (plane + 1) * span] = e_ref[plane, first : first + span]


def weigh(planes):
    near = RADIUS - 1.0
    edge = RADIUS - math.sqrt(2.0)
    beside = [from_below(p) + from_above(p) for p in planes]
    cross = []
    full = []
    for p, side in zip(planes, beside):
        up_down = p[0:ROWS] + p[2 : 2 + ROWS]
        mid, mid_side = p[1 : 1 + ROWS], side[1 : 1 + ROWS]
        cross.append(near * mid + edge * (mid_side + up_down))
        diagonal = side[0:ROWS] + side[2 : 2 + ROWS]
        full.append(RADIUS * mid + near * (mid_side + up_down) + edge * diagonal)
    return [full[k] + cross[k - 1] + cross[k + 1] for k in range(1, 1 + CX)]


def filter_kernel(place_ref, energy_ref, dens_ref, out_ref):
    space, n_space, load, n_load = [place_ref[k] for k in range(4)]
    total = energy_ref[0]
    for block in range(1, energy_ref.shape[0]):
        total = total + energy_ref[block]
    span = ROWS + 2
    before = jnp.maximum(load - 1, 0)
    after = jnp.minimum(load + 1, n_load - 1)
    at_y = load * ROWS - 1 + row_ids((span, NZ))
    in_y = (at_y >= 0) & (at_y < n_load * ROWS)
    weighted, inside, own = [], [], []
    for plane in range(4):
        dens = jnp.concatenate(
            [
                dens_ref[before, 2 + plane][ROWS - 1 : ROWS],
                dens_ref[load, 2 + plane],
                dens_ref[after, 2 + plane][0:1],
            ],
            axis=0,
        )
        at_x = space * CX - 1 + plane
        scale = jnp.where((at_x >= 0) & (at_x < n_space * CX), 1.0, 0.0).astype(F32)
        present = scale * jnp.where(in_y, 1.0, 0.0)
        energy = total[plane * span : (plane + 1) * span]
        sensitivity = -PENALTY * (1.0 - EMIN) * (dens * dens) * energy
        weighted.append(present * (dens * sensitivity))
        inside.append(present)
        if 1 <= plane <= CX:
            own.append(dens[1 : 1 + ROWS])
    sums, counts = weigh(weighted), weigh(inside)
    for plane in range(CX):
        out_ref[plane] = sums[plane] / (own[plane] * counts[plane])


def shifted(array, axis, distance):
    size = lax.axis_size(axis)
    route = [(i, i + distance) for i in range(size) if 0 <= i + distance < size]
    return lax.ppermute(array, axis, route)


def body(density, fixed_dofs, body_loads, point_nodes, point_forces):
    n_load, n_space = lax.axis_size("load"), lax.axis_size("space")
    load, space = lax.axis_index("load"), lax.axis_index("space")
    place = jnp.stack([space, jnp.int32(n_space), load, jnp.int32(n_load)]).astype(jnp.int32)
    plane = (3, NY, NZ)
    own, to_right, to_far = kernel_call(
        loads_kernel, [(4,) + plane, (3,) + plane, (1,) + plane], 1, 4
    )(place, body_loads[0], fixed_dofs, point_nodes, point_forces[0])
    dens = jnp.concatenate(
        [
            shifted(density[1:2], "space", 2),
            shifted(density, "space", 1),
            density,
            shifted(density, "space", -1),
            shifted(density[0:1], "space", -2),
        ],
        axis=0,
    )
    left = shifted(to_right, "space", 1)
    right = shifted(own, "space", -1)
    far = shifted(to_far, "space", -2)
    dens = lax.all_to_all(jnp.broadcast_to(dens[None], (n_load,) + dens.shape), "load", 0, 0)

    padded = (NY + ROWS, NZ)
    zed = lambda planes: pltpu.VMEM((planes, 3) + padded, F32)
    v0, v1, v2, edge, mom = kernel_call(
        krylov_kernel,
        [(5,) + plane, (5,) + plane, (3,) + plane, plane, (8, 128)],
        1,
        5,
        [pltpu.VMEM((8,) + padded, F32), pltpu.VMEM((5, NY, NZ), F32)]
        + [zed(7), zed(7), zed(5), zed(5), zed(3), zed(3)]
        + [pltpu.VMEM((5, 3, ROWS, NZ), F32), pltpu.VMEM((3, 3, ROWS, NZ), F32)],
    )(place, own, left, right, far, dens)
    edge_left = shifted(edge, "space", 1)
    edge_right = shifted(edge, "space", -1)
    mom = lax.all_to_all(jnp.broadcast_to(mom[None], (n_space,) + mom.shape), "space", 0, 0)
    moved, energy = kernel_call(
        energy_kernel,
        [(3, CX, NY, NZ), (CHUNKS, 4 * (ROWS + 2), NZ)],
        0,
        6,
        [zed(5), zed(5), pltpu.VMEM((4, NY + 2 * ROWS, NZ), F32)],
    )(v0, v1, v2, edge_left, edge_right, mom)
    energy = lax.all_to_all(energy, "load", 0, 0)
    (filtered,) = kernel_call(filter_kernel, [(CX, ROWS, NZ)], 1, 2)(place, energy, dens)
    return (moved[None], filtered)


def solution(mesh):
    placed = (
        P("space", "load", None),
        P(None, "space", None, None),
        P("load", None, "space", None, None),
        P("load", None),
        P("load", None, None),
    )
    return jax.shard_map(
        body,
        mesh=mesh,
        in_specs=placed,
        out_specs=(P("load", None, "space", None, None), P("space", "load", None)),
        check_vma=False,
    )
```

```python
import math

import jax
import jax.numpy as jnp
from jax import lax
from jax.experimental import pallas as pl
from jax.experimental.pallas import tpu as pltpu
from jax.sharding import PartitionSpec as P

CX = 2
NY = 64
NZ = 256
ROWS = 8
CHUNKS = NY // ROWS
ZBITS = 8
EMIN = 0.001
PENALTY = 3.0
RADIUS = 1.5
POISSON = 0.3
LAME = POISSON / ((1.0 + POISSON) * (1.0 - 2.0 * POISSON))
SHEAR = 1.0 / (2.0 * (1.0 + POISSON))
KDIAG = (LAME + 4.0 * SHEAR) / 9.0
F32 = jnp.float32
VMEM_LIMIT = 56 * 1024 * 1024
PAIRS = ("ss", "sd", "ds", "dd")


def kernel_call(fn, outs, n_smem, n_in, scratch=()):
    vmem = pl.BlockSpec(memory_space=pltpu.VMEM)
    smem = pl.BlockSpec(memory_space=pltpu.SMEM)
    return pl.pallas_call(
        fn,
        out_shape=[jax.ShapeDtypeStruct(shape, F32) for shape in outs],
        in_specs=[smem] * n_smem + [vmem] * n_in,
        out_specs=[vmem] * len(outs),
        scratch_shapes=list(scratch),
        compiler_params=pltpu.CompilerParams(vmem_limit_bytes=VMEM_LIMIT),
    )


def lane_ids(shape):
    return lax.broadcasted_iota(jnp.int32, shape, 1)


def row_ids(shape):
    return lax.broadcasted_iota(jnp.int32, shape, 0)


def from_above(field):
    return jnp.where(lane_ids(field.shape) == NZ - 1, 0.0, pltpu.roll(field, NZ - 1, 1))


def from_below(field):
    return jnp.where(lane_ids(field.shape) == 0, 0.0, pltpu.roll(field, 1, 1))


def rows_at(chunk):
    return pl.ds(pl.multiple_of(chunk * ROWS, ROWS), ROWS)


def store_z_modes(zs_ref, zd_ref, plane, comp, rows, field):
    up = from_above(field)
    zs_ref[plane, comp, rows] = field + up
    zd_ref[plane, comp, rows] = up - field


def y_modes(cur, nxt):
    first = row_ids(cur.shape) == 0
    up = pltpu.roll(jnp.where(first, nxt, cur), ROWS - 1, 0)
    return cur + up, up - cur


def plane_modes(zs_ref, zd_ref, plane, chunk):
    out = []
    for comp in range(3):
        here, after = rows_at(chunk), rows_at(chunk + 1)
        ss, ds = y_modes(zs_ref[plane, comp, here], zs_ref[plane, comp, after])
        sd, dd = y_modes(zd_ref[plane, comp, here], zd_ref[plane, comp, after])
        out.append({"ss": ss, "sd": sd, "ds": ds, "dd": dd})
    return out


def element_modes(low, high):
    modes = []
    for comp in range(3):
        field = {}
        for pair in PAIRS:
            field["d" + pair] = high[comp][pair] - low[comp][pair]
            if pair != "ss":
                field["s" + pair] = high[comp][pair] + low[comp][pair]
        modes.append(field)
    return modes


NORMAL = ((0, "dss"), (1, "sds"), (2, "ssd"))
SHEARS = (((0, "sds"), (1, "dss")), ((0, "ssd"), (2, "dss")), ((1, "ssd"), (2, "sds")))
BENDS = (((0, "dsd"), (1, "sdd")), ((0, "dds"), (2, "sdd")), ((1, "dds"), (2, "dsd")))
TWISTS = ((0, "sdd"), (1, "dsd"), (2, "dds"))


def element_response(modes, modulus):
    k_lame = modulus * (LAME / 16.0)
    k_two = modulus * (SHEAR / 8.0)
    k_shear = modulus * (SHEAR / 16.0)
    k_bend = modulus * (LAME / 48.0)
    k_twist = modulus * (SHEAR / 48.0)
    k_last = modulus * ((LAME + 4.0 * SHEAR) / 144.0)
    force = [{}, {}, {}]
    get = lambda key: modes[key[0]][key[1]]
    trace = k_lame * (get(NORMAL[0]) + get(NORMAL[1]) + get(NORMAL[2]))
    for comp, name in NORMAL:
        force[comp][name] = k_two * modes[comp][name] + trace
    for one, two in SHEARS:
        both = k_shear * (get(one) + get(two))
        force[one[0]][one[1]] = both
        force[two[0]][two[1]] = both
    for one, two in BENDS:
        both = k_bend * (get(one) + get(two))
        force[one[0]][one[1]] = k_shear * get(one) + both
        force[two[0]][two[1]] = k_shear * get(two) + both
    total = get(TWISTS[0]) + get(TWISTS[1]) + get(TWISTS[2])
    for comp, name in TWISTS:
        force[comp][name] = k_twist * (modes[comp][name] + total)
    for comp in range(3):
        force[comp]["ddd"] = k_last * modes[comp]["ddd"]
    return force


def element_energy(modes):
    get = lambda key: modes[key[0]][key[1]]
    square = lambda value: value * value
    normal = [get(key) for key in NORMAL]
    twist = [get(key) for key in TWISTS]
    energy = (LAME / 16.0) * square(normal[0] + normal[1] + normal[2])
    energy += (SHEAR / 8.0) * (square(normal[0]) + square(normal[1]) + square(normal[2]))
    shear = sum(square(get(one) + get(two)) for one, two in SHEARS)
    shear += sum(square(get(one)) + square(get(two)) for one, two in BENDS)
    energy += (SHEAR / 16.0) * shear
    energy += (LAME / 48.0) * sum(square(get(one) + get(two)) for one, two in BENDS)
    twisted = square(twist[0]) + square(twist[1]) + square(twist[2])
    energy += (SHEAR / 48.0) * (twisted + square(twist[0] + twist[1] + twist[2]))
    last = square(modes[0]["ddd"]) + square(modes[1]["ddd"]) + square(modes[2]["ddd"])
    return energy + ((LAME + 4.0 * SHEAR) / 144.0) * last


def split_x(force):
    low, high = [], []
    for comp in range(3):
        lo, hi = {}, {}
        for pair in PAIRS:
            diff = force[comp]["d" + pair]
            if pair == "ss":
                lo[pair], hi[pair] = -diff, diff
            else:
                mean = force[comp]["s" + pair]
                lo[pair], hi[pair] = mean - diff, mean + diff
        low.append(lo)
        high.append(hi)
    return low, high


def node_force(acc, prev):
    sides = []
    for y_mode in ("s", "d"):
        mean, diff = acc[y_mode + "s"], acc[y_mode + "d"]
        sides.append((mean - diff) + from_below(mean + diff))
    low, high = sides[0] - sides[1], sides[0] + sides[1]
    last = row_ids(low.shape) == ROWS - 1
    return low + pltpu.roll(jnp.where(last, prev, high), 1, 0), high


def apply_rows(zs_ref, zd_ref, planes, e_ref, e_first, e_pad, carry_ref, chunk):
    low = plane_modes(zs_ref, zd_ref, 0, chunk)
    partial = None
    for plane in range(planes - 1):
        high = plane_modes(zs_ref, zd_ref, plane + 1, chunk)
        modulus = e_ref[e_first + plane, rows_at(chunk + e_pad)]
        to_low, to_high = split_x(element_response(element_modes(low, high), modulus))
        if partial is not None:
            forces = []
            for comp in range(3):
                acc = {pair: partial[comp][pair] + to_low[comp][pair] for pair in PAIRS}
                force, carry = node_force(acc, carry_ref[plane - 1, comp])
                carry_ref[plane - 1, comp] = carry
                forces.append(force)
            yield plane, forces
        partial, low = to_high, high


def loads_kernel(
    body_ref, fixed_ref, node_ref, force_ref, load_ref, keep_ref, right_ref, left_ref
):
    cells = CX * NY * NZ
    local = node_ref[...] - lax.axis_index("space") * cells
    valid = (local >= 0) & (local < cells)
    local = jnp.where(valid, local, -1)
    line = lax.shift_right_arithmetic(local, ZBITS)
    depth = lax.bitwise_and(local, NZ - 1)
    points = local.shape[1]
    on_line = row_ids((CX * NY, points)) == line
    lines = [jnp.where(on_line, force_ref[comp : comp + 1, :], 0.0) for comp in range(3)]
    at_depth = jnp.where(row_ids((NZ, points)) == depth, 1.0, 0.0)
    added = lax.dot_general(
        jnp.concatenate(lines, axis=0),
        at_depth,
        (((1,), (1,)), ((), ())),
        precision=lax.Precision.HIGHEST,
        preferred_element_type=F32,
    )
    for plane in range(CX):
        for comp in range(3):
            keep = 1.0 - fixed_ref[comp, plane].astype(F32)
            first = (comp * CX + plane) * NY
            load = keep * (body_ref[comp, plane] + added[first : first + NY])
            load_ref[plane, comp] = load
            keep_ref[plane, comp] = keep
            left_ref[plane, comp] = load
            if plane == 0:
                left_ref[2, comp] = keep
            else:
                right_ref[0, comp] = load
                right_ref[1, comp] = keep


def clear_tails(refs):
    for ref in refs:
        for plane in range(ref.shape[0]):
            for comp in range(3):
                ref[plane, comp, NY : NY + ROWS] = jnp.zeros((ROWS, NZ), F32)


def clear_carry(ref):
    for plane in range(ref.shape[0]):
        for comp in range(3):
            ref[plane, comp] = jnp.zeros((ROWS, NZ), F32)


def folded(values):
    rows = [jnp.sum(v[:, :128] + v[:, 128:], axis=0, keepdims=True) for v in values]
    return jnp.concatenate(rows, axis=0)


def advance(forces, kept, before, inverse):
    image = jnp.where(kept, forces, before)
    return image, jnp.where(kept, forces * inverse, before)


def first_kernel(
    load_ref, keep_ref, left_ref, right_ref, dens_ref,
    v0_ref, v1_ref, v1_far_ref, e_ref, inv_ref, mom_ref,
    zs, zd, carry,
):
    first_x = lax.axis_index("space") * CX
    limit = lax.axis_size("space") * CX
    for plane in range(6):
        at = first_x - 2 + plane
        scale = jnp.where((at >= 0) & (at < limit), 1.0, 0.0).astype(F32)
        e_ref[plane, 0:ROWS] = jnp.zeros((ROWS, NZ), F32)
        for block in range(CHUNKS):
            dens = dens_ref[block, plane]
            rows = slice((block + 1) * ROWS, (block + 2) * ROWS)
            e_ref[plane, rows] = scale * (EMIN + (1.0 - EMIN) * (dens * dens * dens))
    clear_tails([zs, zd])
    clear_carry(carry)
    loads = [left_ref.at[0], load_ref.at[0], load_ref.at[1], right_ref.at[0], right_ref.at[1]]
    keeps = [keep_ref.at[0], keep_ref.at[1], right_ref.at[2]]
    zero = jnp.zeros((ROWS, NZ), F32)

    def start(chunk, total):
        here = rows_at(chunk)
        last = row_ids((ROWS, NZ)) == ROWS - 1
        for plane in range(5):
            cur = e_ref[plane, rows_at(chunk + 1)] + e_ref[plane + 1, rows_at(chunk + 1)]
            before = e_ref[plane, rows_at(chunk)] + e_ref[plane + 1, rows_at(chunk)]
            cur = cur + pltpu.roll(jnp.where(last, before, cur), 1, 0)
            diag = KDIAG * (cur + from_below(cur))
            inverse = 1.0 / jnp.where(diag > 0.0, diag, 1.0)
            if plane < 4:
                inv_ref[plane, here] = inverse
            for comp in range(3):
                load = loads[plane][comp, here]
                value = load * inverse
                if plane < 3:
                    v0_ref[plane, comp, here] = value
                if plane in (1, 2):
                    total = total + load * value
                store_z_modes(zs, zd, plane, comp, here, value)
        return total

    mom0 = lax.fori_loop(0, CHUNKS, start, zero)

    def apply(chunk, totals):
        here = rows_at(chunk)
        odd, even = totals
        for plane, forces in apply_rows(zs, zd, 5, e_ref, 1, 1, carry, chunk):
            inverse = inv_ref[plane, here]
            for comp in range(3):
                kept = keeps[plane - 1][comp, here] > 0.0
                before = loads[plane][comp, here] * inverse
                image, value = advance(forces[comp], kept, before, inverse)
                if plane < 3:
                    v1_ref[plane - 1, comp, here] = value
                    odd = odd + before * image
                    even = even + value * image
                else:
                    v1_far_ref[comp, here] = value
        return odd, even

    mom1, mom2 = lax.fori_loop(0, CHUNKS, apply, (zero, zero))
    mom_ref[...] = folded([mom0, mom1, mom2] + [zero] * 5)


def second_kernel(
    v1_left_ref, v1_ref, v1_far_ref, keep_left_ref, keep_ref, e_ref, inv_ref, sofar_ref,
    v2_ref, mom_ref,
    zs, zd, zs2, zd2, carry,
):
    v1_planes = [v1_left_ref.at[0], v1_left_ref.at[1], v1_ref.at[0], v1_ref.at[1], v1_far_ref]
    keeps = [keep_left_ref.at[1], keep_ref.at[0], keep_ref.at[1]]
    clear_tails([zs, zd, zs2, zd2])
    clear_carry(carry)
    zero = jnp.zeros((ROWS, NZ), F32)

    def start(chunk, done):
        here = rows_at(chunk)
        for plane in range(5):
            for comp in range(3):
                store_z_modes(zs, zd, plane, comp, here, v1_planes[plane][comp, here])
        return done

    lax.fori_loop(0, CHUNKS, start, 0)

    def apply(chunk, totals):
        here = rows_at(chunk)
        odd, even = totals
        for plane, forces in apply_rows(zs, zd, 5, e_ref, 0, 1, carry, chunk):
            inverse = inv_ref[plane - 1, here]
            for comp in range(3):
                kept = keeps[plane - 1][comp, here] > 0.0
                before = v1_planes[plane][comp, here]
                image, value = advance(forces[comp], kept, before, inverse)
                v2_ref[plane - 1, comp, here] = value
                store_z_modes(zs2, zd2, plane - 1, comp, here, value)
                if plane > 1:
                    odd = odd + before * image
                    even = even + value * image
        return odd, even

    mom3, mom4 = lax.fori_loop(0, CHUNKS, apply, (zero, zero))
    at_end = end_flag()

    def last(chunk, total):
        for plane, energy in enumerate(energies(zs2, zd2, chunk)):
            total = total + (e_ref[1 + plane, rows_at(chunk + 1)] * energy) * (at_end if plane == 2 else 1.0)
        return total

    mom5 = lax.fori_loop(0, CHUNKS, last, zero)
    total = sofar_ref[...] + folded([zero] * 3 + [mom3, mom4, mom5] + [zero] * 2)
    for device in range(mom_ref.shape[0]):
        mom_ref[device] = total


def end_flag():
    at_end = lax.axis_index("space") == lax.axis_size("space") - 1
    return jnp.where(at_end, 1.0, 0.0).astype(F32)


def energies(zs, zd, chunk):
    planes = [plane_modes(zs, zd, plane, chunk) for plane in range(3)]
    zero = {pair: jnp.zeros((ROWS, NZ), F32) for pair in PAIRS}
    planes.append([zero] * 3)
    for low, high in zip(planes[:-1], planes[1:]):
        yield element_energy(element_modes(low, high))


def energy_kernel(v0_ref, v1_left_ref, v1_ref, v2_ref, mom_ref, u_ref, out_ref, zs, zd, e_ref):
    total = mom_ref[0]
    for device in range(1, mom_ref.shape[0]):
        total = total + mom_ref[device]
    total = jnp.broadcast_to(jnp.sum(total, axis=1, keepdims=True), (8, 128))
    m0, m1, m2, m3, m4, m5 = [total[k : k + 1] for k in range(6)]
    low10 = m2 / m1
    low20 = m3 / m1
    piv1 = m3 - low10 * m2
    mix = m4 - low20 * m2
    good1 = piv1 > 1e-7 * m3
    safe1 = jnp.where(good1, piv1, 1.0)
    low21 = jnp.where(good1, mix / safe1, 0.0)
    piv2 = m5 - low20 * m3 - low21 * mix
    good2 = good1 & (piv2 > 1e-7 * m5)
    y1 = m1 - low10 * m0
    y2 = m2 - low20 * m0 - low21 * y1
    c2 = jnp.where(good2, y2 / jnp.where(good2, piv2, 1.0), 0.0)
    c1 = jnp.where(good1, y1 / safe1 - low21 * c2, 0.0)
    c0 = m0 / m1 - low10 * c1 - low20 * c2
    c0, c1, c2 = [jnp.broadcast_to(jnp.concatenate([c, c], axis=1), (ROWS, NZ)) for c in (c0, c1, c2)]

    clear_tails([zs, zd])
    for plane in range(3):
        e_ref[plane, 0:ROWS] = jnp.zeros((ROWS, NZ), F32)
        e_ref[plane, NY + ROWS : NY + 2 * ROWS] = jnp.zeros((ROWS, NZ), F32)
    v1_planes = [v1_left_ref.at[1], v1_ref.at[0], v1_ref.at[1]]

    def combine(chunk, done):
        here = rows_at(chunk)
        for plane in range(3):
            for comp in range(3):
                value = c0 * v0_ref[plane, comp, here] + c1 * v1_planes[plane][comp, here]
                value = value + c2 * v2_ref[plane, comp, here]
                if plane > 0:
                    u_ref[comp, plane - 1, here] = value
                store_z_modes(zs, zd, plane, comp, here, value)
        return done

    lax.fori_loop(0, CHUNKS, combine, 0)
    at_end = end_flag()

    def measure(chunk, done):
        for plane, energy in enumerate(energies(zs, zd, chunk)):
            e_ref[plane, rows_at(chunk + 1)] = energy * (at_end if plane == 2 else 1.0)
        return done

    lax.fori_loop(0, CHUNKS, measure, 0)
    span = ROWS + 2
    for block in range(CHUNKS):
        for plane in range(3):
            first = ROWS - 1 + block * ROWS
            out_ref[block, plane * span : (plane + 1) * span] = e_ref[plane, first : first + span]


def weigh(planes):
    near = RADIUS - 1.0
    edge = RADIUS - math.sqrt(2.0)
    beside = [from_below(p) + from_above(p) for p in planes]
    cross = []
    full = []
    for p, side in zip(planes, beside):
        up_down = p[0:ROWS] + p[2 : 2 + ROWS]
        mid, mid_side = p[1 : 1 + ROWS], side[1 : 1 + ROWS]
        cross.append(near * mid + edge * (mid_side + up_down))
        diagonal = side[0:ROWS] + side[2 : 2 + ROWS]
        full.append(RADIUS * mid + near * (mid_side + up_down) + edge * diagonal)
    return [full[k] + cross[k - 1] + cross[k + 1] for k in range(1, 1 + CX)]


def filter_kernel(energy_ref, next_ref, dens_ref, out_ref):
    space, load = lax.axis_index("space"), lax.axis_index("load")
    n_space, n_load = lax.axis_size("space"), lax.axis_size("load")
    span = ROWS + 2
    part = lambda ref, k: ref[k * span : (k + 1) * span]
    total = [
        part(energy_ref, 0),
        part(energy_ref, 1),
        part(energy_ref, 2) + part(next_ref, 0),
        part(next_ref, 1),
    ]
    before = jnp.maximum(load - 1, 0)
    after = jnp.minimum(load + 1, n_load - 1)
    at_y = load * ROWS - 1 + row_ids((span, NZ))
    in_y = (at_y >= 0) & (at_y < n_load * ROWS)
    weighted, inside, own = [], [], []
    for plane in range(4):
        dens = jnp.concatenate(
            [
                dens_ref[before, 1 + plane][ROWS - 1 : ROWS],
                dens_ref[load, 1 + plane],
                dens_ref[after, 1 + plane][0:1],
            ],
            axis=0,
        )
        at_x = space * CX - 1 + plane
        scale = jnp.where((at_x >= 0) & (at_x < n_space * CX), 1.0, 0.0).astype(F32)
        present = scale * jnp.where(in_y, 1.0, 0.0)
        sensitivity = -PENALTY * (1.0 - EMIN) * (dens * dens) * total[plane]
        weighted.append(present * (dens * sensitivity))
        inside.append(present)
        if 1 <= plane <= CX:
            own.append(dens[1 : 1 + ROWS])
    sums, counts = weigh(weighted), weigh(inside)
    for plane in range(CX):
        out_ref[plane] = sums[plane] / (own[plane] * counts[plane])


def shifted(array, axis, distance):
    size = lax.axis_size(axis)
    route = [(i, i + distance) for i in range(size) if 0 <= i + distance < size]
    return lax.ppermute(array, axis, route)


def body(density, fixed_dofs, body_loads, point_nodes, point_forces):
    n_load, n_space = lax.axis_size("load"), lax.axis_size("space")
    dens = jnp.concatenate(
        [shifted(density, "space", 1), density, shifted(density, "space", -1)], axis=0
    )
    plane = (3, NY, NZ)
    load, keep, to_right, to_left = kernel_call(
        loads_kernel, [(2,) + plane, (2,) + plane, (2,) + plane, (3,) + plane], 0, 4
    )(body_loads[0], fixed_dofs, point_nodes, point_forces[0])
    left = shifted(to_right, "space", 1)
    right = shifted(to_left, "space", -1)
    dens = lax.all_to_all(jnp.broadcast_to(dens[None], (n_load,) + dens.shape), "load", 0, 0)

    padded = (NY + ROWS, NZ)
    zed = lambda planes: pltpu.VMEM((planes, 3) + padded, F32)
    carry = pltpu.VMEM((3, 3, ROWS, NZ), F32)
    v0, v1, v1_far, modulus, inverse, mom = kernel_call(
        first_kernel,
        [(3,) + plane, (2,) + plane, plane, (6,) + padded, (4, NY, NZ), (8, 128)],
        0,
        5,
        [zed(5), zed(5), carry],
    )(load, keep, left, right, dens)
    v1_left = shifted(v1, "space", 1)
    v2, mom = kernel_call(
        second_kernel,
        [(3,) + plane, (n_space, 8, 128)],
        0,
        8,
        [zed(5), zed(5), zed(3), zed(3), carry],
    )(v1_left, v1, v1_far, left, keep, modulus, inverse, mom)
    mom = lax.all_to_all(mom, "space", 0, 0)
    span = ROWS + 2
    moved, energy = kernel_call(
        energy_kernel,
        [(3, CX, NY, NZ), (CHUNKS, 3 * span, NZ)],
        0,
        5,
        [zed(3), zed(3), pltpu.VMEM((3, NY + 2 * ROWS, NZ), F32)],
    )(v0, v1_left, v1, v2, mom)
    energy = jnp.sum(lax.all_to_all(energy, "load", 0, 0), axis=0)
    following = shifted(energy[: 2 * span], "space", -1)
    (filtered,) = kernel_call(filter_kernel, [(CX, ROWS, NZ)], 0, 3)(energy, following, dens)
    return (moved[None], filtered)


def solution(mesh):
    placed = (
        P("space", "load", None),
        P(None, "space", None, None),
        P("load", None, "space", None, None),
        P("load", None),
        P("load", None, None),
    )
    return jax.shard_map(
        body,
        mesh=mesh,
        in_specs=placed,
        out_specs=(P("load", None, "space", None, None), P("space", "load", None)),
        check_vma=False,
    )
```

```python
import math

import jax
import jax.numpy as jnp
from jax import lax
from jax.experimental import pallas as pl
from jax.experimental.pallas import tpu as pltpu
from jax.sharding import PartitionSpec as P

CX = 2
NY = 64
NZ = 256
ROWS = 8
CHUNKS = NY // ROWS
ZBITS = 8
EMIN = 0.001
PENALTY = 3.0
RADIUS = 1.5
POISSON = 0.3
LAME = POISSON / ((1.0 + POISSON) * (1.0 - 2.0 * POISSON))
SHEAR = 1.0 / (2.0 * (1.0 + POISSON))
KDIAG = (LAME + 4.0 * SHEAR) / 9.0
F32 = jnp.float32
VMEM_LIMIT = 16 * 1024 * 1024
PAIRS = ("ss", "sd", "ds", "dd")


def kernel_call(fn, outs, n_smem, n_in, scratch=()):
    vmem = pl.BlockSpec(memory_space=pltpu.VMEM)
    smem = pl.BlockSpec(memory_space=pltpu.SMEM)
    return pl.pallas_call(
        fn,
        out_shape=[jax.ShapeDtypeStruct(shape, F32) for shape in outs],
        in_specs=[smem] * n_smem + [vmem] * n_in,
        out_specs=[vmem] * len(outs),
        scratch_shapes=list(scratch),
        compiler_params=pltpu.CompilerParams(vmem_limit_bytes=VMEM_LIMIT),
    )


def lane_ids(shape):
    return lax.broadcasted_iota(jnp.int32, shape, 1)


def row_ids(shape):
    return lax.broadcasted_iota(jnp.int32, shape, 0)


def from_above(field):
    return jnp.where(lane_ids(field.shape) == NZ - 1, 0.0, pltpu.roll(field, NZ - 1, 1))


def from_below(field):
    return jnp.where(lane_ids(field.shape) == 0, 0.0, pltpu.roll(field, 1, 1))


def rows_at(chunk):
    return pl.ds(pl.multiple_of(chunk * ROWS, ROWS), ROWS)


def store_z_modes(zs_ref, zd_ref, plane, comp, rows, field):
    up = from_above(field)
    zs_ref[plane, comp, rows] = field + up
    zd_ref[plane, comp, rows] = up - field


def y_modes(cur, nxt):
    first = row_ids(cur.shape) == 0
    up = pltpu.roll(jnp.where(first, nxt, cur), ROWS - 1, 0)
    return cur + up, up - cur


def plane_modes(zs_ref, zd_ref, plane, chunk):
    out = []
    for comp in range(3):
        here, after = rows_at(chunk), rows_at(chunk + 1)
        ss, ds = y_modes(zs_ref[plane, comp, here], zs_ref[plane, comp, after])
        sd, dd = y_modes(zd_ref[plane, comp, here], zd_ref[plane, comp, after])
        out.append({"ss": ss, "sd": sd, "ds": ds, "dd": dd})
    return out


def element_modes(low, high):
    modes = []
    for comp in range(3):
        field = {}
        for pair in PAIRS:
            field["d" + pair] = high[comp][pair] - low[comp][pair]
            if pair != "ss":
                field["s" + pair] = high[comp][pair] + low[comp][pair]
        modes.append(field)
    return modes


NORMAL = ((0, "dss"), (1, "sds"), (2, "ssd"))
SHEARS = (((0, "sds"), (1, "dss")), ((0, "ssd"), (2, "dss")), ((1, "ssd"), (2, "sds")))
BENDS = (((0, "dsd"), (1, "sdd")), ((0, "dds"), (2, "sdd")), ((1, "dds"), (2, "dsd")))
TWISTS = ((0, "sdd"), (1, "dsd"), (2, "dds"))


def element_response(modes, modulus):
    k_lame = modulus * (LAME / 16.0)
    k_two = modulus * (SHEAR / 8.0)
    k_shear = modulus * (SHEAR / 16.0)
    k_bend = modulus * (LAME / 48.0)
    k_twist = modulus * (SHEAR / 48.0)
    k_last = modulus * ((LAME + 4.0 * SHEAR) / 144.0)
    force = [{}, {}, {}]
    get = lambda key: modes[key[0]][key[1]]
    trace = k_lame * (get(NORMAL[0]) + get(NORMAL[1]) + get(NORMAL[2]))
    for comp, name in NORMAL:
        force[comp][name] = k_two * modes[comp][name] + trace
    for one, two in SHEARS:
        both = k_shear * (get(one) + get(two))
        force[one[0]][one[1]] = both
        force[two[0]][two[1]] = both
    for one, two in BENDS:
        both = k_bend * (get(one) + get(two))
        force[one[0]][one[1]] = k_shear * get(one) + both
        force[two[0]][two[1]] = k_shear * get(two) + both
    total = get(TWISTS[0]) + get(TWISTS[1]) + get(TWISTS[2])
    for comp, name in TWISTS:
        force[comp][name] = k_twist * (modes[comp][name] + total)
    for comp in range(3):
        force[comp]["ddd"] = k_last * modes[comp]["ddd"]
    return force


def element_energy(modes):
    get = lambda key: modes[key[0]][key[1]]
    square = lambda value: value * value
    normal = [get(key) for key in NORMAL]
    twist = [get(key) for key in TWISTS]
    energy = (LAME / 16.0) * square(normal[0] + normal[1] + normal[2])
    energy += (SHEAR / 8.0) * (square(normal[0]) + square(normal[1]) + square(normal[2]))
    shear = sum(square(get(one) + get(two)) for one, two in SHEARS)
    shear += sum(square(get(one)) + square(get(two)) for one, two in BENDS)
    energy += (SHEAR / 16.0) * shear
    energy += (LAME / 48.0) * sum(square(get(one) + get(two)) for one, two in BENDS)
    twisted = square(twist[0]) + square(twist[1]) + square(twist[2])
    energy += (SHEAR / 48.0) * (twisted + square(twist[0] + twist[1] + twist[2]))
    last = square(modes[0]["ddd"]) + square(modes[1]["ddd"]) + square(modes[2]["ddd"])
    return energy + ((LAME + 4.0 * SHEAR) / 144.0) * last


def split_x(force):
    low, high = [], []
    for comp in range(3):
        lo, hi = {}, {}
        for pair in PAIRS:
            diff = force[comp]["d" + pair]
            if pair == "ss":
                lo[pair], hi[pair] = -diff, diff
            else:
                mean = force[comp]["s" + pair]
                lo[pair], hi[pair] = mean - diff, mean + diff
        low.append(lo)
        high.append(hi)
    return low, high


def node_force(acc, prev):
    sides = []
    for y_mode in ("s", "d"):
        mean, diff = acc[y_mode + "s"], acc[y_mode + "d"]
        sides.append((mean - diff) + from_below(mean + diff))
    low, high = sides[0] - sides[1], sides[0] + sides[1]
    last = row_ids(low.shape) == ROWS - 1
    return low + pltpu.roll(jnp.where(last, prev, high), 1, 0), high


def apply_rows(zs_ref, zd_ref, planes, e_ref, e_first, e_pad, carry_ref, chunk):
    low = plane_modes(zs_ref, zd_ref, 0, chunk)
    partial = None
    for plane in range(planes - 1):
        high = plane_modes(zs_ref, zd_ref, plane + 1, chunk)
        modulus = e_ref[e_first + plane, rows_at(chunk + e_pad)]
        to_low, to_high = split_x(element_response(element_modes(low, high), modulus))
        if partial is not None:
            forces = []
            for comp in range(3):
                acc = {pair: partial[comp][pair] + to_low[comp][pair] for pair in PAIRS}
                force, carry = node_force(acc, carry_ref[plane - 1, comp])
                carry_ref[plane - 1, comp] = carry
                forces.append(force)
            yield plane, forces
        partial, low = to_high, high


def loads_kernel(
    body_ref, fixed_ref, node_ref, force_ref, load_ref, keep_ref, right_ref, left_ref
):
    cells = CX * NY * NZ
    local = node_ref[...] - lax.axis_index("space") * cells
    valid = (local >= 0) & (local < cells)
    local = jnp.where(valid, local, -1)
    line = lax.shift_right_arithmetic(local, ZBITS)
    depth = lax.bitwise_and(local, NZ - 1)
    points = local.shape[1]
    on_line = row_ids((CX * NY, points)) == line
    lines = [jnp.where(on_line, force_ref[comp : comp + 1, :], 0.0) for comp in range(3)]
    at_depth = jnp.where(row_ids((NZ, points)) == depth, 1.0, 0.0)
    added = lax.dot_general(
        jnp.concatenate(lines, axis=0),
        at_depth,
        (((1,), (1,)), ((), ())),
        precision=lax.Precision.HIGHEST,
        preferred_element_type=F32,
    )
    for plane in range(CX):
        for comp in range(3):
            keep = 1.0 - fixed_ref[comp, plane].astype(F32)
            first = (comp * CX + plane) * NY
            load = keep * (body_ref[comp, plane] + added[first : first + NY])
            load_ref[plane, comp] = load
            keep_ref[plane, comp] = keep
            left_ref[plane, comp] = load
            if plane == 0:
                left_ref[2, comp] = keep
            else:
                right_ref[0, comp] = load
                right_ref[1, comp] = keep


def clear_tails(refs):
    for ref in refs:
        for plane in range(ref.shape[0]):
            for comp in range(3):
                ref[plane, comp, NY : NY + ROWS] = jnp.zeros((ROWS, NZ), F32)


def clear_carry(ref):
    for plane in range(ref.shape[0]):
        for comp in range(3):
            ref[plane, comp] = jnp.zeros((ROWS, NZ), F32)


def folded(values):
    rows = [jnp.sum(v[:, :128] + v[:, 128:], axis=0, keepdims=True) for v in values]
    return jnp.concatenate(rows, axis=0)


def advance(forces, kept, before, inverse):
    image = jnp.where(kept, forces, before)
    return image, jnp.where(kept, forces * inverse, before)


def first_kernel(
    load_ref, keep_ref, left_ref, right_ref, dens_ref,
    v0_ref, v1_ref, v1_far_ref, e_ref, inv_ref, mom_ref,
    zs, zd, carry,
):
    first_x = lax.axis_index("space") * CX
    limit = lax.axis_size("space") * CX
    for plane in range(6):
        at = first_x - 2 + plane
        scale = jnp.where((at >= 0) & (at < limit), 1.0, 0.0).astype(F32)
        e_ref[plane, 0:ROWS] = jnp.zeros((ROWS, NZ), F32)
        for block in range(CHUNKS):
            dens = dens_ref[block, plane]
            rows = slice((block + 1) * ROWS, (block + 2) * ROWS)
            e_ref[plane, rows] = scale * (EMIN + (1.0 - EMIN) * (dens * dens * dens))
    clear_tails([zs, zd])
    clear_carry(carry)
    loads = [left_ref.at[0], load_ref.at[0], load_ref.at[1], right_ref.at[0], right_ref.at[1]]
    keeps = [keep_ref.at[0], keep_ref.at[1], right_ref.at[2]]
    zero = jnp.zeros((ROWS, NZ), F32)
    has_right = 1.0 - end_flag()
    scaled = lambda value, plane: value * has_right if plane > 2 else value

    def start(chunk, total):
        here = rows_at(chunk)
        last = row_ids((ROWS, NZ)) == ROWS - 1
        for plane in range(5):
            cur = e_ref[plane, rows_at(chunk + 1)] + e_ref[plane + 1, rows_at(chunk + 1)]
            before = e_ref[plane, rows_at(chunk)] + e_ref[plane + 1, rows_at(chunk)]
            cur = cur + pltpu.roll(jnp.where(last, before, cur), 1, 0)
            diag = KDIAG * (cur + from_below(cur))
            inverse = 1.0 / jnp.where(diag > 0.0, diag, 1.0)
            if plane < 4:
                inv_ref[plane, here] = inverse
            for comp in range(3):
                load = scaled(loads[plane][comp, here], plane)
                value = load * inverse
                if plane < 3:
                    v0_ref[plane, comp, here] = value
                if plane in (1, 2):
                    total = total + load * value
                store_z_modes(zs, zd, plane, comp, here, value)
        return total

    mom0 = lax.fori_loop(0, CHUNKS, start, zero)

    def apply(chunk, totals):
        here = rows_at(chunk)
        odd, even = totals
        for plane, forces in apply_rows(zs, zd, 5, e_ref, 1, 1, carry, chunk):
            inverse = inv_ref[plane, here]
            for comp in range(3):
                kept = scaled(keeps[plane - 1][comp, here], plane) > 0.0
                before = scaled(loads[plane][comp, here], plane) * inverse
                image, value = advance(forces[comp], kept, before, inverse)
                if plane < 3:
                    v1_ref[plane - 1, comp, here] = value
                    odd = odd + before * image
                    even = even + value * image
                else:
                    v1_far_ref[comp, here] = value
        return odd, even

    mom1, mom2 = lax.fori_loop(0, CHUNKS, apply, (zero, zero))
    mom_ref[...] = folded([mom0, mom1, mom2] + [zero] * 5)


def second_kernel(
    v1_left_ref, v1_ref, v1_far_ref, keep_left_ref, keep_ref, e_ref, inv_ref, sofar_ref,
    v2_ref, mom_ref,
    zs, zd, zs2, zd2, carry,
):
    v1_planes = [v1_left_ref.at[0], v1_left_ref.at[1], v1_ref.at[0], v1_ref.at[1], v1_far_ref]
    keeps = [keep_left_ref.at[1], keep_ref.at[0], keep_ref.at[1]]
    clear_tails([zs, zd, zs2, zd2])
    clear_carry(carry)
    zero = jnp.zeros((ROWS, NZ), F32)

    def start(chunk, done):
        here = rows_at(chunk)
        for plane in range(5):
            for comp in range(3):
                store_z_modes(zs, zd, plane, comp, here, v1_planes[plane][comp, here])
        return done

    lax.fori_loop(0, CHUNKS, start, 0)

    def apply(chunk, totals):
        here = rows_at(chunk)
        odd, even = totals
        for plane, forces in apply_rows(zs, zd, 5, e_ref, 0, 1, carry, chunk):
            inverse = inv_ref[plane - 1, here]
            for comp in range(3):
                kept = keeps[plane - 1][comp, here] > 0.0
                before = v1_planes[plane][comp, here]
                image, value = advance(forces[comp], kept, before, inverse)
                v2_ref[plane - 1, comp, here] = value
                store_z_modes(zs2, zd2, plane - 1, comp, here, value)
                if plane > 1:
                    odd = odd + before * image
                    even = even + value * image
        return odd, even

    mom3, mom4 = lax.fori_loop(0, CHUNKS, apply, (zero, zero))
    at_end = end_flag()

    def last(chunk, total):
        for plane, energy in enumerate(energies(zs2, zd2, chunk)):
            total = total + (e_ref[1 + plane, rows_at(chunk + 1)] * energy) * (at_end if plane == 2 else 1.0)
        return total

    mom5 = lax.fori_loop(0, CHUNKS, last, zero)
    total = sofar_ref[...] + folded([zero] * 3 + [mom3, mom4, mom5] + [zero] * 2)
    for device in range(mom_ref.shape[0]):
        mom_ref[device] = total


def end_flag():
    at_end = lax.axis_index("space") == lax.axis_size("space") - 1
    return jnp.where(at_end, 1.0, 0.0).astype(F32)


def energies(zs, zd, chunk):
    planes = [plane_modes(zs, zd, plane, chunk) for plane in range(3)]
    zero = {pair: jnp.zeros((ROWS, NZ), F32) for pair in PAIRS}
    planes.append([zero] * 3)
    for low, high in zip(planes[:-1], planes[1:]):
        yield element_energy(element_modes(low, high))


def energy_kernel(v0_ref, v1_left_ref, v1_ref, v2_ref, mom_ref, u_ref, out_ref, zs, zd, e_ref):
    total = mom_ref[0]
    for device in range(1, mom_ref.shape[0]):
        total = total + mom_ref[device]
    total = jnp.broadcast_to(jnp.sum(total, axis=1, keepdims=True), (8, 128))
    m0, m1, m2, m3, m4, m5 = [total[k : k + 1] for k in range(6)]
    low10 = m2 / m1
    low20 = m3 / m1
    piv1 = m3 - low10 * m2
    mix = m4 - low20 * m2
    good1 = piv1 > 1e-7 * m3
    safe1 = jnp.where(good1, piv1, 1.0)
    low21 = jnp.where(good1, mix / safe1, 0.0)
    piv2 = m5 - low20 * m3 - low21 * mix
    good2 = good1 & (piv2 > 1e-7 * m5)
    y1 = m1 - low10 * m0
    y2 = m2 - low20 * m0 - low21 * y1
    c2 = jnp.where(good2, y2 / jnp.where(good2, piv2, 1.0), 0.0)
    c1 = jnp.where(good1, y1 / safe1 - low21 * c2, 0.0)
    c0 = m0 / m1 - low10 * c1 - low20 * c2
    c0, c1, c2 = [jnp.broadcast_to(jnp.concatenate([c, c], axis=1), (ROWS, NZ)) for c in (c0, c1, c2)]

    clear_tails([zs, zd])
    for plane in range(3):
        e_ref[plane, 0:ROWS] = jnp.zeros((ROWS, NZ), F32)
        e_ref[plane, NY + ROWS : NY + 2 * ROWS] = jnp.zeros((ROWS, NZ), F32)
    v1_planes = [v1_left_ref.at[1], v1_ref.at[0], v1_ref.at[1]]

    def combine(chunk, done):
        here = rows_at(chunk)
        for plane in range(3):
            for comp in range(3):
                value = c0 * v0_ref[plane, comp, here] + c1 * v1_planes[plane][comp, here]
                value = value + c2 * v2_ref[plane, comp, here]
                if plane > 0:
                    u_ref[comp, plane - 1, here] = value
                store_z_modes(zs, zd, plane, comp, here, value)
        return done

    lax.fori_loop(0, CHUNKS, combine, 0)
    at_end = end_flag()

    def measure(chunk, done):
        for plane, energy in enumerate(energies(zs, zd, chunk)):
            e_ref[plane, rows_at(chunk + 1)] = energy * (at_end if plane == 2 else 1.0)
        return done

    lax.fori_loop(0, CHUNKS, measure, 0)
    span = ROWS + 2
    for block in range(CHUNKS):
        for plane in range(3):
            first = ROWS - 1 + block * ROWS
            out_ref[block, plane * span : (plane + 1) * span] = e_ref[plane, first : first + span]


def weigh(planes):
    near = RADIUS - 1.0
    edge = RADIUS - math.sqrt(2.0)
    beside = [from_below(p) + from_above(p) for p in planes]
    cross = []
    full = []
    for p, side in zip(planes, beside):
        up_down = p[0:ROWS] + p[2 : 2 + ROWS]
        mid, mid_side = p[1 : 1 + ROWS], side[1 : 1 + ROWS]
        cross.append(near * mid + edge * (mid_side + up_down))
        diagonal = side[0:ROWS] + side[2 : 2 + ROWS]
        full.append(RADIUS * mid + near * (mid_side + up_down) + edge * diagonal)
    return [full[k] + cross[k - 1] + cross[k + 1] for k in range(1, 1 + CX)]


def filter_kernel(energy_ref, next_ref, dens_ref, out_ref):
    space, load = lax.axis_index("space"), lax.axis_index("load")
    n_space, n_load = lax.axis_size("space"), lax.axis_size("load")
    span = ROWS + 2
    part = lambda ref, k: ref[k * span : (k + 1) * span]
    total = [
        part(energy_ref, 0),
        part(energy_ref, 1),
        part(energy_ref, 2) + (1.0 - end_flag()) * part(next_ref, 0),
        part(next_ref, 1),
    ]
    before = jnp.maximum(load - 1, 0)
    after = jnp.minimum(load + 1, n_load - 1)
    at_y = load * ROWS - 1 + row_ids((span, NZ))
    in_y = (at_y >= 0) & (at_y < n_load * ROWS)
    weighted, inside, own = [], [], []
    for plane in range(4):
        dens = jnp.concatenate(
            [
                dens_ref[before, 1 + plane][ROWS - 1 : ROWS],
                dens_ref[load, 1 + plane],
                dens_ref[after, 1 + plane][0:1],
            ],
            axis=0,
        )
        at_x = space * CX - 1 + plane
        scale = jnp.where((at_x >= 0) & (at_x < n_space * CX), 1.0, 0.0).astype(F32)
        present = scale * jnp.where(in_y, 1.0, 0.0)
        sensitivity = -PENALTY * (1.0 - EMIN) * (dens * dens) * total[plane]
        weighted.append(present * (dens * sensitivity))
        inside.append(present)
        if 1 <= plane <= CX:
            own.append(dens[1 : 1 + ROWS])
    sums, counts = weigh(weighted), weigh(inside)
    for plane in range(CX):
        out_ref[plane] = sums[plane] / (own[plane] * counts[plane])


def shifted(array, axis, distance):
    size = lax.axis_size(axis)
    return lax.ppermute(array, axis, [(i, (i + distance) % size) for i in range(size)])


def body(density, fixed_dofs, body_loads, point_nodes, point_forces):
    n_load, n_space = lax.axis_size("load"), lax.axis_size("space")
    dens = jnp.concatenate(
        [shifted(density, "space", 1), density, shifted(density, "space", -1)], axis=0
    )
    plane = (3, NY, NZ)
    load, keep, to_right, to_left = kernel_call(
        loads_kernel, [(2,) + plane, (2,) + plane, (2,) + plane, (3,) + plane], 0, 4
    )(body_loads[0], fixed_dofs, point_nodes, point_forces[0])
    left = shifted(to_right, "space", 1)
    right = shifted(to_left, "space", -1)
    dens = lax.all_to_all(jnp.broadcast_to(dens[None], (n_load,) + dens.shape), "load", 0, 0)

    padded = (NY + ROWS, NZ)
    zed = lambda planes: pltpu.VMEM((planes, 3) + padded, F32)
    carry = pltpu.VMEM((3, 3, ROWS, NZ), F32)
    v0, v1, v1_far, modulus, inverse, mom = kernel_call(
        first_kernel,
        [(3,) + plane, (2,) + plane, plane, (6,) + padded, (4, NY, NZ), (8, 128)],
        0,
        5,
        [zed(5), zed(5), carry],
    )(load, keep, left, right, dens)
    v1_left = shifted(v1, "space", 1)
    v2, mom = kernel_call(
        second_kernel,
        [(3,) + plane, (n_space, 8, 128)],
        0,
        8,
        [zed(5), zed(5), zed(3), zed(3), carry],
    )(v1_left, v1, v1_far, left, keep, modulus, inverse, mom)
    mom = lax.all_to_all(mom, "space", 0, 0)
    span = ROWS + 2
    moved, energy = kernel_call(
        energy_kernel,
        [(3, CX, NY, NZ), (CHUNKS, 3 * span, NZ)],
        0,
        5,
        [zed(3), zed(3), pltpu.VMEM((3, NY + 2 * ROWS, NZ), F32)],
    )(v0, v1_left, v1, v2, mom)
    energy = jnp.sum(lax.all_to_all(energy, "load", 0, 0), axis=0)
    following = shifted(energy[: 2 * span], "space", -1)
    (filtered,) = kernel_call(filter_kernel, [(CX, ROWS, NZ)], 0, 3)(energy, following, dens)
    return (moved[None], filtered)


def solution(mesh):
    placed = (
        P("space", "load", None),
        P(None, "space", None, None),
        P("load", None, "space", None, None),
        P("load", None),
        P("load", None, None),
    )
    return jax.shard_map(
        body,
        mesh=mesh,
        in_specs=placed,
        out_specs=(P("load", None, "space", None, None), P("space", "load", None)),
        check_vma=False,
    )
```

```python
import math

import jax
import jax.numpy as jnp
from jax import lax
from jax.experimental import pallas as pl
from jax.experimental.pallas import tpu as pltpu
from jax.sharding import PartitionSpec as P

CX = 2
NY = 64
NZ = 256
ROWS = 8
CHUNKS = NY // ROWS
ZBITS = 8
EMIN = 0.001
PENALTY = 3.0
RADIUS = 1.5
POISSON = 0.3
LAME = POISSON / ((1.0 + POISSON) * (1.0 - 2.0 * POISSON))
SHEAR = 1.0 / (2.0 * (1.0 + POISSON))
KDIAG = (LAME + 4.0 * SHEAR) / 9.0
F32 = jnp.float32
VMEM_LIMIT = 16 * 1024 * 1024
PAIRS = ("ss", "sd", "ds", "dd")


def kernel_call(fn, outs, n_smem, n_in, scratch=()):
    vmem = pl.BlockSpec(memory_space=pltpu.VMEM)
    smem = pl.BlockSpec(memory_space=pltpu.SMEM)
    return pl.pallas_call(
        fn,
        out_shape=[jax.ShapeDtypeStruct(shape, F32) for shape in outs],
        in_specs=[smem] * n_smem + [vmem] * n_in,
        out_specs=[vmem] * len(outs),
        scratch_shapes=list(scratch),
        compiler_params=pltpu.CompilerParams(vmem_limit_bytes=VMEM_LIMIT),
    )


def lane_ids(shape):
    return lax.broadcasted_iota(jnp.int32, shape, 1)


def row_ids(shape):
    return lax.broadcasted_iota(jnp.int32, shape, 0)


def from_above(field):
    return jnp.where(lane_ids(field.shape) == NZ - 1, 0.0, pltpu.roll(field, NZ - 1, 1))


def from_below(field):
    return jnp.where(lane_ids(field.shape) == 0, 0.0, pltpu.roll(field, 1, 1))


def rows_at(chunk):
    return pl.ds(pl.multiple_of(chunk * ROWS, ROWS), ROWS)


def store_z_modes(zs_ref, zd_ref, plane, comp, rows, field):
    up = from_above(field)
    zs_ref[plane, comp, rows] = field + up
    zd_ref[plane, comp, rows] = up - field


def y_modes(cur, nxt):
    first = row_ids(cur.shape) == 0
    up = pltpu.roll(jnp.where(first, nxt, cur), ROWS - 1, 0)
    return cur + up, up - cur


def plane_modes(zs_ref, zd_ref, plane, chunk):
    out = []
    for comp in range(3):
        here, after = rows_at(chunk), rows_at(chunk + 1)
        ss, ds = y_modes(zs_ref[plane, comp, here], zs_ref[plane, comp, after])
        sd, dd = y_modes(zd_ref[plane, comp, here], zd_ref[plane, comp, after])
        out.append({"ss": ss, "sd": sd, "ds": ds, "dd": dd})
    return out


def element_modes(low, high):
    modes = []
    for comp in range(3):
        field = {}
        for pair in PAIRS:
            field["d" + pair] = high[comp][pair] - low[comp][pair]
            if pair != "ss":
                field["s" + pair] = high[comp][pair] + low[comp][pair]
        modes.append(field)
    return modes


NORMAL = ((0, "dss"), (1, "sds"), (2, "ssd"))
SHEARS = (((0, "sds"), (1, "dss")), ((0, "ssd"), (2, "dss")), ((1, "ssd"), (2, "sds")))
BENDS = (((0, "dsd"), (1, "sdd")), ((0, "dds"), (2, "sdd")), ((1, "dds"), (2, "dsd")))
TWISTS = ((0, "sdd"), (1, "dsd"), (2, "dds"))


def element_response(modes, modulus):
    k_lame = modulus * (LAME / 16.0)
    k_two = modulus * (SHEAR / 8.0)
    k_shear = modulus * (SHEAR / 16.0)
    k_bend = modulus * (LAME / 48.0)
    k_twist = modulus * (SHEAR / 48.0)
    k_last = modulus * ((LAME + 4.0 * SHEAR) / 144.0)
    force = [{}, {}, {}]
    get = lambda key: modes[key[0]][key[1]]
    trace = k_lame * (get(NORMAL[0]) + get(NORMAL[1]) + get(NORMAL[2]))
    for comp, name in NORMAL:
        force[comp][name] = k_two * modes[comp][name] + trace
    for one, two in SHEARS:
        both = k_shear * (get(one) + get(two))
        force[one[0]][one[1]] = both
        force[two[0]][two[1]] = both
    for one, two in BENDS:
        both = k_bend * (get(one) + get(two))
        force[one[0]][one[1]] = k_shear * get(one) + both
        force[two[0]][two[1]] = k_shear * get(two) + both
    total = get(TWISTS[0]) + get(TWISTS[1]) + get(TWISTS[2])
    for comp, name in TWISTS:
        force[comp][name] = k_twist * (modes[comp][name] + total)
    for comp in range(3):
        force[comp]["ddd"] = k_last * modes[comp]["ddd"]
    return force


def element_energy(modes):
    get = lambda key: modes[key[0]][key[1]]
    square = lambda value: value * value
    normal = [get(key) for key in NORMAL]
    twist = [get(key) for key in TWISTS]
    energy = (LAME / 16.0) * square(normal[0] + normal[1] + normal[2])
    energy += (SHEAR / 8.0) * (square(normal[0]) + square(normal[1]) + square(normal[2]))
    shear = sum(square(get(one) + get(two)) for one, two in SHEARS)
    shear += sum(square(get(one)) + square(get(two)) for one, two in BENDS)
    energy += (SHEAR / 16.0) * shear
    energy += (LAME / 48.0) * sum(square(get(one) + get(two)) for one, two in BENDS)
    twisted = square(twist[0]) + square(twist[1]) + square(twist[2])
    energy += (SHEAR / 48.0) * (twisted + square(twist[0] + twist[1] + twist[2]))
    last = square(modes[0]["ddd"]) + square(modes[1]["ddd"]) + square(modes[2]["ddd"])
    return energy + ((LAME + 4.0 * SHEAR) / 144.0) * last


def split_x(force):
    low, high = [], []
    for comp in range(3):
        lo, hi = {}, {}
        for pair in PAIRS:
            diff = force[comp]["d" + pair]
            if pair == "ss":
                lo[pair], hi[pair] = -diff, diff
            else:
                mean = force[comp]["s" + pair]
                lo[pair], hi[pair] = mean - diff, mean + diff
        low.append(lo)
        high.append(hi)
    return low, high


def node_force(acc, prev):
    sides = []
    for y_mode in ("s", "d"):
        mean, diff = acc[y_mode + "s"], acc[y_mode + "d"]
        sides.append((mean - diff) + from_below(mean + diff))
    low, high = sides[0] - sides[1], sides[0] + sides[1]
    last = row_ids(low.shape) == ROWS - 1
    return low + pltpu.roll(jnp.where(last, prev, high), 1, 0), high


def apply_rows(zs_ref, zd_ref, planes, e_ref, e_first, e_pad, carry_ref, chunk):
    low = plane_modes(zs_ref, zd_ref, 0, chunk)
    partial = None
    for plane in range(planes - 1):
        high = plane_modes(zs_ref, zd_ref, plane + 1, chunk)
        modulus = e_ref[e_first + plane, rows_at(chunk + e_pad)]
        to_low, to_high = split_x(element_response(element_modes(low, high), modulus))
        if partial is not None:
            forces = []
            for comp in range(3):
                acc = {pair: partial[comp][pair] + to_low[comp][pair] for pair in PAIRS}
                force, carry = node_force(acc, carry_ref[plane - 1, comp])
                carry_ref[plane - 1, comp] = carry
                forces.append(force)
            yield plane, forces
        partial, low = to_high, high


def loads_kernel(
    body_ref, fixed_ref, node_ref, force_ref, load_ref, keep_ref, right_ref, left_ref
):
    cells = CX * NY * NZ
    local = node_ref[...] - lax.axis_index("space") * cells
    valid = (local >= 0) & (local < cells)
    local = jnp.where(valid, local, -1)
    line = lax.shift_right_arithmetic(local, ZBITS)
    depth = lax.bitwise_and(local, NZ - 1)
    points = local.shape[1]
    on_line = row_ids((CX * NY, points)) == line
    lines = [jnp.where(on_line, force_ref[comp : comp + 1, :], 0.0) for comp in range(3)]
    at_depth = jnp.where(row_ids((NZ, points)) == depth, 1.0, 0.0)
    added = lax.dot_general(
        jnp.concatenate(lines, axis=0),
        at_depth,
        (((1,), (1,)), ((), ())),
        precision=lax.Precision.HIGHEST,
        preferred_element_type=F32,
    )
    for plane in range(CX):
        for comp in range(3):
            keep = 1.0 - fixed_ref[comp, plane].astype(F32)
            first = (comp * CX + plane) * NY
            load = keep * (body_ref[comp, plane] + added[first : first + NY])
            load_ref[plane, comp] = load
            keep_ref[plane, comp] = keep
            left_ref[plane, comp] = load
            if plane == 0:
                left_ref[2, comp] = keep
            else:
                right_ref[0, comp] = load
                right_ref[1, comp] = keep


def pack_kernel(before_ref, own_ref, after_ref, pack_ref):
    for block in range(pack_ref.shape[0]):
        for plane in range(CX):
            pack_ref[block, plane] = before_ref[plane]
            pack_ref[block, CX + plane] = own_ref[plane]
            pack_ref[block, 2 * CX + plane] = after_ref[plane]


def clear_tails(refs):
    for ref in refs:
        for plane in range(ref.shape[0]):
            for comp in range(3):
                ref[plane, comp, NY : NY + ROWS] = jnp.zeros((ROWS, NZ), F32)


def clear_carry(ref):
    for plane in range(ref.shape[0]):
        for comp in range(3):
            ref[plane, comp] = jnp.zeros((ROWS, NZ), F32)


def folded(values):
    rows = [jnp.sum(v[:, :128] + v[:, 128:], axis=0, keepdims=True) for v in values]
    return jnp.concatenate(rows, axis=0)


def advance(forces, kept, before, inverse):
    image = jnp.where(kept, forces, before)
    return image, jnp.where(kept, forces * inverse, before)


def first_kernel(
    load_ref, keep_ref, left_ref, right_ref, dens_ref,
    v0_ref, v1_ref, v1_far_ref, e_ref, inv_ref, mom_ref,
    zs, zd, carry,
):
    first_x = lax.axis_index("space") * CX
    limit = lax.axis_size("space") * CX
    for plane in range(6):
        at = first_x - 2 + plane
        scale = jnp.where((at >= 0) & (at < limit), 1.0, 0.0).astype(F32)
        e_ref[plane, 0:ROWS] = jnp.zeros((ROWS, NZ), F32)
        for block in range(CHUNKS):
            dens = dens_ref[block, plane]
            rows = slice((block + 1) * ROWS, (block + 2) * ROWS)
            e_ref[plane, rows] = scale * (EMIN + (1.0 - EMIN) * (dens * dens * dens))
    clear_tails([zs, zd])
    clear_carry(carry)
    loads = [left_ref.at[0], load_ref.at[0], load_ref.at[1], right_ref.at[0], right_ref.at[1]]
    keeps = [keep_ref.at[0], keep_ref.at[1], right_ref.at[2]]
    zero = jnp.zeros((ROWS, NZ), F32)
    has_right = 1.0 - end_flag()
    scaled = lambda value, plane: value * has_right if plane > 2 else value

    def start(chunk, total):
        here = rows_at(chunk)
        last = row_ids((ROWS, NZ)) == ROWS - 1
        for plane in range(5):
            cur = e_ref[plane, rows_at(chunk + 1)] + e_ref[plane + 1, rows_at(chunk + 1)]
            before = e_ref[plane, rows_at(chunk)] + e_ref[plane + 1, rows_at(chunk)]
            cur = cur + pltpu.roll(jnp.where(last, before, cur), 1, 0)
            diag = KDIAG * (cur + from_below(cur))
            inverse = 1.0 / jnp.where(diag > 0.0, diag, 1.0)
            if plane < 4:
                inv_ref[plane, here] = inverse
            for comp in range(3):
                load = scaled(loads[plane][comp, here], plane)
                value = load * inverse
                if plane < 3:
                    v0_ref[plane, comp, here] = value
                if plane in (1, 2):
                    total = total + load * value
                store_z_modes(zs, zd, plane, comp, here, value)
        return total

    mom0 = lax.fori_loop(0, CHUNKS, start, zero)

    def apply(chunk, totals):
        here = rows_at(chunk)
        odd, even = totals
        for plane, forces in apply_rows(zs, zd, 5, e_ref, 1, 1, carry, chunk):
            inverse = inv_ref[plane, here]
            for comp in range(3):
                kept = scaled(keeps[plane - 1][comp, here], plane) > 0.0
                before = scaled(loads[plane][comp, here], plane) * inverse
                image, value = advance(forces[comp], kept, before, inverse)
                if plane < 3:
                    v1_ref[plane - 1, comp, here] = value
                    odd = odd + before * image
                    even = even + value * image
                else:
                    v1_far_ref[comp, here] = value
        return odd, even

    mom1, mom2 = lax.fori_loop(0, CHUNKS, apply, (zero, zero))
    mom_ref[...] = folded([mom0, mom1, mom2] + [zero] * 5)


def second_kernel(
    v1_left_ref, v1_ref, v1_far_ref, keep_left_ref, keep_ref, e_ref, inv_ref, sofar_ref,
    v2_ref, mom_ref,
    zs, zd, zs2, zd2, carry,
):
    v1_planes = [v1_left_ref.at[0], v1_left_ref.at[1], v1_ref.at[0], v1_ref.at[1], v1_far_ref]
    keeps = [keep_left_ref.at[1], keep_ref.at[0], keep_ref.at[1]]
    clear_tails([zs, zd, zs2, zd2])
    clear_carry(carry)
    zero = jnp.zeros((ROWS, NZ), F32)

    def start(chunk, done):
        here = rows_at(chunk)
        for plane in range(5):
            for comp in range(3):
                store_z_modes(zs, zd, plane, comp, here, v1_planes[plane][comp, here])
        return done

    lax.fori_loop(0, CHUNKS, start, 0)

    def apply(chunk, totals):
        here = rows_at(chunk)
        odd, even = totals
        for plane, forces in apply_rows(zs, zd, 5, e_ref, 0, 1, carry, chunk):
            inverse = inv_ref[plane - 1, here]
            for comp in range(3):
                kept = keeps[plane - 1][comp, here] > 0.0
                before = v1_planes[plane][comp, here]
                image, value = advance(forces[comp], kept, before, inverse)
                v2_ref[plane - 1, comp, here] = value
                store_z_modes(zs2, zd2, plane - 1, comp, here, value)
                if plane > 1:
                    odd = odd + before * image
                    even = even + value * image
        return odd, even

    mom3, mom4 = lax.fori_loop(0, CHUNKS, apply, (zero, zero))
    at_end = end_flag()

    def last(chunk, total):
        for plane, energy in enumerate(energies(zs2, zd2, chunk)):
            total = total + (e_ref[1 + plane, rows_at(chunk + 1)] * energy) * (at_end if plane == 2 else 1.0)
        return total

    mom5 = lax.fori_loop(0, CHUNKS, last, zero)
    total = sofar_ref[...] + folded([zero] * 3 + [mom3, mom4, mom5] + [zero] * 2)
    for device in range(mom_ref.shape[0]):
        mom_ref[device] = total


def end_flag():
    at_end = lax.axis_index("space") == lax.axis_size("space") - 1
    return jnp.where(at_end, 1.0, 0.0).astype(F32)


def energies(zs, zd, chunk):
    planes = [plane_modes(zs, zd, plane, chunk) for plane in range(3)]
    zero = {pair: jnp.zeros((ROWS, NZ), F32) for pair in PAIRS}
    planes.append([zero] * 3)
    for low, high in zip(planes[:-1], planes[1:]):
        yield element_energy(element_modes(low, high))


def energy_kernel(v0_ref, v1_left_ref, v1_ref, v2_ref, mom_ref, u_ref, out_ref, zs, zd, e_ref):
    total = mom_ref[0]
    for device in range(1, mom_ref.shape[0]):
        total = total + mom_ref[device]
    total = jnp.broadcast_to(jnp.sum(total, axis=1, keepdims=True), (8, 128))
    m0, m1, m2, m3, m4, m5 = [total[k : k + 1] for k in range(6)]
    low10 = m2 / m1
    low20 = m3 / m1
    piv1 = m3 - low10 * m2
    mix = m4 - low20 * m2
    good1 = piv1 > 1e-7 * m3
    safe1 = jnp.where(good1, piv1, 1.0)
    low21 = jnp.where(good1, mix / safe1, 0.0)
    piv2 = m5 - low20 * m3 - low21 * mix
    good2 = good1 & (piv2 > 1e-7 * m5)
    y1 = m1 - low10 * m0
    y2 = m2 - low20 * m0 - low21 * y1
    c2 = jnp.where(good2, y2 / jnp.where(good2, piv2, 1.0), 0.0)
    c1 = jnp.where(good1, y1 / safe1 - low21 * c2, 0.0)
    c0 = m0 / m1 - low10 * c1 - low20 * c2
    c0, c1, c2 = [jnp.broadcast_to(jnp.concatenate([c, c], axis=1), (ROWS, NZ)) for c in (c0, c1, c2)]

    clear_tails([zs, zd])
    for plane in range(3):
        e_ref[plane, 0:ROWS] = jnp.zeros((ROWS, NZ), F32)
        e_ref[plane, NY + ROWS : NY + 2 * ROWS] = jnp.zeros((ROWS, NZ), F32)
    v1_planes = [v1_left_ref.at[1], v1_ref.at[0], v1_ref.at[1]]

    def combine(chunk, done):
        here = rows_at(chunk)
        for plane in range(3):
            for comp in range(3):
                value = c0 * v0_ref[plane, comp, here] + c1 * v1_planes[plane][comp, here]
                value = value + c2 * v2_ref[plane, comp, here]
                if plane > 0:
                    u_ref[comp, plane - 1, here] = value
                store_z_modes(zs, zd, plane, comp, here, value)
        return done

    lax.fori_loop(0, CHUNKS, combine, 0)
    at_end = end_flag()

    def measure(chunk, done):
        for plane, energy in enumerate(energies(zs, zd, chunk)):
            e_ref[plane, rows_at(chunk + 1)] = energy * (at_end if plane == 2 else 1.0)
        return done

    lax.fori_loop(0, CHUNKS, measure, 0)
    span = ROWS + 2
    for block in range(CHUNKS):
        for plane in range(3):
            first = ROWS - 1 + block * ROWS
            out_ref[block, plane * span : (plane + 1) * span] = e_ref[plane, first : first + span]


def weigh(planes):
    near = RADIUS - 1.0
    edge = RADIUS - math.sqrt(2.0)
    beside = [from_below(p) + from_above(p) for p in planes]
    cross = []
    full = []
    for p, side in zip(planes, beside):
        up_down = p[0:ROWS] + p[2 : 2 + ROWS]
        mid, mid_side = p[1 : 1 + ROWS], side[1 : 1 + ROWS]
        cross.append(near * mid + edge * (mid_side + up_down))
        diagonal = side[0:ROWS] + side[2 : 2 + ROWS]
        full.append(RADIUS * mid + near * (mid_side + up_down) + edge * diagonal)
    return [full[k] + cross[k - 1] + cross[k + 1] for k in range(1, 1 + CX)]


def filter_kernel(energy_ref, next_ref, dens_ref, out_ref):
    space, load = lax.axis_index("space"), lax.axis_index("load")
    n_space, n_load = lax.axis_size("space"), lax.axis_size("load")
    span = ROWS + 2
    part = lambda ref, k: ref[k * span : (k + 1) * span]
    total = [
        part(energy_ref, 0),
        part(energy_ref, 1),
        part(energy_ref, 2) + (1.0 - end_flag()) * part(next_ref, 0),
        part(next_ref, 1),
    ]
    before = jnp.maximum(load - 1, 0)
    after = jnp.minimum(load + 1, n_load - 1)
    at_y = load * ROWS - 1 + row_ids((span, NZ))
    in_y = (at_y >= 0) & (at_y < n_load * ROWS)
    weighted, inside, own = [], [], []
    for plane in range(4):
        dens = jnp.concatenate(
            [
                dens_ref[before, 1 + plane][ROWS - 1 : ROWS],
                dens_ref[load, 1 + plane],
                dens_ref[after, 1 + plane][0:1],
            ],
            axis=0,
        )
        at_x = space * CX - 1 + plane
        scale = jnp.where((at_x >= 0) & (at_x < n_space * CX), 1.0, 0.0).astype(F32)
        present = scale * jnp.where(in_y, 1.0, 0.0)
        sensitivity = -PENALTY * (1.0 - EMIN) * (dens * dens) * total[plane]
        weighted.append(present * (dens * sensitivity))
        inside.append(present)
        if 1 <= plane <= CX:
            own.append(dens[1 : 1 + ROWS])
    sums, counts = weigh(weighted), weigh(inside)
    for plane in range(CX):
        out_ref[plane] = sums[plane] / (own[plane] * counts[plane])


def shifted(array, axis, distance):
    size = lax.axis_size(axis)
    return lax.ppermute(array, axis, [(i, (i + distance) % size) for i in range(size)])


def body(density, fixed_dofs, body_loads, point_nodes, point_forces):
    n_load, n_space = lax.axis_size("load"), lax.axis_size("space")
    dens_left = shifted(density, "space", 1)
    dens_right = shifted(density, "space", -1)
    plane = (3, NY, NZ)
    load, keep, to_right, to_left = kernel_call(
        loads_kernel, [(2,) + plane, (2,) + plane, (2,) + plane, (3,) + plane], 0, 4
    )(body_loads[0], fixed_dofs, point_nodes, point_forces[0])
    (dens,) = kernel_call(pack_kernel, [(n_load, 3 * CX, ROWS, NZ)], 0, 3)(
        dens_left, density, dens_right
    )
    dens, to_right, to_left = lax.optimization_barrier((dens, to_right, to_left))
    left = shifted(to_right, "space", 1)
    right = shifted(to_left, "space", -1)
    dens = lax.all_to_all(dens, "load", 0, 0)

    padded = (NY + ROWS, NZ)
    zed = lambda planes: pltpu.VMEM((planes, 3) + padded, F32)
    carry = pltpu.VMEM((3, 3, ROWS, NZ), F32)
    v0, v1, v1_far, modulus, inverse, mom = kernel_call(
        first_kernel,
        [(3,) + plane, (2,) + plane, plane, (6,) + padded, (4, NY, NZ), (8, 128)],
        0,
        5,
        [zed(5), zed(5), carry],
    )(load, keep, left, right, dens)
    v1_left = shifted(v1, "space", 1)
    v2, mom = kernel_call(
        second_kernel,
        [(3,) + plane, (n_space, 8, 128)],
        0,
        8,
        [zed(5), zed(5), zed(3), zed(3), carry],
    )(v1_left, v1, v1_far, left, keep, modulus, inverse, mom)
    mom = lax.all_to_all(mom, "space", 0, 0)
    span = ROWS + 2
    moved, energy = kernel_call(
        energy_kernel,
        [(3, CX, NY, NZ), (CHUNKS, 3 * span, NZ)],
        0,
        5,
        [zed(3), zed(3), pltpu.VMEM((3, NY + 2 * ROWS, NZ), F32)],
    )(v0, v1_left, v1, v2, mom)
    energy = jnp.sum(lax.all_to_all(energy, "load", 0, 0), axis=0)
    following = shifted(energy[: 2 * span], "space", -1)
    (filtered,) = kernel_call(filter_kernel, [(CX, ROWS, NZ)], 0, 3)(energy, following, dens)
    return (moved[None], filtered)


def solution(mesh):
    placed = (
        P("space", "load", None),
        P(None, "space", None, None),
        P("load", None, "space", None, None),
        P("load", None),
        P("load", None, None),
    )
    return jax.shard_map(
        body,
        mesh=mesh,
        in_specs=placed,
        out_specs=(P("load", None, "space", None, None), P("space", "load", None)),
        check_vma=False,
    )
```

```python
import math

import jax
import jax.numpy as jnp
from jax import lax
from jax.experimental import pallas as pl
from jax.experimental.pallas import tpu as pltpu
from jax.sharding import PartitionSpec as P

CX = 2
NY = 64
NZ = 256
ROWS = 8
CHUNKS = NY // ROWS
ZBITS = 8
EMIN = 0.001
PENALTY = 3.0
RADIUS = 1.5
POISSON = 0.3
LAME = POISSON / ((1.0 + POISSON) * (1.0 - 2.0 * POISSON))
SHEAR = 1.0 / (2.0 * (1.0 + POISSON))
KDIAG = (LAME + 4.0 * SHEAR) / 9.0
F32 = jnp.float32
VMEM_LIMIT = 16 * 1024 * 1024
PAIRS = ("ss", "sd", "ds", "dd")


def kernel_call(fn, outs, n_smem, n_in, scratch=()):
    vmem = pl.BlockSpec(memory_space=pltpu.VMEM)
    smem = pl.BlockSpec(memory_space=pltpu.SMEM)
    return pl.pallas_call(
        fn,
        out_shape=[jax.ShapeDtypeStruct(shape, F32) for shape in outs],
        in_specs=[smem] * n_smem + [vmem] * n_in,
        out_specs=[vmem] * len(outs),
        scratch_shapes=list(scratch),
        compiler_params=pltpu.CompilerParams(vmem_limit_bytes=VMEM_LIMIT),
    )


def lane_ids(shape):
    return lax.broadcasted_iota(jnp.int32, shape, 1)


def row_ids(shape):
    return lax.broadcasted_iota(jnp.int32, shape, 0)


def from_above(field):
    return jnp.where(lane_ids(field.shape) == NZ - 1, 0.0, pltpu.roll(field, NZ - 1, 1))


def from_below(field):
    return jnp.where(lane_ids(field.shape) == 0, 0.0, pltpu.roll(field, 1, 1))


def rows_at(chunk):
    return pl.ds(pl.multiple_of(chunk * ROWS, ROWS), ROWS)


def store_z_modes(zs_ref, zd_ref, plane, comp, rows, field):
    up = from_above(field)
    zs_ref[plane, comp, rows] = field + up
    zd_ref[plane, comp, rows] = up - field


def y_modes(cur, nxt):
    first = row_ids(cur.shape) == 0
    up = pltpu.roll(jnp.where(first, nxt, cur), ROWS - 1, 0)
    return cur + up, up - cur


def plane_modes(zs_ref, zd_ref, plane, chunk):
    out = []
    for comp in range(3):
        here, after = rows_at(chunk), rows_at(chunk + 1)
        ss, ds = y_modes(zs_ref[plane, comp, here], zs_ref[plane, comp, after])
        sd, dd = y_modes(zd_ref[plane, comp, here], zd_ref[plane, comp, after])
        out.append({"ss": ss, "sd": sd, "ds": ds, "dd": dd})
    return out


def element_modes(low, high):
    modes = []
    for comp in range(3):
        field = {}
        for pair in PAIRS:
            field["d" + pair] = high[comp][pair] - low[comp][pair]
            if pair != "ss":
                field["s" + pair] = high[comp][pair] + low[comp][pair]
        modes.append(field)
    return modes


NORMAL = ((0, "dss"), (1, "sds"), (2, "ssd"))
SHEARS = (((0, "sds"), (1, "dss")), ((0, "ssd"), (2, "dss")), ((1, "ssd"), (2, "sds")))
BENDS = (((0, "dsd"), (1, "sdd")), ((0, "dds"), (2, "sdd")), ((1, "dds"), (2, "dsd")))
TWISTS = ((0, "sdd"), (1, "dsd"), (2, "dds"))


def element_response(modes, modulus):
    k_lame = modulus * (LAME / 16.0)
    k_two = modulus * (SHEAR / 8.0)
    k_shear = modulus * (SHEAR / 16.0)
    k_bend = modulus * (LAME / 48.0)
    k_twist = modulus * (SHEAR / 48.0)
    k_last = modulus * ((LAME + 4.0 * SHEAR) / 144.0)
    force = [{}, {}, {}]
    get = lambda key: modes[key[0]][key[1]]
    trace = k_lame * (get(NORMAL[0]) + get(NORMAL[1]) + get(NORMAL[2]))
    for comp, name in NORMAL:
        force[comp][name] = k_two * modes[comp][name] + trace
    for one, two in SHEARS:
        both = k_shear * (get(one) + get(two))
        force[one[0]][one[1]] = both
        force[two[0]][two[1]] = both
    for one, two in BENDS:
        both = k_bend * (get(one) + get(two))
        force[one[0]][one[1]] = k_shear * get(one) + both
        force[two[0]][two[1]] = k_shear * get(two) + both
    total = get(TWISTS[0]) + get(TWISTS[1]) + get(TWISTS[2])
    for comp, name in TWISTS:
        force[comp][name] = k_twist * (modes[comp][name] + total)
    for comp in range(3):
        force[comp]["ddd"] = k_last * modes[comp]["ddd"]
    return force


def element_energy(modes):
    get = lambda key: modes[key[0]][key[1]]
    square = lambda value: value * value
    normal = [get(key) for key in NORMAL]
    twist = [get(key) for key in TWISTS]
    energy = (LAME / 16.0) * square(normal[0] + normal[1] + normal[2])
    energy += (SHEAR / 8.0) * (square(normal[0]) + square(normal[1]) + square(normal[2]))
    shear = sum(square(get(one) + get(two)) for one, two in SHEARS)
    shear += sum(square(get(one)) + square(get(two)) for one, two in BENDS)
    energy += (SHEAR / 16.0) * shear
    energy += (LAME / 48.0) * sum(square(get(one) + get(two)) for one, two in BENDS)
    twisted = square(twist[0]) + square(twist[1]) + square(twist[2])
    energy += (SHEAR / 48.0) * (twisted + square(twist[0] + twist[1] + twist[2]))
    last = square(modes[0]["ddd"]) + square(modes[1]["ddd"]) + square(modes[2]["ddd"])
    return energy + ((LAME + 4.0 * SHEAR) / 144.0) * last


def split_x(force):
    low, high = [], []
    for comp in range(3):
        lo, hi = {}, {}
        for pair in PAIRS:
            diff = force[comp]["d" + pair]
            if pair == "ss":
                lo[pair], hi[pair] = -diff, diff
            else:
                mean = force[comp]["s" + pair]
                lo[pair], hi[pair] = mean - diff, mean + diff
        low.append(lo)
        high.append(hi)
    return low, high


def node_force(acc, prev):
    sides = []
    for y_mode in ("s", "d"):
        mean, diff = acc[y_mode + "s"], acc[y_mode + "d"]
        sides.append((mean - diff) + from_below(mean + diff))
    low, high = sides[0] - sides[1], sides[0] + sides[1]
    last = row_ids(low.shape) == ROWS - 1
    return low + pltpu.roll(jnp.where(last, prev, high), 1, 0), high


def apply_rows(planes, moduli, carry_ref, chunk, first_edge=False, last_edge=False):
    slot = 0

    def finish(acc):
        nonlocal slot
        forces = []
        for comp in range(3):
            force, carry = node_force(acc[comp], carry_ref[slot, comp])
            carry_ref[slot, comp] = carry
            forces.append(force)
        slot += 1
        return forces

    low = plane_modes(*planes[0], chunk)
    partial = None
    for index, modulus in enumerate(moduli):
        high = plane_modes(*planes[index + 1], chunk)
        to_low, to_high = split_x(element_response(element_modes(low, high), modulus))
        if partial is not None:
            acc = [{p: partial[c][p] + to_low[c][p] for p in PAIRS} for c in range(3)]
            yield index, finish(acc)
        elif first_edge:
            yield index, finish(to_low)
        partial, low = to_high, high
    if last_edge:
        yield len(moduli), finish(partial)


def loads_kernel(
    body_ref, fixed_ref, node_ref, force_ref, load_ref, keep_ref, right_ref, left_ref
):
    cells = CX * NY * NZ
    local = node_ref[...] - lax.axis_index("space") * cells
    valid = (local >= 0) & (local < cells)
    local = jnp.where(valid, local, -1)
    line = lax.shift_right_arithmetic(local, ZBITS)
    depth = lax.bitwise_and(local, NZ - 1)
    points = local.shape[1]
    on_line = row_ids((CX * NY, points)) == line
    lines = [jnp.where(on_line, force_ref[comp : comp + 1, :], 0.0) for comp in range(3)]
    at_depth = jnp.where(row_ids((NZ, points)) == depth, 1.0, 0.0)
    added = lax.dot_general(
        jnp.concatenate(lines, axis=0),
        at_depth,
        (((1,), (1,)), ((), ())),
        precision=lax.Precision.HIGHEST,
        preferred_element_type=F32,
    )
    for plane in range(CX):
        for comp in range(3):
            keep = 1.0 - fixed_ref[comp, plane].astype(F32)
            first = (comp * CX + plane) * NY
            load = keep * (body_ref[comp, plane] + added[first : first + NY])
            load_ref[plane, comp] = load
            keep_ref[plane, comp] = keep
            left_ref[plane, comp] = load
            if plane == 0:
                left_ref[2, comp] = keep
            else:
                right_ref[0, comp] = load
                right_ref[1, comp] = keep


def pack_kernel(before_ref, own_ref, after_ref, pack_ref):
    for block in range(pack_ref.shape[0]):
        for plane in range(CX):
            pack_ref[block, plane] = before_ref[plane]
            pack_ref[block, CX + plane] = own_ref[plane]
            pack_ref[block, 2 * CX + plane] = after_ref[plane]


def clear_tails(refs):
    for ref in refs:
        for plane in range(ref.shape[0]):
            for comp in range(3):
                ref[plane, comp, NY : NY + ROWS] = jnp.zeros((ROWS, NZ), F32)


def clear_carry(ref):
    for plane in range(ref.shape[0]):
        for comp in range(3):
            ref[plane, comp] = jnp.zeros((ROWS, NZ), F32)


def folded(values):
    rows = [jnp.sum(v[:, :128] + v[:, 128:], axis=0, keepdims=True) for v in values]
    return jnp.concatenate(rows, axis=0)


def advance(forces, kept, before, inverse):
    image = jnp.where(kept, forces, before)
    return image, jnp.where(kept, forces * inverse, before)


def modulus_rows(e_ref, plane, chunk):
    return e_ref[plane, rows_at(chunk + 1)]


def inverse_diagonal(e_ref, plane, chunk):
    last = row_ids((ROWS, NZ)) == ROWS - 1
    cur = modulus_rows(e_ref, plane, chunk) + modulus_rows(e_ref, plane + 1, chunk)
    before = modulus_rows(e_ref, plane, chunk - 1) + modulus_rows(e_ref, plane + 1, chunk - 1)
    cur = cur + pltpu.roll(jnp.where(last, before, cur), 1, 0)
    diag = KDIAG * (cur + from_below(cur))
    return 1.0 / jnp.where(diag > 0.0, diag, 1.0)


def first_kernel(
    load_ref, keep_ref, left_ref, right_ref, dens_ref,
    v1_ref, v0_ref, e_ref, inv_ref, zs, zd, mom_ref,
    carry,
):
    first_x = lax.axis_index("space") * CX
    limit = lax.axis_size("space") * CX
    for plane in range(6):
        at = first_x - 2 + plane
        scale = jnp.where((at >= 0) & (at < limit), 1.0, 0.0).astype(F32)
        e_ref[plane, 0:ROWS] = jnp.zeros((ROWS, NZ), F32)
        for block in range(CHUNKS):
            dens = dens_ref[block, plane]
            rows = slice((block + 1) * ROWS, (block + 2) * ROWS)
            e_ref[plane, rows] = scale * (EMIN + (1.0 - EMIN) * (dens * dens * dens))
    clear_tails([zs, zd])
    clear_carry(carry)
    loads = [left_ref.at[0], load_ref.at[0], load_ref.at[1], right_ref.at[0]]
    has_right = 1.0 - end_flag()
    zero = jnp.zeros((ROWS, NZ), F32)

    def start(chunk, total):
        here = rows_at(chunk)
        for plane in range(4):
            inverse = inverse_diagonal(e_ref, plane, chunk)
            inv_ref[plane, here] = inverse
            for comp in range(3):
                load = loads[plane][comp, here]
                if plane == 3:
                    load = load * has_right
                value = load * inverse
                if plane < 3:
                    v0_ref[plane, comp, here] = value
                if plane in (1, 2):
                    total = total + load * value
                store_z_modes(zs, zd, plane, comp, here, value)
        return total

    mom0 = lax.fori_loop(0, CHUNKS, start, zero)

    def apply(chunk, totals):
        here = rows_at(chunk)
        odd, even = totals
        moduli = [modulus_rows(e_ref, plane, chunk) for plane in (1, 2, 3)]
        for plane, forces in apply_rows([(zs, zd, k) for k in range(4)], moduli, carry, chunk):
            inverse = inv_ref[plane, here]
            for comp in range(3):
                kept = keep_ref[plane - 1, comp, here] > 0.0
                before = v0_ref[plane, comp, here]
                image, value = advance(forces[comp], kept, before, inverse)
                v1_ref[plane - 1, comp, here] = value
                odd = odd + before * image
                even = even + value * image
        return odd, even

    mom1, mom2 = lax.fori_loop(0, CHUNKS, apply, (zero, zero))
    mom_ref[...] = folded([mom0, mom1, mom2] + [zero] * 5)


def middle_kernel(
    v1_ref, zs0, zd0, e_ref, inv_ref, right_ref, keep_ref, sofar_ref,
    v2_ref, zs1, zd1, zs2, zd2, force_ref, mom_ref,
    zs, zd, zs_far, zd_far, carry,
):
    clear_tails([zs, zd, zs1, zd1, zs2, zd2, zs_far, zd_far])
    clear_carry(carry)
    has_right = 1.0 - end_flag()
    zero = jnp.zeros((ROWS, NZ), F32)

    def start(chunk, done):
        here = rows_at(chunk)
        inverse = inverse_diagonal(e_ref, 4, chunk)
        for comp in range(3):
            store_z_modes(zs, zd, 0, comp, here, right_ref[1, comp, here] * has_right * inverse)
            store_z_modes(zs1, zd1, 0, comp, here, v1_ref[0, comp, here])
            store_z_modes(zs_far, zd_far, 0, comp, here, v1_ref[1, comp, here])
        return done

    lax.fori_loop(0, CHUNKS, start, 0)

    def outer(chunk, done):
        here = rows_at(chunk)
        moduli = [modulus_rows(e_ref, plane, chunk) for plane in (3, 4)]
        planes = [(zs0, zd0, 2), (zs0, zd0, 3), (zs, zd, 0)]
        for _, forces in apply_rows(planes, moduli, carry.at[0:1], chunk):
            inverse = inv_ref[3, here]
            for comp in range(3):
                kept = right_ref[2, comp, here] * has_right > 0.0
                before = right_ref[0, comp, here] * has_right * inverse
                _, value = advance(forces[comp], kept, before, inverse)
                store_z_modes(zs_far, zd_far, 1, comp, here, value)
        return done

    lax.fori_loop(0, CHUNKS, outer, 0)

    def apply(chunk, totals):
        here = rows_at(chunk)
        odd, even = totals
        moduli = [modulus_rows(e_ref, plane, chunk) for plane in (2, 3)]
        planes = [(zs1, zd1, 0), (zs_far, zd_far, 0), (zs_far, zd_far, 1)]
        for plane, forces in apply_rows(planes, moduli, carry.at[1:3], chunk, first_edge=True):
            if plane == 0:
                for comp in range(3):
                    force_ref[comp, here] = forces[comp]
                continue
            inverse = inv_ref[2, here]
            for comp in range(3):
                kept = keep_ref[1, comp, here] > 0.0
                before = v1_ref[1, comp, here]
                image, value = advance(forces[comp], kept, before, inverse)
                v2_ref[comp, here] = value
                store_z_modes(zs2, zd2, 0, comp, here, value)
                odd = odd + before * image
                even = even + value * image
        return odd, even

    mom3, mom4 = lax.fori_loop(0, CHUNKS, apply, (zero, zero))
    at_end = end_flag()

    def last(chunk, total):
        modes = plane_modes(zs2, zd2, 0, chunk)
        energy = element_energy(element_modes(modes, zero_modes()))
        return total + modulus_rows(e_ref, 3, chunk) * energy

    mom5 = at_end * lax.fori_loop(0, CHUNKS, last, zero)
    mom_ref[...] = sofar_ref[...] + folded([zero] * 3 + [mom3, mom4, mom5] + [zero] * 2)


def second_kernel(
    v1_left_ref, v1_ref, keep_left_ref, keep_ref, e_ref, inv_ref,
    zs1, zd1, zs2_far, zd2_far, force_ref, sofar_ref,
    v2_ref, mom_ref,
    zs, zd, zs2, zd2, carry,
):
    clear_tails([zs, zd, zs2, zd2])
    clear_carry(carry)
    zero = jnp.zeros((ROWS, NZ), F32)

    def start(chunk, done):
        here = rows_at(chunk)
        for plane in range(2):
            for comp in range(3):
                store_z_modes(zs, zd, plane, comp, here, v1_left_ref[plane, comp, here])
        return done

    lax.fori_loop(0, CHUNKS, start, 0)

    def apply(chunk, totals):
        here = rows_at(chunk)
        odd, even = totals
        moduli = [modulus_rows(e_ref, plane, chunk) for plane in (0, 1)]
        planes = [(zs, zd, 0), (zs, zd, 1), (zs1, zd1, 0)]
        for plane, forces in apply_rows(planes, moduli, carry, chunk, last_edge=True):
            inverse = inv_ref[plane - 1, here]
            for comp in range(3):
                if plane == 1:
                    kept, before = keep_left_ref[1, comp, here] > 0.0, v1_left_ref[1, comp, here]
                    force = forces[comp]
                else:
                    kept, before = keep_ref[0, comp, here] > 0.0, v1_ref[0, comp, here]
                    force = forces[comp] + force_ref[comp, here]
                image, value = advance(force, kept, before, inverse)
                v2_ref[plane - 1, comp, here] = value
                store_z_modes(zs2, zd2, plane - 1, comp, here, value)
                if plane == 2:
                    odd = odd + before * image
                    even = even + value * image
        return odd, even

    mom3, mom4 = lax.fori_loop(0, CHUNKS, apply, (zero, zero))

    def last(chunk, total):
        low = plane_modes(zs2, zd2, 0, chunk)
        for plane, where in enumerate(((zs2, zd2, 1), (zs2_far, zd2_far, 0))):
            high = plane_modes(*where, chunk)
            energy = element_energy(element_modes(low, high))
            total = total + modulus_rows(e_ref, 1 + plane, chunk) * energy
            low = high
        return total

    mom5 = lax.fori_loop(0, CHUNKS, last, zero)
    total = sofar_ref[...] + folded([zero] * 3 + [mom3, mom4, mom5] + [zero] * 2)
    for device in range(mom_ref.shape[0]):
        mom_ref[device] = total


def zero_modes():
    return [{pair: jnp.zeros((ROWS, NZ), F32) for pair in PAIRS}] * 3


def end_flag():
    at_end = lax.axis_index("space") == lax.axis_size("space") - 1
    return jnp.where(at_end, 1.0, 0.0).astype(F32)


def energies(zs, zd, chunk):
    planes = [plane_modes(zs, zd, plane, chunk) for plane in range(3)]
    planes.append(zero_modes())
    for low, high in zip(planes[:-1], planes[1:]):
        yield element_energy(element_modes(low, high))


def energy_kernel(v0_ref, v1_left_ref, v1_ref, v2_ref, v2_far_ref, mom_ref, u_ref, out_ref, zs, zd, e_ref):
    total = mom_ref[0]
    for device in range(1, mom_ref.shape[0]):
        total = total + mom_ref[device]
    total = jnp.broadcast_to(jnp.sum(total, axis=1, keepdims=True), (8, 128))
    m0, m1, m2, m3, m4, m5 = [total[k : k + 1] for k in range(6)]
    low10 = m2 / m1
    low20 = m3 / m1
    piv1 = m3 - low10 * m2
    mix = m4 - low20 * m2
    good1 = piv1 > 1e-7 * m3
    safe1 = jnp.where(good1, piv1, 1.0)
    low21 = jnp.where(good1, mix / safe1, 0.0)
    piv2 = m5 - low20 * m3 - low21 * mix
    good2 = good1 & (piv2 > 1e-7 * m5)
    y1 = m1 - low10 * m0
    y2 = m2 - low20 * m0 - low21 * y1
    c2 = jnp.where(good2, y2 / jnp.where(good2, piv2, 1.0), 0.0)
    c1 = jnp.where(good1, y1 / safe1 - low21 * c2, 0.0)
    c0 = m0 / m1 - low10 * c1 - low20 * c2
    c0, c1, c2 = [jnp.broadcast_to(jnp.concatenate([c, c], axis=1), (ROWS, NZ)) for c in (c0, c1, c2)]

    clear_tails([zs, zd])
    for plane in range(3):
        e_ref[plane, 0:ROWS] = jnp.zeros((ROWS, NZ), F32)
        e_ref[plane, NY + ROWS : NY + 2 * ROWS] = jnp.zeros((ROWS, NZ), F32)
    v1_planes = [v1_left_ref.at[1], v1_ref.at[0], v1_ref.at[1]]
    v2_planes = [v2_ref.at[0], v2_ref.at[1], v2_far_ref]

    def combine(chunk, done):
        here = rows_at(chunk)
        for plane in range(3):
            for comp in range(3):
                value = c0 * v0_ref[plane, comp, here] + c1 * v1_planes[plane][comp, here]
                value = value + c2 * v2_planes[plane][comp, here]
                if plane > 0:
                    u_ref[comp, plane - 1, here] = value
                store_z_modes(zs, zd, plane, comp, here, value)
        return done

    lax.fori_loop(0, CHUNKS, combine, 0)
    at_end = end_flag()

    def measure(chunk, done):
        for plane, energy in enumerate(energies(zs, zd, chunk)):
            e_ref[plane, rows_at(chunk + 1)] = energy * (at_end if plane == 2 else 1.0)
        return done

    lax.fori_loop(0, CHUNKS, measure, 0)
    span = ROWS + 2
    for block in range(CHUNKS):
        for plane in range(3):
            first = ROWS - 1 + block * ROWS
            out_ref[block, plane * span : (plane + 1) * span] = e_ref[plane, first : first + span]


def weigh(planes):
    near = RADIUS - 1.0
    edge = RADIUS - math.sqrt(2.0)
    beside = [from_below(p) + from_above(p) for p in planes]
    cross = []
    full = []
    for p, side in zip(planes, beside):
        up_down = p[0:ROWS] + p[2 : 2 + ROWS]
        mid, mid_side = p[1 : 1 + ROWS], side[1 : 1 + ROWS]
        cross.append(near * mid + edge * (mid_side + up_down))
        diagonal = side[0:ROWS] + side[2 : 2 + ROWS]
        full.append(RADIUS * mid + near * (mid_side + up_down) + edge * diagonal)
    return [full[k] + cross[k - 1] + cross[k + 1] for k in range(1, 1 + CX)]


def filter_kernel(energy_ref, next_ref, dens_ref, out_ref):
    space, load = lax.axis_index("space"), lax.axis_index("load")
    n_space, n_load = lax.axis_size("space"), lax.axis_size("load")
    span = ROWS + 2
    part = lambda ref, k: ref[k * span : (k + 1) * span]
    total = [
        part(energy_ref, 0),
        part(energy_ref, 1),
        part(energy_ref, 2) + (1.0 - end_flag()) * part(next_ref, 0),
        part(next_ref, 1),
    ]
    before = jnp.maximum(load - 1, 0)
    after = jnp.minimum(load + 1, n_load - 1)
    at_y = load * ROWS - 1 + row_ids((span, NZ))
    in_y = (at_y >= 0) & (at_y < n_load * ROWS)
    weighted, inside, own = [], [], []
    for plane in range(4):
        dens = jnp.concatenate(
            [
                dens_ref[before, 1 + plane][ROWS - 1 : ROWS],
                dens_ref[load, 1 + plane],
                dens_ref[after, 1 + plane][0:1],
            ],
            axis=0,
        )
        at_x = space * CX - 1 + plane
        scale = jnp.where((at_x >= 0) & (at_x < n_space * CX), 1.0, 0.0).astype(F32)
        present = scale * jnp.where(in_y, 1.0, 0.0)
        sensitivity = -PENALTY * (1.0 - EMIN) * (dens * dens) * total[plane]
        weighted.append(present * (dens * sensitivity))
        inside.append(present)
        if 1 <= plane <= CX:
            own.append(dens[1 : 1 + ROWS])
    sums, counts = weigh(weighted), weigh(inside)
    for plane in range(CX):
        out_ref[plane] = sums[plane] / (own[plane] * counts[plane])


def shifted(array, axis, distance):
    size = lax.axis_size(axis)
    return lax.ppermute(array, axis, [(i, (i + distance) % size) for i in range(size)])


def body(density, fixed_dofs, body_loads, point_nodes, point_forces):
    n_load, n_space = lax.axis_size("load"), lax.axis_size("space")
    dens_left = shifted(density, "space", 1)
    dens_right = shifted(density, "space", -1)
    plane = (3, NY, NZ)
    load, keep, to_right, to_left = kernel_call(
        loads_kernel, [(2,) + plane, (2,) + plane, (2,) + plane, (3,) + plane], 0, 4
    )(body_loads[0], fixed_dofs, point_nodes, point_forces[0])
    (dens,) = kernel_call(pack_kernel, [(n_load, 3 * CX, ROWS, NZ)], 0, 3)(
        dens_left, density, dens_right
    )
    dens, to_right, to_left = lax.optimization_barrier((dens, to_right, to_left))
    left = shifted(to_right, "space", 1)
    right = shifted(to_left, "space", -1)
    dens = lax.all_to_all(dens, "load", 0, 0)

    padded = (NY + ROWS, NZ)
    modes = lambda planes: (planes, 3) + padded
    zed = lambda planes: pltpu.VMEM(modes(planes), F32)
    carried = lambda slots: pltpu.VMEM((slots, 3, ROWS, NZ), F32)
    v1, v0, modulus, inverse, zs0, zd0, mom = kernel_call(
        first_kernel,
        [(2,) + plane, (3,) + plane, (6,) + padded, (4, NY, NZ), modes(4), modes(4), (8, 128)],
        0,
        5,
        [carried(2)],
    )(load, keep, left, right, dens)
    v1_left = shifted(v1, "space", 1)
    v2_far, zs1, zd1, zs2, zd2, force, mom = kernel_call(
        middle_kernel,
        [plane, modes(1), modes(1), modes(1), modes(1), plane, (8, 128)],
        0,
        8,
        [zed(1), zed(1), zed(2), zed(2), carried(3)],
    )(v1, zs0, zd0, modulus, inverse, right, keep, mom)
    v2, mom = kernel_call(
        second_kernel,
        [(2,) + plane, (n_space, 8, 128)],
        0,
        12,
        [zed(2), zed(2), zed(2), zed(2), carried(2)],
    )(v1_left, v1, left, keep, modulus, inverse, zs1, zd1, zs2, zd2, force, mom)
    mom = lax.all_to_all(mom, "space", 0, 0)
    span = ROWS + 2
    moved, energy = kernel_call(
        energy_kernel,
        [(3, CX, NY, NZ), (CHUNKS, 3 * span, NZ)],
        0,
        6,
        [zed(3), zed(3), pltpu.VMEM((3, NY + 2 * ROWS, NZ), F32)],
    )(v0, v1_left, v1, v2, v2_far, mom)
    energy = jnp.sum(lax.all_to_all(energy, "load", 0, 0), axis=0)
    following = shifted(energy[: 2 * span], "space", -1)
    (filtered,) = kernel_call(filter_kernel, [(CX, ROWS, NZ)], 0, 3)(energy, following, dens)
    return (moved[None], filtered)


def solution(mesh):
    placed = (
        P("space", "load", None),
        P(None, "space", None, None),
        P("load", None, "space", None, None),
        P("load", None),
        P("load", None, None),
    )
    return jax.shard_map(
        body,
        mesh=mesh,
        in_specs=placed,
        out_specs=(P("load", None, "space", None, None), P("space", "load", None)),
        check_vma=False,
    )
```

```python
import math

import jax
import jax.numpy as jnp
from jax import lax
from jax.experimental import pallas as pl
from jax.experimental.pallas import tpu as pltpu
from jax.sharding import PartitionSpec as P

CX = 2
NY = 64
NZ = 256
ROWS = 8
CHUNKS = NY // ROWS
ZBITS = 8
EMIN = 0.001
PENALTY = 3.0
RADIUS = 1.5
POISSON = 0.3
LAME = POISSON / ((1.0 + POISSON) * (1.0 - 2.0 * POISSON))
SHEAR = 1.0 / (2.0 * (1.0 + POISSON))
KDIAG = (LAME + 4.0 * SHEAR) / 9.0
F32 = jnp.float32
VMEM_LIMIT = 16 * 1024 * 1024
PAIRS = ("ss", "sd", "ds", "dd")


def kernel_call(fn, outs, n_hbm, n_in, scratch=()):
    vmem = pl.BlockSpec(memory_space=pltpu.VMEM)
    hbm = pl.BlockSpec(memory_space=pltpu.HBM)
    return pl.pallas_call(
        fn,
        out_shape=[jax.ShapeDtypeStruct(shape, F32) for shape in outs],
        in_specs=[hbm] * n_hbm + [vmem] * n_in,
        out_specs=[vmem] * len(outs),
        scratch_shapes=list(scratch),
        compiler_params=pltpu.CompilerParams(vmem_limit_bytes=VMEM_LIMIT),
    )


def lane_ids(shape):
    return lax.broadcasted_iota(jnp.int32, shape, 1)


def row_ids(shape):
    return lax.broadcasted_iota(jnp.int32, shape, 0)


def from_above(field):
    return jnp.where(lane_ids(field.shape) == NZ - 1, 0.0, pltpu.roll(field, NZ - 1, 1))


def from_below(field):
    return jnp.where(lane_ids(field.shape) == 0, 0.0, pltpu.roll(field, 1, 1))


def rows_at(chunk):
    return pl.ds(pl.multiple_of(chunk * ROWS, ROWS), ROWS)


def store_z_modes(zs_ref, zd_ref, plane, comp, rows, field):
    up = from_above(field)
    zs_ref[plane, comp, rows] = field + up
    zd_ref[plane, comp, rows] = up - field


def y_modes(cur, nxt):
    first = row_ids(cur.shape) == 0
    up = pltpu.roll(jnp.where(first, nxt, cur), ROWS - 1, 0)
    return cur + up, up - cur


def plane_modes(zs_ref, zd_ref, plane, chunk):
    out = []
    for comp in range(3):
        here, after = rows_at(chunk), rows_at(chunk + 1)
        ss, ds = y_modes(zs_ref[plane, comp, here], zs_ref[plane, comp, after])
        sd, dd = y_modes(zd_ref[plane, comp, here], zd_ref[plane, comp, after])
        out.append({"ss": ss, "sd": sd, "ds": ds, "dd": dd})
    return out


def element_modes(low, high):
    modes = []
    for comp in range(3):
        field = {}
        for pair in PAIRS:
            field["d" + pair] = high[comp][pair] - low[comp][pair]
            if pair != "ss":
                field["s" + pair] = high[comp][pair] + low[comp][pair]
        modes.append(field)
    return modes


NORMAL = ((0, "dss"), (1, "sds"), (2, "ssd"))
SHEARS = (((0, "sds"), (1, "dss")), ((0, "ssd"), (2, "dss")), ((1, "ssd"), (2, "sds")))
BENDS = (((0, "dsd"), (1, "sdd")), ((0, "dds"), (2, "sdd")), ((1, "dds"), (2, "dsd")))
TWISTS = ((0, "sdd"), (1, "dsd"), (2, "dds"))


def element_response(modes, modulus):
    k_lame = modulus * (LAME / 16.0)
    k_two = modulus * (SHEAR / 8.0)
    k_shear = modulus * (SHEAR / 16.0)
    k_bend = modulus * (LAME / 48.0)
    k_twist = modulus * (SHEAR / 48.0)
    k_last = modulus * ((LAME + 4.0 * SHEAR) / 144.0)
    force = [{}, {}, {}]
    get = lambda key: modes[key[0]][key[1]]
    trace = k_lame * (get(NORMAL[0]) + get(NORMAL[1]) + get(NORMAL[2]))
    for comp, name in NORMAL:
        force[comp][name] = k_two * modes[comp][name] + trace
    for one, two in SHEARS:
        both = k_shear * (get(one) + get(two))
        force[one[0]][one[1]] = both
        force[two[0]][two[1]] = both
    for one, two in BENDS:
        both = k_bend * (get(one) + get(two))
        force[one[0]][one[1]] = k_shear * get(one) + both
        force[two[0]][two[1]] = k_shear * get(two) + both
    total = get(TWISTS[0]) + get(TWISTS[1]) + get(TWISTS[2])
    for comp, name in TWISTS:
        force[comp][name] = k_twist * (modes[comp][name] + total)
    for comp in range(3):
        force[comp]["ddd"] = k_last * modes[comp]["ddd"]
    return force


def element_energy(modes):
    get = lambda key: modes[key[0]][key[1]]
    square = lambda value: value * value
    normal = [get(key) for key in NORMAL]
    twist = [get(key) for key in TWISTS]
    energy = (LAME / 16.0) * square(normal[0] + normal[1] + normal[2])
    energy += (SHEAR / 8.0) * (square(normal[0]) + square(normal[1]) + square(normal[2]))
    shear = sum(square(get(one) + get(two)) for one, two in SHEARS)
    shear += sum(square(get(one)) + square(get(two)) for one, two in BENDS)
    energy += (SHEAR / 16.0) * shear
    energy += (LAME / 48.0) * sum(square(get(one) + get(two)) for one, two in BENDS)
    twisted = square(twist[0]) + square(twist[1]) + square(twist[2])
    energy += (SHEAR / 48.0) * (twisted + square(twist[0] + twist[1] + twist[2]))
    last = square(modes[0]["ddd"]) + square(modes[1]["ddd"]) + square(modes[2]["ddd"])
    return energy + ((LAME + 4.0 * SHEAR) / 144.0) * last


def split_x(force):
    low, high = [], []
    for comp in range(3):
        lo, hi = {}, {}
        for pair in PAIRS:
            diff = force[comp]["d" + pair]
            if pair == "ss":
                lo[pair], hi[pair] = -diff, diff
            else:
                mean = force[comp]["s" + pair]
                lo[pair], hi[pair] = mean - diff, mean + diff
        low.append(lo)
        high.append(hi)
    return low, high


def node_force(acc, prev):
    sides = []
    for y_mode in ("s", "d"):
        mean, diff = acc[y_mode + "s"], acc[y_mode + "d"]
        sides.append((mean - diff) + from_below(mean + diff))
    low, high = sides[0] - sides[1], sides[0] + sides[1]
    last = row_ids(low.shape) == ROWS - 1
    return low + pltpu.roll(jnp.where(last, prev, high), 1, 0), high


def apply_rows(planes, moduli, carry_ref, chunk, first_edge=False, last_edge=False):
    slot = 0

    def finish(acc):
        nonlocal slot
        forces = []
        for comp in range(3):
            force, carry = node_force(acc[comp], carry_ref[slot, comp])
            carry_ref[slot, comp] = carry
            forces.append(force)
        slot += 1
        return forces

    low = plane_modes(*planes[0], chunk)
    partial = None
    for index, modulus in enumerate(moduli):
        high = plane_modes(*planes[index + 1], chunk)
        to_low, to_high = split_x(element_response(element_modes(low, high), modulus))
        if partial is not None:
            acc = [{p: partial[c][p] + to_low[c][p] for p in PAIRS} for c in range(3)]
            yield index, finish(acc)
        elif first_edge:
            yield index, finish(to_low)
        partial, low = to_high, high
    if last_edge:
        yield len(moduli), finish(partial)


def loads_kernel(
    body_hbm, fixed_hbm, node_hbm, force_hbm, load_ref, keep_ref, right_ref, left_ref,
    body_ref, fixed_ref, node_ref, force_ref, sems,
):
    pairs = ((node_hbm, node_ref), (force_hbm, force_ref), (body_hbm, body_ref), (fixed_hbm, fixed_ref))
    copies = [pltpu.make_async_copy(src, dst, sems.at[k]) for k, (src, dst) in enumerate(pairs)]
    for copy in copies:
        copy.start()
    copies[0].wait()
    copies[1].wait()
    cells = CX * NY * NZ
    local = node_ref[...] - lax.axis_index("space") * cells
    valid = (local >= 0) & (local < cells)
    local = jnp.where(valid, local, -1)
    line = lax.shift_right_arithmetic(local, ZBITS)
    depth = lax.bitwise_and(local, NZ - 1)
    points = local.shape[1]
    on_line = row_ids((CX * NY, points)) == line
    lines = [jnp.where(on_line, force_ref[comp], 0.0) for comp in range(3)]
    at_depth = jnp.where(row_ids((NZ, points)) == depth, 1.0, 0.0)
    added = lax.dot_general(
        jnp.concatenate(lines, axis=0),
        at_depth,
        (((1,), (1,)), ((), ())),
        precision=lax.Precision.HIGHEST,
        preferred_element_type=F32,
    )
    copies[2].wait()
    copies[3].wait()
    for plane in range(CX):
        for comp in range(3):
            keep = 1.0 - fixed_ref[comp, plane].astype(F32)
            first = (comp * CX + plane) * NY
            load = keep * (body_ref[0, comp, plane] + added[first : first + NY])
            load_ref[plane, comp] = load
            keep_ref[plane, comp] = keep
            left_ref[plane, comp] = load
            if plane == 0:
                left_ref[2, comp] = keep
            else:
                right_ref[0, comp] = load
                right_ref[1, comp] = keep


def pack_kernel(before_ref, own_ref, after_ref, pack_ref):
    for block in range(pack_ref.shape[0]):
        for plane in range(CX):
            pack_ref[block, plane] = before_ref[plane]
            pack_ref[block, CX + plane] = own_ref[plane]
            pack_ref[block, 2 * CX + plane] = after_ref[plane]


def clear_tails(refs):
    for ref in refs:
        for plane in range(ref.shape[0]):
            for comp in range(3):
                ref[plane, comp, NY : NY + ROWS] = jnp.zeros((ROWS, NZ), F32)


def clear_carry(ref):
    for plane in range(ref.shape[0]):
        for comp in range(3):
            ref[plane, comp] = jnp.zeros((ROWS, NZ), F32)


def folded(values):
    rows = [jnp.sum(v[:, :128] + v[:, 128:], axis=0, keepdims=True) for v in values]
    return jnp.concatenate(rows, axis=0)


def advance(forces, kept, before, inverse):
    image = jnp.where(kept, forces, before)
    return image, jnp.where(kept, forces * inverse, before)


def modulus_rows(e_ref, plane, chunk):
    return e_ref[plane, rows_at(chunk + 1)]


def inverse_diagonal(e_ref, plane, chunk):
    last = row_ids((ROWS, NZ)) == ROWS - 1
    cur = modulus_rows(e_ref, plane, chunk) + modulus_rows(e_ref, plane + 1, chunk)
    before = modulus_rows(e_ref, plane, chunk - 1) + modulus_rows(e_ref, plane + 1, chunk - 1)
    cur = cur + pltpu.roll(jnp.where(last, before, cur), 1, 0)
    diag = KDIAG * (cur + from_below(cur))
    return 1.0 / jnp.where(diag > 0.0, diag, 1.0)


def first_kernel(
    load_ref, keep_ref, left_ref, right_ref, dens_ref,
    v1_ref, v0_ref, e_ref, inv_ref, zs, zd, mom_ref,
    carry,
):
    first_x = lax.axis_index("space") * CX
    limit = lax.axis_size("space") * CX
    for plane in range(6):
        at = first_x - 2 + plane
        scale = jnp.where((at >= 0) & (at < limit), 1.0, 0.0).astype(F32)
        e_ref[plane, 0:ROWS] = jnp.zeros((ROWS, NZ), F32)
        for block in range(CHUNKS):
            dens = dens_ref[block, plane]
            rows = slice((block + 1) * ROWS, (block + 2) * ROWS)
            e_ref[plane, rows] = scale * (EMIN + (1.0 - EMIN) * (dens * dens * dens))
    clear_tails([zs, zd])
    clear_carry(carry)
    loads = [left_ref.at[0], load_ref.at[0], load_ref.at[1], right_ref.at[0]]
    has_right = 1.0 - end_flag()
    zero = jnp.zeros((ROWS, NZ), F32)

    def start(chunk, total):
        here = rows_at(chunk)
        for plane in range(4):
            inverse = inverse_diagonal(e_ref, plane, chunk)
            inv_ref[plane, here] = inverse
            for comp in range(3):
                load = loads[plane][comp, here]
                if plane == 3:
                    load = load * has_right
                value = load * inverse
                if plane < 3:
                    v0_ref[plane, comp, here] = value
                if plane in (1, 2):
                    total = total + load * value
                store_z_modes(zs, zd, plane, comp, here, value)
        return total

    mom0 = lax.fori_loop(0, CHUNKS, start, zero, unroll=CHUNKS // 2)

    def apply(chunk, totals):
        here = rows_at(chunk)
        odd, even = totals
        moduli = [modulus_rows(e_ref, plane, chunk) for plane in (1, 2, 3)]
        for plane, forces in apply_rows([(zs, zd, k) for k in range(4)], moduli, carry, chunk):
            inverse = inv_ref[plane, here]
            for comp in range(3):
                kept = keep_ref[plane - 1, comp, here] > 0.0
                before = v0_ref[plane, comp, here]
                image, value = advance(forces[comp], kept, before, inverse)
                v1_ref[plane - 1, comp, here] = value
                odd = odd + before * image
                even = even + value * image
        return odd, even

    mom1, mom2 = lax.fori_loop(0, CHUNKS, apply, (zero, zero), unroll=CHUNKS // 2)
    mom_ref[...] = folded([mom0, mom1, mom2] + [zero] * 5)


def middle_kernel(
    v1_ref, zs0, zd0, e_ref, inv_ref, right_ref, keep_ref, sofar_ref,
    v2_ref, zs1, zd1, zs2, zd2, force_ref, mom_ref,
    zs, zd, zs_far, zd_far, carry,
):
    clear_tails([zs, zd, zs1, zd1, zs2, zd2, zs_far, zd_far])
    clear_carry(carry)
    has_right = 1.0 - end_flag()
    zero = jnp.zeros((ROWS, NZ), F32)

    def start(chunk, done):
        here = rows_at(chunk)
        inverse = inverse_diagonal(e_ref, 4, chunk)
        for comp in range(3):
            store_z_modes(zs, zd, 0, comp, here, right_ref[1, comp, here] * has_right * inverse)
            store_z_modes(zs1, zd1, 0, comp, here, v1_ref[0, comp, here])
            store_z_modes(zs_far, zd_far, 0, comp, here, v1_ref[1, comp, here])
        return done

    lax.fori_loop(0, CHUNKS, start, 0, unroll=CHUNKS)

    def outer(chunk, done):
        here = rows_at(chunk)
        moduli = [modulus_rows(e_ref, plane, chunk) for plane in (3, 4)]
        planes = [(zs0, zd0, 2), (zs0, zd0, 3), (zs, zd, 0)]
        for _, forces in apply_rows(planes, moduli, carry.at[0:1], chunk):
            inverse = inv_ref[3, here]
            for comp in range(3):
                kept = right_ref[2, comp, here] * has_right > 0.0
                before = right_ref[0, comp, here] * has_right * inverse
                _, value = advance(forces[comp], kept, before, inverse)
                store_z_modes(zs_far, zd_far, 1, comp, here, value)
        return done

    lax.fori_loop(0, CHUNKS, outer, 0, unroll=CHUNKS)

    def apply(chunk, totals):
        here = rows_at(chunk)
        odd, even = totals
        moduli = [modulus_rows(e_ref, plane, chunk) for plane in (2, 3)]
        planes = [(zs1, zd1, 0), (zs_far, zd_far, 0), (zs_far, zd_far, 1)]
        for plane, forces in apply_rows(planes, moduli, carry.at[1:3], chunk, first_edge=True):
            if plane == 0:
                for comp in range(3):
                    force_ref[comp, here] = forces[comp]
                continue
            inverse = inv_ref[2, here]
            for comp in range(3):
                kept = keep_ref[1, comp, here] > 0.0
                before = v1_ref[1, comp, here]
                image, value = advance(forces[comp], kept, before, inverse)
                v2_ref[comp, here] = value
                store_z_modes(zs2, zd2, 0, comp, here, value)
                odd = odd + before * image
                even = even + value * image
        return odd, even

    mom3, mom4 = lax.fori_loop(0, CHUNKS, apply, (zero, zero), unroll=CHUNKS)
    at_end = end_flag()

    def last(chunk, total):
        modes = plane_modes(zs2, zd2, 0, chunk)
        energy = element_energy(element_modes(modes, zero_modes()))
        return total + modulus_rows(e_ref, 3, chunk) * energy

    mom5 = at_end * lax.fori_loop(0, CHUNKS, last, zero, unroll=CHUNKS)
    mom_ref[...] = sofar_ref[...] + folded([zero] * 3 + [mom3, mom4, mom5] + [zero] * 2)


def second_kernel(
    v1_left_ref, v1_ref, keep_left_ref, keep_ref, e_ref, inv_ref,
    zs1, zd1, zs2_far, zd2_far, force_ref, sofar_ref,
    v2_ref, mom_ref,
    zs, zd, zs2, zd2, carry,
):
    clear_tails([zs, zd, zs2, zd2])
    clear_carry(carry)
    zero = jnp.zeros((ROWS, NZ), F32)

    def start(chunk, done):
        here = rows_at(chunk)
        for plane in range(2):
            for comp in range(3):
                store_z_modes(zs, zd, plane, comp, here, v1_left_ref[plane, comp, here])
        return done

    lax.fori_loop(0, CHUNKS, start, 0, unroll=CHUNKS)

    def apply(chunk, totals):
        here = rows_at(chunk)
        odd, even = totals
        moduli = [modulus_rows(e_ref, plane, chunk) for plane in (0, 1)]
        planes = [(zs, zd, 0), (zs, zd, 1), (zs1, zd1, 0)]
        for plane, forces in apply_rows(planes, moduli, carry, chunk, last_edge=True):
            inverse = inv_ref[plane - 1, here]
            for comp in range(3):
                if plane == 1:
                    kept, before = keep_left_ref[1, comp, here] > 0.0, v1_left_ref[1, comp, here]
                    force = forces[comp]
                else:
                    kept, before = keep_ref[0, comp, here] > 0.0, v1_ref[0, comp, here]
                    force = forces[comp] + force_ref[comp, here]
                image, value = advance(force, kept, before, inverse)
                v2_ref[plane - 1, comp, here] = value
                store_z_modes(zs2, zd2, plane - 1, comp, here, value)
                if plane == 2:
                    odd = odd + before * image
                    even = even + value * image
        return odd, even

    mom3, mom4 = lax.fori_loop(0, CHUNKS, apply, (zero, zero), unroll=CHUNKS)

    def last(chunk, total):
        low = plane_modes(zs2, zd2, 0, chunk)
        for plane, where in enumerate(((zs2, zd2, 1), (zs2_far, zd2_far, 0))):
            high = plane_modes(*where, chunk)
            energy = element_energy(element_modes(low, high))
            total = total + modulus_rows(e_ref, 1 + plane, chunk) * energy
            low = high
        return total

    mom5 = lax.fori_loop(0, CHUNKS, last, zero, unroll=CHUNKS)
    total = sofar_ref[...] + folded([zero] * 3 + [mom3, mom4, mom5] + [zero] * 2)
    for device in range(mom_ref.shape[0]):
        mom_ref[device] = total


def zero_modes():
    return [{pair: jnp.zeros((ROWS, NZ), F32) for pair in PAIRS}] * 3


def end_flag():
    at_end = lax.axis_index("space") == lax.axis_size("space") - 1
    return jnp.where(at_end, 1.0, 0.0).astype(F32)


def energies(zs, zd, chunk):
    planes = [plane_modes(zs, zd, plane, chunk) for plane in range(3)]
    planes.append(zero_modes())
    for low, high in zip(planes[:-1], planes[1:]):
        yield element_energy(element_modes(low, high))


def energy_kernel(v0_ref, v1_left_ref, v1_ref, v2_ref, v2_far_ref, mom_ref, u_ref, out_ref, zs, zd, e_ref):
    total = mom_ref[0]
    for device in range(1, mom_ref.shape[0]):
        total = total + mom_ref[device]
    total = jnp.broadcast_to(jnp.sum(total, axis=1, keepdims=True), (8, 128))
    m0, m1, m2, m3, m4, m5 = [total[k : k + 1] for k in range(6)]
    low10 = m2 / m1
    low20 = m3 / m1
    piv1 = m3 - low10 * m2
    mix = m4 - low20 * m2
    good1 = piv1 > 1e-7 * m3
    safe1 = jnp.where(good1, piv1, 1.0)
    low21 = jnp.where(good1, mix / safe1, 0.0)
    piv2 = m5 - low20 * m3 - low21 * mix
    good2 = good1 & (piv2 > 1e-7 * m5)
    y1 = m1 - low10 * m0
    y2 = m2 - low20 * m0 - low21 * y1
    c2 = jnp.where(good2, y2 / jnp.where(good2, piv2, 1.0), 0.0)
    c1 = jnp.where(good1, y1 / safe1 - low21 * c2, 0.0)
    c0 = m0 / m1 - low10 * c1 - low20 * c2
    c0, c1, c2 = [jnp.broadcast_to(jnp.concatenate([c, c], axis=1), (ROWS, NZ)) for c in (c0, c1, c2)]

    clear_tails([zs, zd])
    for plane in range(3):
        e_ref[plane, 0:ROWS] = jnp.zeros((ROWS, NZ), F32)
        e_ref[plane, NY + ROWS : NY + 2 * ROWS] = jnp.zeros((ROWS, NZ), F32)
    v1_planes = [v1_left_ref.at[1], v1_ref.at[0], v1_ref.at[1]]
    v2_planes = [v2_ref.at[0], v2_ref.at[1], v2_far_ref]

    def combine(chunk, done):
        here = rows_at(chunk)
        for plane in range(3):
            for comp in range(3):
                value = c0 * v0_ref[plane, comp, here] + c1 * v1_planes[plane][comp, here]
                value = value + c2 * v2_planes[plane][comp, here]
                if plane > 0:
                    u_ref[comp, plane - 1, here] = value
                store_z_modes(zs, zd, plane, comp, here, value)
        return done

    lax.fori_loop(0, CHUNKS, combine, 0, unroll=CHUNKS)
    at_end = end_flag()

    def measure(chunk, done):
        for plane, energy in enumerate(energies(zs, zd, chunk)):
            e_ref[plane, rows_at(chunk + 1)] = energy * (at_end if plane == 2 else 1.0)
        return done

    lax.fori_loop(0, CHUNKS, measure, 0, unroll=CHUNKS)
    span = ROWS + 2
    for block in range(CHUNKS):
        for plane in range(3):
            first = ROWS - 1 + block * ROWS
            out_ref[block, plane * span : (plane + 1) * span] = e_ref[plane, first : first + span]


def weigh(planes):
    near = RADIUS - 1.0
    edge = RADIUS - math.sqrt(2.0)
    beside = [from_below(p) + from_above(p) for p in planes]
    cross = []
    full = []
    for p, side in zip(planes, beside):
        up_down = p[0:ROWS] + p[2 : 2 + ROWS]
        mid, mid_side = p[1 : 1 + ROWS], side[1 : 1 + ROWS]
        cross.append(near * mid + edge * (mid_side + up_down))
        diagonal = side[0:ROWS] + side[2 : 2 + ROWS]
        full.append(RADIUS * mid + near * (mid_side + up_down) + edge * diagonal)
    return [full[k] + cross[k - 1] + cross[k + 1] for k in range(1, 1 + CX)]


def filter_kernel(energy_ref, next_ref, dens_ref, out_ref):
    space, load = lax.axis_index("space"), lax.axis_index("load")
    n_space, n_load = lax.axis_size("space"), lax.axis_size("load")
    span = ROWS + 2
    part = lambda ref, k: ref[k * span : (k + 1) * span]
    total = [
        part(energy_ref, 0),
        part(energy_ref, 1),
        part(energy_ref, 2) + (1.0 - end_flag()) * part(next_ref, 0),
        part(next_ref, 1),
    ]
    before = jnp.maximum(load - 1, 0)
    after = jnp.minimum(load + 1, n_load - 1)
    at_y = load * ROWS - 1 + row_ids((span, NZ))
    in_y = (at_y >= 0) & (at_y < n_load * ROWS)
    weighted, inside, own = [], [], []
    for plane in range(4):
        dens = jnp.concatenate(
            [
                dens_ref[before, 1 + plane][ROWS - 1 : ROWS],
                dens_ref[load, 1 + plane],
                dens_ref[after, 1 + plane][0:1],
            ],
            axis=0,
        )
        at_x = space * CX - 1 + plane
        scale = jnp.where((at_x >= 0) & (at_x < n_space * CX), 1.0, 0.0).astype(F32)
        present = scale * jnp.where(in_y, 1.0, 0.0)
        sensitivity = -PENALTY * (1.0 - EMIN) * (dens * dens) * total[plane]
        weighted.append(present * (dens * sensitivity))
        inside.append(present)
        if 1 <= plane <= CX:
            own.append(dens[1 : 1 + ROWS])
    sums, counts = weigh(weighted), weigh(inside)
    for plane in range(CX):
        out_ref[plane] = sums[plane] / (own[plane] * counts[plane])


def shifted(array, axis, distance):
    size = lax.axis_size(axis)
    return lax.ppermute(array, axis, [(i, (i + distance) % size) for i in range(size)])


def body(density, fixed_dofs, body_loads, point_nodes, point_forces):
    n_load, n_space = lax.axis_size("load"), lax.axis_size("space")
    dens_left = shifted(density, "space", 1)
    dens_right = shifted(density, "space", -1)
    plane = (3, NY, NZ)
    by_component = jnp.swapaxes(point_forces, 0, 1)
    load, keep, to_right, to_left = kernel_call(
        loads_kernel,
        [(2,) + plane, (2,) + plane, (2,) + plane, (3,) + plane],
        4,
        0,
        [
            pltpu.VMEM(body_loads.shape, F32),
            pltpu.VMEM(fixed_dofs.shape, jnp.int32),
            pltpu.VMEM(point_nodes.shape, jnp.int32),
            pltpu.VMEM(by_component.shape, F32),
            pltpu.SemaphoreType.DMA((4,)),
        ],
    )(*[pltpu.with_memory_space_constraint(x, pltpu.HBM) for x in (body_loads, fixed_dofs, point_nodes, by_component)])
    (dens,) = kernel_call(pack_kernel, [(n_load, 3 * CX, ROWS, NZ)], 0, 3)(
        dens_left, density, dens_right
    )
    dens, to_right, to_left = lax.optimization_barrier((dens, to_right, to_left))
    left = shifted(to_right, "space", 1)
    right = shifted(to_left, "space", -1)
    dens = lax.all_to_all(dens, "load", 0, 0)

    padded = (NY + ROWS, NZ)
    modes = lambda planes: (planes, 3) + padded
    zed = lambda planes: pltpu.VMEM(modes(planes), F32)
    carried = lambda slots: pltpu.VMEM((slots, 3, ROWS, NZ), F32)
    v1, v0, modulus, inverse, zs0, zd0, mom = kernel_call(
        first_kernel,
        [(2,) + plane, (3,) + plane, (6,) + padded, (4, NY, NZ), modes(4), modes(4), (8, 128)],
        0,
        5,
        [carried(2)],
    )(load, keep, left, right, dens)
    v1_left = shifted(v1, "space", 1)
    v2_far, zs1, zd1, zs2, zd2, force, mom = kernel_call(
        middle_kernel,
        [plane, modes(1), modes(1), modes(1), modes(1), plane, (8, 128)],
        0,
        8,
        [zed(1), zed(1), zed(2), zed(2), carried(3)],
    )(v1, zs0, zd0, modulus, inverse, right, keep, mom)
    v2, mom = kernel_call(
        second_kernel,
        [(2,) + plane, (n_space, 8, 128)],
        0,
        12,
        [zed(2), zed(2), zed(2), zed(2), carried(2)],
    )(v1_left, v1, left, keep, modulus, inverse, zs1, zd1, zs2, zd2, force, mom)
    mom = lax.all_to_all(mom, "space", 0, 0)
    span = ROWS + 2
    moved, energy = kernel_call(
        energy_kernel,
        [(3, CX, NY, NZ), (CHUNKS, 3 * span, NZ)],
        0,
        6,
        [zed(3), zed(3), pltpu.VMEM((3, NY + 2 * ROWS, NZ), F32)],
    )(v0, v1_left, v1, v2, v2_far, mom)
    energy = jnp.sum(lax.all_to_all(energy, "load", 0, 0), axis=0)
    following = shifted(energy[: 2 * span], "space", -1)
    (filtered,) = kernel_call(filter_kernel, [(CX, ROWS, NZ)], 0, 3)(energy, following, dens)
    return (moved[None], filtered)


def solution(mesh):
    placed = (
        P("space", "load", None),
        P(None, "space", None, None),
        P("load", None, "space", None, None),
        P("load", None),
        P("load", None, None),
    )
    return jax.shard_map(
        body,
        mesh=mesh,
        in_specs=placed,
        out_specs=(P("load", None, "space", None, None), P("space", "load", None)),
        check_vma=False,
    )
```

```python
import math

import jax
import jax.numpy as jnp
from jax import lax
from jax.experimental import pallas as pl
from jax.experimental.pallas import tpu as pltpu
from jax.sharding import PartitionSpec as P

CX = 2
NY = 64
NZ = 256
ROWS = 8
CHUNKS = NY // ROWS
ZBITS = 8
EMIN = 0.001
PENALTY = 3.0
RADIUS = 1.5
POISSON = 0.3
LAME = POISSON / ((1.0 + POISSON) * (1.0 - 2.0 * POISSON))
SHEAR = 1.0 / (2.0 * (1.0 + POISSON))
KDIAG = (LAME + 4.0 * SHEAR) / 9.0
F32 = jnp.float32
VMEM_LIMIT = 16 * 1024 * 1024
PAIRS = ("ss", "sd", "ds", "dd")


def kernel_call(fn, outs, n_hbm, n_in, scratch=()):
    vmem = pl.BlockSpec(memory_space=pltpu.VMEM)
    hbm = pl.BlockSpec(memory_space=pltpu.HBM)
    return pl.pallas_call(
        fn,
        out_shape=[jax.ShapeDtypeStruct(shape, F32) for shape in outs],
        in_specs=[hbm] * n_hbm + [vmem] * n_in,
        out_specs=[vmem] * len(outs),
        scratch_shapes=list(scratch),
        compiler_params=pltpu.CompilerParams(vmem_limit_bytes=VMEM_LIMIT),
    )


def lane_ids(shape):
    return lax.broadcasted_iota(jnp.int32, shape, 1)


def row_ids(shape):
    return lax.broadcasted_iota(jnp.int32, shape, 0)


def from_above(field):
    return jnp.where(lane_ids(field.shape) == NZ - 1, 0.0, pltpu.roll(field, NZ - 1, 1))


def from_below(field):
    return jnp.where(lane_ids(field.shape) == 0, 0.0, pltpu.roll(field, 1, 1))


def rows_at(chunk):
    return pl.ds(pl.multiple_of(chunk * ROWS, ROWS), ROWS)


def store_z_modes(zs_ref, zd_ref, plane, comp, rows, field):
    up = from_above(field)
    zs_ref[plane, comp, rows] = field + up
    zd_ref[plane, comp, rows] = up - field


def y_modes(cur, nxt):
    first = row_ids(cur.shape) == 0
    up = pltpu.roll(jnp.where(first, nxt, cur), ROWS - 1, 0)
    return cur + up, up - cur


def plane_modes(zs_ref, zd_ref, plane, chunk):
    out = []
    for comp in range(3):
        here, after = rows_at(chunk), rows_at(chunk + 1)
        ss, ds = y_modes(zs_ref[plane, comp, here], zs_ref[plane, comp, after])
        sd, dd = y_modes(zd_ref[plane, comp, here], zd_ref[plane, comp, after])
        out.append({"ss": ss, "sd": sd, "ds": ds, "dd": dd})
    return out


def element_modes(low, high):
    modes = []
    for comp in range(3):
        field = {}
        for pair in PAIRS:
            field["d" + pair] = high[comp][pair] - low[comp][pair]
            if pair != "ss":
                field["s" + pair] = high[comp][pair] + low[comp][pair]
        modes.append(field)
    return modes


NORMAL = ((0, "dss"), (1, "sds"), (2, "ssd"))
SHEARS = (((0, "sds"), (1, "dss")), ((0, "ssd"), (2, "dss")), ((1, "ssd"), (2, "sds")))
BENDS = (((0, "dsd"), (1, "sdd")), ((0, "dds"), (2, "sdd")), ((1, "dds"), (2, "dsd")))
TWISTS = ((0, "sdd"), (1, "dsd"), (2, "dds"))


def element_response(modes, modulus):
    k_lame = modulus * (LAME / 16.0)
    k_two = modulus * (SHEAR / 8.0)
    k_shear = modulus * (SHEAR / 16.0)
    k_bend = modulus * (LAME / 48.0)
    k_twist = modulus * (SHEAR / 48.0)
    k_last = modulus * ((LAME + 4.0 * SHEAR) / 144.0)
    force = [{}, {}, {}]
    get = lambda key: modes[key[0]][key[1]]
    trace = k_lame * (get(NORMAL[0]) + get(NORMAL[1]) + get(NORMAL[2]))
    for comp, name in NORMAL:
        force[comp][name] = k_two * modes[comp][name] + trace
    for one, two in SHEARS:
        both = k_shear * (get(one) + get(two))
        force[one[0]][one[1]] = both
        force[two[0]][two[1]] = both
    for one, two in BENDS:
        both = k_bend * (get(one) + get(two))
        force[one[0]][one[1]] = k_shear * get(one) + both
        force[two[0]][two[1]] = k_shear * get(two) + both
    total = get(TWISTS[0]) + get(TWISTS[1]) + get(TWISTS[2])
    for comp, name in TWISTS:
        force[comp][name] = k_twist * (modes[comp][name] + total)
    for comp in range(3):
        force[comp]["ddd"] = k_last * modes[comp]["ddd"]
    return force


def element_energy(modes):
    get = lambda key: modes[key[0]][key[1]]
    square = lambda value: value * value
    normal = [get(key) for key in NORMAL]
    twist = [get(key) for key in TWISTS]
    energy = (LAME / 16.0) * square(normal[0] + normal[1] + normal[2])
    energy += (SHEAR / 8.0) * (square(normal[0]) + square(normal[1]) + square(normal[2]))
    shear = sum(square(get(one) + get(two)) for one, two in SHEARS)
    shear += sum(square(get(one)) + square(get(two)) for one, two in BENDS)
    energy += (SHEAR / 16.0) * shear
    energy += (LAME / 48.0) * sum(square(get(one) + get(two)) for one, two in BENDS)
    twisted = square(twist[0]) + square(twist[1]) + square(twist[2])
    energy += (SHEAR / 48.0) * (twisted + square(twist[0] + twist[1] + twist[2]))
    last = square(modes[0]["ddd"]) + square(modes[1]["ddd"]) + square(modes[2]["ddd"])
    return energy + ((LAME + 4.0 * SHEAR) / 144.0) * last


def split_x(force):
    low, high = [], []
    for comp in range(3):
        lo, hi = {}, {}
        for pair in PAIRS:
            diff = force[comp]["d" + pair]
            if pair == "ss":
                lo[pair], hi[pair] = -diff, diff
            else:
                mean = force[comp]["s" + pair]
                lo[pair], hi[pair] = mean - diff, mean + diff
        low.append(lo)
        high.append(hi)
    return low, high


def node_force(acc, prev):
    sides = []
    for y_mode in ("s", "d"):
        mean, diff = acc[y_mode + "s"], acc[y_mode + "d"]
        sides.append((mean - diff) + from_below(mean + diff))
    low, high = sides[0] - sides[1], sides[0] + sides[1]
    last = row_ids(low.shape) == ROWS - 1
    return low + pltpu.roll(jnp.where(last, prev, high), 1, 0), high


def apply_rows(planes, moduli, carry_ref, chunk, first_edge=False, last_scale=None):
    slot = 0

    def finish(acc):
        nonlocal slot
        forces = []
        for comp in range(3):
            force, carry = node_force(acc[comp], carry_ref[slot, comp])
            carry_ref[slot, comp] = carry
            forces.append(force)
        slot += 1
        return forces

    low = plane_modes(*planes[0], chunk)
    partial = None
    for index, modulus in enumerate(moduli):
        high = plane_modes(*planes[index + 1], chunk)
        if last_scale is not None and index + 1 == len(moduli):
            high = scaled_modes(high, last_scale)
        to_low, to_high = split_x(element_response(element_modes(low, high), modulus))
        if partial is not None:
            acc = [{p: partial[c][p] + to_low[c][p] for p in PAIRS} for c in range(3)]
            yield index, finish(acc)
        elif first_edge:
            yield index, finish(to_low)
        partial, low = to_high, high
    if last_scale is not None:
        yield len(moduli), [force * last_scale for force in finish(partial)]


def scaled_modes(modes, scale):
    return [{pair: field[pair] * scale for pair in PAIRS} for field in modes]


def has_left():
    return jnp.where(lax.axis_index("space") == 0, 0.0, 1.0).astype(F32)


def loads_kernel(
    body_hbm, fixed_hbm, node_hbm, force_hbm, load_ref, keep_ref, chip_ref, link_ref,
    body_ref, fixed_ref, node_ref, force_ref, sems,
):
    pairs = ((node_hbm, node_ref), (force_hbm, force_ref), (body_hbm, body_ref), (fixed_hbm, fixed_ref))
    copies = [pltpu.make_async_copy(src, dst, sems.at[k]) for k, (src, dst) in enumerate(pairs)]
    for copy in copies:
        copy.start()
    copies[0].wait()
    copies[1].wait()
    cells = CX * NY * NZ
    local = node_ref[...] - lax.axis_index("space") * cells
    valid = (local >= 0) & (local < cells)
    local = jnp.where(valid, local, -1)
    line = lax.shift_right_arithmetic(local, ZBITS)
    depth = lax.bitwise_and(local, NZ - 1)
    points = local.shape[1]
    on_line = row_ids((CX * NY, points)) == line
    lines = [jnp.where(on_line, force_ref[comp], 0.0) for comp in range(3)]
    at_depth = jnp.where(row_ids((NZ, points)) == depth, 1.0, 0.0)
    added = lax.dot_general(
        jnp.concatenate(lines, axis=0),
        at_depth,
        (((1,), (1,)), ((), ())),
        precision=lax.Precision.HIGHEST,
        preferred_element_type=F32,
    )
    copies[2].wait()
    copies[3].wait()
    on_even = is_even()
    for comp in range(3):
        loads, keeps = [], []
        for plane in range(CX):
            keep = 1.0 - fixed_ref[comp, plane].astype(F32)
            first = (comp * CX + plane) * NY
            loads.append(keep * (body_ref[0, comp, plane] + added[first : first + NY]))
            keeps.append(keep)
            load_ref[plane, comp] = loads[plane]
            keep_ref[plane, comp] = keep
        to_left, to_right = (loads[1], loads[0], keeps[0]), (loads[1], keeps[1], keeps[1])
        for part in range(3):
            chip_ref[part, comp] = jnp.where(on_even, to_right[part], to_left[part])
            link_ref[part, comp] = jnp.where(on_even, to_left[part], to_right[part])


def is_even():
    return lax.rem(lax.axis_index("space"), 2) == 0


def swapped(array, across):
    size = lax.axis_size("space")
    partner = lambda i: (i + (1 if (i % 2 == 0) != across else -1)) % size
    return lax.ppermute(array, "space", [(i, partner(i)) for i in range(size)])


def pack_kernel(chip_ref, own_ref, link_ref, pack_ref):
    on_even = is_even()
    for plane in range(CX):
        before = jnp.where(on_even, link_ref[plane], chip_ref[plane])
        after = jnp.where(on_even, chip_ref[plane], link_ref[plane])
        for block in range(pack_ref.shape[0]):
            pack_ref[block, plane] = before
            pack_ref[block, CX + plane] = own_ref[plane]
            pack_ref[block, 2 * CX + plane] = after


def clear_tails(refs):
    for ref in refs:
        for plane in range(ref.shape[0]):
            for comp in range(3):
                ref[plane, comp, NY : NY + ROWS] = jnp.zeros((ROWS, NZ), F32)


def clear_carry(ref):
    for plane in range(ref.shape[0]):
        for comp in range(3):
            ref[plane, comp] = jnp.zeros((ROWS, NZ), F32)


def folded(values):
    rows = [jnp.sum(v[:, :128] + v[:, 128:], axis=0, keepdims=True) for v in values]
    return jnp.concatenate(rows, axis=0)


def advance(forces, kept, before, inverse):
    image = jnp.where(kept, forces, before)
    return image, jnp.where(kept, forces * inverse, before)


def modulus_rows(e_ref, plane, chunk):
    return e_ref[plane, rows_at(chunk + 1)]


def inverse_diagonal(e_ref, plane, chunk, scale=1.0):
    last = row_ids((ROWS, NZ)) == ROWS - 1
    cur = scale * modulus_rows(e_ref, plane, chunk) + modulus_rows(e_ref, plane + 1, chunk)
    before = scale * modulus_rows(e_ref, plane, chunk - 1) + modulus_rows(e_ref, plane + 1, chunk - 1)
    cur = cur + pltpu.roll(jnp.where(last, before, cur), 1, 0)
    diag = KDIAG * (cur + from_below(cur))
    return 1.0 / jnp.where(diag > 0.0, diag, 1.0)


def first_kernel(
    load_ref, keep_ref, chip_ref, link_ref, dens_ref,
    v1_ref, v0_ref, e_ref, inv_ref, zs, zd, mom_ref,
    carry,
):
    first_x = lax.axis_index("space") * CX
    limit = lax.axis_size("space") * CX
    for plane in range(6):
        at = first_x - 2 + plane
        scale = jnp.where(at < limit, 1.0, 0.0).astype(F32)
        e_ref[plane, 0:ROWS] = jnp.zeros((ROWS, NZ), F32)
        for block in range(CHUNKS):
            dens = dens_ref[block, plane]
            rows = slice((block + 1) * ROWS, (block + 2) * ROWS)
            e_ref[plane, rows] = scale * (EMIN + (1.0 - EMIN) * (dens * dens * dens))
    clear_tails([zs, zd])
    clear_carry(carry)
    on_even = is_even()
    has_right, joined = 1.0 - end_flag(), has_left()
    zero = jnp.zeros((ROWS, NZ), F32)

    def start(chunk, total):
        here = rows_at(chunk)
        for plane in range(4):
            inverse = inverse_diagonal(e_ref, plane, chunk, joined if plane == 1 else 1.0)
            inv_ref[plane, here] = inverse
            for comp in range(3):
                if plane == 0:
                    load = jnp.where(on_even, link_ref[0, comp, here], chip_ref[0, comp, here])
                elif plane == 3:
                    load = has_right * jnp.where(on_even, chip_ref[1, comp, here], link_ref[1, comp, here])
                else:
                    load = load_ref[plane - 1, comp, here]
                value = load * inverse
                if plane < 3:
                    v0_ref[plane, comp, here] = value
                if plane in (1, 2):
                    total = total + load * value
                store_z_modes(zs, zd, plane, comp, here, value)
        return total

    mom0 = lax.fori_loop(0, CHUNKS, start, zero, unroll=CHUNKS // 2)

    def apply(chunk, totals):
        here = rows_at(chunk)
        odd, even = totals
        moduli = [modulus_rows(e_ref, plane, chunk) for plane in (1, 2, 3)]
        moduli[0] = moduli[0] * joined
        for plane, forces in apply_rows([(zs, zd, k) for k in range(4)], moduli, carry, chunk):
            inverse = inv_ref[plane, here]
            for comp in range(3):
                kept = keep_ref[plane - 1, comp, here] > 0.0
                before = v0_ref[plane, comp, here]
                image, value = advance(forces[comp], kept, before, inverse)
                v1_ref[plane - 1, comp, here] = value
                odd = odd + before * image
                even = even + value * image
        return odd, even

    mom1, mom2 = lax.fori_loop(0, CHUNKS, apply, (zero, zero), unroll=CHUNKS)
    mom_ref[...] = folded([mom0, mom1, mom2] + [zero] * 5)


def middle_kernel(
    v1_ref, zs0, zd0, e_ref, inv_ref, chip_ref, link_ref, keep_ref, sofar_ref,
    v2_ref, zs1, zd1, zs2, zd2, force_ref, mom_ref,
    zs, zd, zs_far, zd_far, carry,
):
    clear_tails([zs, zd, zs1, zd1, zs2, zd2, zs_far, zd_far])
    clear_carry(carry)
    has_right, on_even = 1.0 - end_flag(), is_even()
    zero = jnp.zeros((ROWS, NZ), F32)

    def right(part, comp, here):
        return has_right * jnp.where(on_even, chip_ref[part, comp, here], link_ref[part, comp, here])

    def start(chunk, done):
        here = rows_at(chunk)
        inverse = inverse_diagonal(e_ref, 4, chunk)
        for comp in range(3):
            store_z_modes(zs, zd, 0, comp, here, right(0, comp, here) * inverse)
            store_z_modes(zs1, zd1, 0, comp, here, v1_ref[0, comp, here])
            store_z_modes(zs_far, zd_far, 0, comp, here, v1_ref[1, comp, here])
        return done

    lax.fori_loop(0, CHUNKS, start, 0, unroll=CHUNKS)

    def outer(chunk, done):
        here = rows_at(chunk)
        moduli = [modulus_rows(e_ref, plane, chunk) for plane in (3, 4)]
        planes = [(zs0, zd0, 2), (zs0, zd0, 3), (zs, zd, 0)]
        for _, forces in apply_rows(planes, moduli, carry.at[0:1], chunk):
            inverse = inv_ref[3, here]
            for comp in range(3):
                kept = right(2, comp, here) > 0.0
                before = right(1, comp, here) * inverse
                _, value = advance(forces[comp], kept, before, inverse)
                store_z_modes(zs_far, zd_far, 1, comp, here, value)
        return done

    lax.fori_loop(0, CHUNKS, outer, 0, unroll=CHUNKS)

    def apply(chunk, totals):
        here = rows_at(chunk)
        odd, even = totals
        moduli = [modulus_rows(e_ref, plane, chunk) for plane in (2, 3)]
        planes = [(zs1, zd1, 0), (zs_far, zd_far, 0), (zs_far, zd_far, 1)]
        for plane, forces in apply_rows(planes, moduli, carry.at[1:3], chunk, first_edge=True):
            if plane == 0:
                for comp in range(3):
                    force_ref[comp, here] = forces[comp]
                continue
            inverse = inv_ref[2, here]
            for comp in range(3):
                kept = keep_ref[1, comp, here] > 0.0
                before = v1_ref[1, comp, here]
                image, value = advance(forces[comp], kept, before, inverse)
                v2_ref[comp, here] = value
                store_z_modes(zs2, zd2, 0, comp, here, value)
                odd = odd + before * image
                even = even + value * image
        return odd, even

    mom3, mom4 = lax.fori_loop(0, CHUNKS, apply, (zero, zero), unroll=CHUNKS)
    mom_ref[...] = sofar_ref[...] + folded([zero] * 3 + [mom3, mom4] + [zero] * 3)


def second_kernel(
    v1_left_ref, v1_ref, chip_ref, link_ref, keep_ref, e_ref, inv_ref,
    zs1, zd1, zs2_far, zd2_far, force_ref, sofar_ref,
    v2_ref, mom_ref,
    zs, zd, zs2, zd2, carry,
):
    on_even, joined = is_even(), has_left()
    clear_tails([zs, zd, zs2, zd2])
    clear_carry(carry)
    zero = jnp.zeros((ROWS, NZ), F32)

    def start(chunk, done):
        here = rows_at(chunk)
        for plane in range(2):
            for comp in range(3):
                store_z_modes(zs, zd, plane, comp, here, v1_left_ref[plane, comp, here])
        return done

    lax.fori_loop(0, CHUNKS, start, 0, unroll=CHUNKS)

    def apply(chunk, totals):
        here = rows_at(chunk)
        odd, even = totals
        moduli = [modulus_rows(e_ref, plane, chunk) for plane in (0, 1)]
        planes = [(zs, zd, 0), (zs, zd, 1), (zs1, zd1, 0)]
        for plane, forces in apply_rows(planes, moduli, carry, chunk, last_scale=joined):
            inverse = inv_ref[plane - 1, here]
            for comp in range(3):
                if plane == 1:
                    keep = jnp.where(on_even, link_ref[1, comp, here], chip_ref[1, comp, here])
                    kept, before = keep > 0.0, v1_left_ref[1, comp, here]
                    force = forces[comp]
                else:
                    kept, before = keep_ref[0, comp, here] > 0.0, v1_ref[0, comp, here]
                    force = forces[comp] + force_ref[comp, here]
                image, value = advance(force, kept, before, inverse)
                v2_ref[plane - 1, comp, here] = value
                store_z_modes(zs2, zd2, plane - 1, comp, here, value)
                if plane == 2:
                    odd = odd + before * image
                    even = even + value * image
        return odd, even

    mom3, mom4 = lax.fori_loop(0, CHUNKS, apply, (zero, zero), unroll=CHUNKS)

    def last(chunk, total):
        for plane, energy in enumerate(energies(zs2, zd2, (zs2_far, zd2_far, 0), joined, chunk)):
            total = total + modulus_rows(e_ref, 1 + plane, chunk) * energy
        return total

    mom5 = lax.fori_loop(0, CHUNKS, last, zero, unroll=CHUNKS)
    total = sofar_ref[...] + folded([zero] * 3 + [mom3, mom4, mom5] + [zero] * 2)
    for device in range(mom_ref.shape[0]):
        mom_ref[device] = total


def end_flag():
    at_end = lax.axis_index("space") == lax.axis_size("space") - 1
    return jnp.where(at_end, 1.0, 0.0).astype(F32)


def energies(zs, zd, last_plane, joined, chunk):
    low, here, high = [
        plane_modes(*where, chunk) for where in ((zs, zd, 0), (zs, zd, 1), last_plane)
    ]
    yield element_energy(element_modes(low, scaled_modes(here, joined)))
    yield element_energy(element_modes(here, high))


def energy_kernel(v0_ref, v1_left_ref, v1_ref, v2_ref, v2_far_ref, mom_ref, u_ref, out_ref, zs, zd, e_ref):
    total = mom_ref[0]
    for device in range(1, mom_ref.shape[0]):
        total = total + mom_ref[device]
    total = jnp.broadcast_to(jnp.sum(total, axis=1, keepdims=True), (8, 128))
    m0, m1, m2, m3, m4, m5 = [total[k : k + 1] for k in range(6)]
    low10 = m2 / m1
    low20 = m3 / m1
    piv1 = m3 - low10 * m2
    mix = m4 - low20 * m2
    good1 = piv1 > 1e-7 * m3
    safe1 = jnp.where(good1, piv1, 1.0)
    low21 = jnp.where(good1, mix / safe1, 0.0)
    piv2 = m5 - low20 * m3 - low21 * mix
    good2 = good1 & (piv2 > 1e-7 * m5)
    y1 = m1 - low10 * m0
    y2 = m2 - low20 * m0 - low21 * y1
    c2 = jnp.where(good2, y2 / jnp.where(good2, piv2, 1.0), 0.0)
    c1 = jnp.where(good1, y1 / safe1 - low21 * c2, 0.0)
    c0 = m0 / m1 - low10 * c1 - low20 * c2
    c0, c1, c2 = [jnp.broadcast_to(jnp.concatenate([c, c], axis=1), (ROWS, NZ)) for c in (c0, c1, c2)]

    clear_tails([zs, zd])
    for plane in range(2):
        e_ref[plane, 0:ROWS] = jnp.zeros((ROWS, NZ), F32)
        e_ref[plane, NY + ROWS : NY + 2 * ROWS] = jnp.zeros((ROWS, NZ), F32)
    v1_planes = [v1_left_ref.at[1], v1_ref.at[0], v1_ref.at[1]]
    v2_planes = [v2_ref.at[0], v2_ref.at[1], v2_far_ref]

    def combine(chunk, done):
        here = rows_at(chunk)
        for plane in range(3):
            for comp in range(3):
                value = c0 * v0_ref[plane, comp, here] + c1 * v1_planes[plane][comp, here]
                value = value + c2 * v2_planes[plane][comp, here]
                if plane > 0:
                    u_ref[comp, plane - 1, here] = value
                store_z_modes(zs, zd, plane, comp, here, value)
        return done

    lax.fori_loop(0, CHUNKS, combine, 0, unroll=CHUNKS)
    joined = has_left()

    def measure(chunk, done):
        for plane, energy in enumerate(energies(zs, zd, (zs, zd, 2), joined, chunk)):
            e_ref[plane, rows_at(chunk + 1)] = energy
        return done

    lax.fori_loop(0, CHUNKS, measure, 0, unroll=CHUNKS)
    span = ROWS + 2
    for block in range(CHUNKS):
        for plane in range(2):
            first = ROWS - 1 + block * ROWS
            out_ref[block, plane * span : (plane + 1) * span] = e_ref[plane, first : first + span]


def weigh(planes):
    near = RADIUS - 1.0
    edge = RADIUS - math.sqrt(2.0)
    beside = [from_below(p) + from_above(p) for p in planes]
    cross = []
    full = []
    for p, side in zip(planes, beside):
        up_down = p[0:ROWS] + p[2 : 2 + ROWS]
        mid, mid_side = p[1 : 1 + ROWS], side[1 : 1 + ROWS]
        cross.append(near * mid + edge * (mid_side + up_down))
        diagonal = side[0:ROWS] + side[2 : 2 + ROWS]
        full.append(RADIUS * mid + near * (mid_side + up_down) + edge * diagonal)
    return [full[k] + cross[k - 1] + cross[k + 1] for k in range(1, 1 + CX)]


def filter_kernel(energy_ref, next_ref, dens_ref, out_ref):
    space, load = lax.axis_index("space"), lax.axis_index("load")
    n_space, n_load = lax.axis_size("space"), lax.axis_size("load")
    span = ROWS + 2
    part = lambda ref, k: ref[k * span : (k + 1) * span]
    total = [part(ref, k) for ref in (energy_ref, next_ref) for k in range(2)]
    before = jnp.maximum(load - 1, 0)
    after = jnp.minimum(load + 1, n_load - 1)
    at_y = load * ROWS - 1 + row_ids((span, NZ))
    in_y = (at_y >= 0) & (at_y < n_load * ROWS)
    weighted, inside, own = [], [], []
    for plane in range(4):
        dens = jnp.concatenate(
            [
                dens_ref[before, 1 + plane][ROWS - 1 : ROWS],
                dens_ref[load, 1 + plane],
                dens_ref[after, 1 + plane][0:1],
            ],
            axis=0,
        )
        at_x = space * CX - 1 + plane
        scale = jnp.where((at_x >= 0) & (at_x < n_space * CX), 1.0, 0.0).astype(F32)
        present = scale * jnp.where(in_y, 1.0, 0.0)
        sensitivity = -PENALTY * (1.0 - EMIN) * (dens * dens) * total[plane]
        weighted.append(present * (dens * sensitivity))
        inside.append(present)
        if 1 <= plane <= CX:
            own.append(dens[1 : 1 + ROWS])
    sums, counts = weigh(weighted), weigh(inside)
    for plane in range(CX):
        out_ref[plane] = sums[plane] / (own[plane] * counts[plane])


def shifted(array, axis, distance):
    size = lax.axis_size(axis)
    return lax.ppermute(array, axis, [(i, (i + distance) % size) for i in range(size)])


def body(density, fixed_dofs, body_loads, point_nodes, point_forces):
    n_load, n_space = lax.axis_size("load"), lax.axis_size("space")
    dens_chip = swapped(density, False)
    dens_link = swapped(density, True)
    plane = (3, NY, NZ)
    by_component = jnp.swapaxes(point_forces, 0, 1)
    load, keep, to_chip, to_link = kernel_call(
        loads_kernel,
        [(2,) + plane, (2,) + plane, (3,) + plane, (3,) + plane],
        4,
        0,
        [
            pltpu.VMEM(body_loads.shape, F32),
            pltpu.VMEM(fixed_dofs.shape, jnp.int32),
            pltpu.VMEM(point_nodes.shape, jnp.int32),
            pltpu.VMEM(by_component.shape, F32),
            pltpu.SemaphoreType.DMA((4,)),
        ],
    )(*[pltpu.with_memory_space_constraint(x, pltpu.HBM) for x in (body_loads, fixed_dofs, point_nodes, by_component)])
    (dens,) = kernel_call(pack_kernel, [(n_load, 3 * CX, ROWS, NZ)], 0, 3)(
        dens_chip, density, dens_link
    )
    dens, to_chip, to_link = lax.optimization_barrier((dens, to_chip, to_link))
    chip = swapped(to_chip, False)
    link = swapped(to_link, True)
    dens = lax.all_to_all(dens, "load", 0, 0)

    padded = (NY + ROWS, NZ)
    modes = lambda planes: (planes, 3) + padded
    zed = lambda planes: pltpu.VMEM(modes(planes), F32)
    carried = lambda slots: pltpu.VMEM((slots, 3, ROWS, NZ), F32)
    v1, v0, modulus, inverse, zs0, zd0, mom = kernel_call(
        first_kernel,
        [(2,) + plane, (3,) + plane, (6,) + padded, (4, NY, NZ), modes(4), modes(4), (8, 128)],
        0,
        5,
        [carried(2)],
    )(load, keep, chip, link, dens)
    v1_left = shifted(v1, "space", 1)
    v2_far, zs1, zd1, zs2, zd2, force, mom = kernel_call(
        middle_kernel,
        [plane, modes(1), modes(1), modes(1), modes(1), plane, (8, 128)],
        0,
        9,
        [zed(1), zed(1), zed(2), zed(2), carried(3)],
    )(v1, zs0, zd0, modulus, inverse, chip, link, keep, mom)
    v2, mom = kernel_call(
        second_kernel,
        [(2,) + plane, (n_space, 8, 128)],
        0,
        13,
        [zed(2), zed(2), zed(2), zed(2), carried(2)],
    )(v1_left, v1, chip, link, keep, modulus, inverse, zs1, zd1, zs2, zd2, force, mom)
    mom = lax.all_to_all(mom, "space", 0, 0)
    span = ROWS + 2
    moved, energy = kernel_call(
        energy_kernel,
        [(3, CX, NY, NZ), (CHUNKS, 2 * span, NZ)],
        0,
        6,
        [zed(3), zed(3), pltpu.VMEM((2, NY + 2 * ROWS, NZ), F32)],
    )(v0, v1_left, v1, v2, v2_far, mom)
    energy = jnp.sum(lax.all_to_all(energy, "load", 0, 0), axis=0)
    following = shifted(energy, "space", -1)
    (filtered,) = kernel_call(filter_kernel, [(CX, ROWS, NZ)], 0, 3)(energy, following, dens)
    return (moved[None], filtered)


def solution(mesh):
    placed = (
        P("space", "load", None),
        P(None, "space", None, None),
        P("load", None, "space", None, None),
        P("load", None),
        P("load", None, None),
    )
    return jax.shard_map(
        body,
        mesh=mesh,
        in_specs=placed,
        out_specs=(P("load", None, "space", None, None), P("space", "load", None)),
        check_vma=False,
    )
```

```python
import math

import jax
import jax.numpy as jnp
from jax import lax
from jax.experimental import pallas as pl
from jax.experimental.pallas import tpu as pltpu
from jax.sharding import PartitionSpec as P

CX = 2
NY = 64
NZ = 256
ROWS = 8
CHUNKS = NY // ROWS
ZBITS = 8
EMIN = 0.001
PENALTY = 3.0
RADIUS = 1.5
POISSON = 0.3
LAME = POISSON / ((1.0 + POISSON) * (1.0 - 2.0 * POISSON))
SHEAR = 1.0 / (2.0 * (1.0 + POISSON))
KDIAG = (LAME + 4.0 * SHEAR) / 9.0
F32 = jnp.float32
VMEM_LIMIT = 16 * 1024 * 1024
PAIRS = ("ss", "sd", "ds", "dd")


def kernel_call(fn, outs, n_hbm, n_in, scratch=()):
    vmem = pl.BlockSpec(memory_space=pltpu.VMEM)
    hbm = pl.BlockSpec(memory_space=pltpu.HBM)
    return pl.pallas_call(
        fn,
        out_shape=[jax.ShapeDtypeStruct(shape, F32) for shape in outs],
        in_specs=[hbm] * n_hbm + [vmem] * n_in,
        out_specs=[vmem] * len(outs),
        scratch_shapes=list(scratch),
        compiler_params=pltpu.CompilerParams(vmem_limit_bytes=VMEM_LIMIT),
    )


def lane_ids(shape):
    return lax.broadcasted_iota(jnp.int32, shape, 1)


def row_ids(shape):
    return lax.broadcasted_iota(jnp.int32, shape, 0)


def from_above(field):
    return jnp.where(lane_ids(field.shape) == NZ - 1, 0.0, pltpu.roll(field, NZ - 1, 1))


def from_below(field):
    return jnp.where(lane_ids(field.shape) == 0, 0.0, pltpu.roll(field, 1, 1))


def rows_at(chunk):
    return pl.ds(pl.multiple_of(chunk * ROWS, ROWS), ROWS)


def store_z_modes(zs_ref, zd_ref, plane, comp, rows, field):
    up = from_above(field)
    zs_ref[plane, comp, rows] = field + up
    zd_ref[plane, comp, rows] = up - field


def y_modes(cur, nxt):
    first = row_ids(cur.shape) == 0
    up = pltpu.roll(jnp.where(first, nxt, cur), ROWS - 1, 0)
    return cur + up, up - cur


def plane_modes(zs_ref, zd_ref, plane, chunk):
    out = []
    for comp in range(3):
        here, after = rows_at(chunk), rows_at(chunk + 1)
        ss, ds = y_modes(zs_ref[plane, comp, here], zs_ref[plane, comp, after])
        sd, dd = y_modes(zd_ref[plane, comp, here], zd_ref[plane, comp, after])
        out.append({"ss": ss, "sd": sd, "ds": ds, "dd": dd})
    return out


def element_modes(low, high):
    modes = []
    for comp in range(3):
        field = {}
        for pair in PAIRS:
            field["d" + pair] = high[comp][pair] - low[comp][pair]
            if pair != "ss":
                field["s" + pair] = high[comp][pair] + low[comp][pair]
        modes.append(field)
    return modes


NORMAL = ((0, "dss"), (1, "sds"), (2, "ssd"))
SHEARS = (((0, "sds"), (1, "dss")), ((0, "ssd"), (2, "dss")), ((1, "ssd"), (2, "sds")))
BENDS = (((0, "dsd"), (1, "sdd")), ((0, "dds"), (2, "sdd")), ((1, "dds"), (2, "dsd")))
TWISTS = ((0, "sdd"), (1, "dsd"), (2, "dds"))


def element_response(modes, modulus):
    k_lame = modulus * (LAME / 16.0)
    k_two = modulus * (SHEAR / 8.0)
    k_shear = modulus * (SHEAR / 16.0)
    k_bend = modulus * (LAME / 48.0)
    k_twist = modulus * (SHEAR / 48.0)
    k_last = modulus * ((LAME + 4.0 * SHEAR) / 144.0)
    force = [{}, {}, {}]
    get = lambda key: modes[key[0]][key[1]]
    trace = k_lame * (get(NORMAL[0]) + get(NORMAL[1]) + get(NORMAL[2]))
    for comp, name in NORMAL:
        force[comp][name] = k_two * modes[comp][name] + trace
    for one, two in SHEARS:
        both = k_shear * (get(one) + get(two))
        force[one[0]][one[1]] = both
        force[two[0]][two[1]] = both
    for one, two in BENDS:
        both = k_bend * (get(one) + get(two))
        force[one[0]][one[1]] = k_shear * get(one) + both
        force[two[0]][two[1]] = k_shear * get(two) + both
    total = get(TWISTS[0]) + get(TWISTS[1]) + get(TWISTS[2])
    for comp, name in TWISTS:
        force[comp][name] = k_twist * (modes[comp][name] + total)
    for comp in range(3):
        force[comp]["ddd"] = k_last * modes[comp]["ddd"]
    return force


def element_energy(modes):
    get = lambda key: modes[key[0]][key[1]]
    square = lambda value: value * value
    normal = [get(key) for key in NORMAL]
    twist = [get(key) for key in TWISTS]
    energy = (LAME / 16.0) * square(normal[0] + normal[1] + normal[2])
    energy += (SHEAR / 8.0) * (square(normal[0]) + square(normal[1]) + square(normal[2]))
    shear = sum(square(get(one) + get(two)) for one, two in SHEARS)
    shear += sum(square(get(one)) + square(get(two)) for one, two in BENDS)
    energy += (SHEAR / 16.0) * shear
    energy += (LAME / 48.0) * sum(square(get(one) + get(two)) for one, two in BENDS)
    twisted = square(twist[0]) + square(twist[1]) + square(twist[2])
    energy += (SHEAR / 48.0) * (twisted + square(twist[0] + twist[1] + twist[2]))
    last = square(modes[0]["ddd"]) + square(modes[1]["ddd"]) + square(modes[2]["ddd"])
    return energy + ((LAME + 4.0 * SHEAR) / 144.0) * last


def split_x(force):
    low, high = [], []
    for comp in range(3):
        lo, hi = {}, {}
        for pair in PAIRS:
            diff = force[comp]["d" + pair]
            if pair == "ss":
                lo[pair], hi[pair] = -diff, diff
            else:
                mean = force[comp]["s" + pair]
                lo[pair], hi[pair] = mean - diff, mean + diff
        low.append(lo)
        high.append(hi)
    return low, high


def node_force(acc, prev):
    sides = []
    for y_mode in ("s", "d"):
        mean, diff = acc[y_mode + "s"], acc[y_mode + "d"]
        sides.append((mean - diff) + from_below(mean + diff))
    low, high = sides[0] - sides[1], sides[0] + sides[1]
    last = row_ids(low.shape) == ROWS - 1
    return low + pltpu.roll(jnp.where(last, prev, high), 1, 0), high


def apply_rows(planes, moduli, carry_ref, chunk, first_edge=False, last_scale=None):
    slot = 0

    def finish(acc):
        nonlocal slot
        forces = []
        for comp in range(3):
            force, carry = node_force(acc[comp], carry_ref[slot, comp])
            carry_ref[slot, comp] = carry
            forces.append(force)
        slot += 1
        return forces

    low = plane_modes(*planes[0], chunk)
    partial = None
    for index, modulus in enumerate(moduli):
        high = plane_modes(*planes[index + 1], chunk)
        if last_scale is not None and index + 1 == len(moduli):
            high = scaled_modes(high, last_scale)
        to_low, to_high = split_x(element_response(element_modes(low, high), modulus))
        if partial is not None:
            acc = [{p: partial[c][p] + to_low[c][p] for p in PAIRS} for c in range(3)]
            yield index, finish(acc)
        elif first_edge:
            yield index, finish(to_low)
        partial, low = to_high, high
    if last_scale is not None:
        yield len(moduli), [force * last_scale for force in finish(partial)]


def scaled_modes(modes, scale):
    return [{pair: field[pair] * scale for pair in PAIRS} for field in modes]


def has_left():
    return jnp.where(lax.axis_index("space") == 0, 0.0, 1.0).astype(F32)


def loads_kernel(
    body_hbm, fixed_hbm, node_hbm, force_hbm, load_ref, keep_ref, chip_ref, link_ref,
    body_ref, fixed_ref, node_ref, force_ref, sems,
):
    pairs = ((node_hbm, node_ref), (force_hbm, force_ref), (body_hbm, body_ref), (fixed_hbm, fixed_ref))
    copies = [pltpu.make_async_copy(src, dst, sems.at[k]) for k, (src, dst) in enumerate(pairs)]
    for copy in copies:
        copy.start()
    copies[0].wait()
    copies[1].wait()
    cells = CX * NY * NZ
    local = node_ref[...] - lax.axis_index("space") * cells
    valid = (local >= 0) & (local < cells)
    local = jnp.where(valid, local, -1)
    line = lax.shift_right_arithmetic(local, ZBITS)
    depth = lax.bitwise_and(local, NZ - 1)
    points = local.shape[1]
    on_line = row_ids((CX * NY, points)) == line
    lines = [jnp.where(on_line, force_ref[comp], 0.0) for comp in range(3)]
    at_depth = jnp.where(row_ids((NZ, points)) == depth, 1.0, 0.0)
    added = lax.dot_general(
        jnp.concatenate(lines, axis=0),
        at_depth,
        (((1,), (1,)), ((), ())),
        precision=lax.Precision.HIGHEST,
        preferred_element_type=F32,
    )
    copies[2].wait()
    copies[3].wait()
    on_even = is_even()
    for comp in range(3):
        loads, keeps = [], []
        for plane in range(CX):
            keep = 1.0 - fixed_ref[comp, plane].astype(F32)
            first = (comp * CX + plane) * NY
            loads.append(keep * (body_ref[0, comp, plane] + added[first : first + NY]))
            keeps.append(keep)
            load_ref[plane, comp] = loads[plane]
            keep_ref[plane, comp] = keep
        to_left, to_right = (loads[1], loads[0], keeps[0]), (loads[1], keeps[1], keeps[1])
        for part in range(3):
            chip_ref[part, comp] = jnp.where(on_even, to_right[part], to_left[part])
            link_ref[part, comp] = jnp.where(on_even, to_left[part], to_right[part])


def is_even():
    return lax.rem(lax.axis_index("space"), 2) == 0


def swapped(array, across):
    size = lax.axis_size("space")
    partner = lambda i: (i + (1 if (i % 2 == 0) != across else -1)) % size
    return lax.ppermute(array, "space", [(i, partner(i)) for i in range(size)])


def pack_kernel(chip_ref, own_ref, link_ref, pack_ref):
    on_even = is_even()
    for plane in range(CX):
        before = jnp.where(on_even, link_ref[plane], chip_ref[plane])
        after = jnp.where(on_even, chip_ref[plane], link_ref[plane])
        for block in range(pack_ref.shape[0]):
            pack_ref[block, plane] = before
            pack_ref[block, CX + plane] = own_ref[plane]
            pack_ref[block, 2 * CX + plane] = after


def clear_tails(refs):
    for ref in refs:
        for plane in range(ref.shape[0]):
            for comp in range(3):
                ref[plane, comp, NY : NY + ROWS] = jnp.zeros((ROWS, NZ), F32)


def clear_carry(ref):
    for plane in range(ref.shape[0]):
        for comp in range(3):
            ref[plane, comp] = jnp.zeros((ROWS, NZ), F32)


def folded(values):
    rows = [jnp.sum(v[:, :128] + v[:, 128:], axis=0, keepdims=True) for v in values]
    return jnp.concatenate(rows, axis=0)


def advance(forces, kept, before, inverse):
    image = jnp.where(kept, forces, before)
    return image, jnp.where(kept, forces * inverse, before)


def modulus_rows(e_ref, plane, chunk):
    return e_ref[plane, rows_at(chunk + 1)]


def inverse_diagonal(e_ref, plane, chunk, scale=1.0):
    last = row_ids((ROWS, NZ)) == ROWS - 1
    cur = scale * modulus_rows(e_ref, plane, chunk) + modulus_rows(e_ref, plane + 1, chunk)
    before = scale * modulus_rows(e_ref, plane, chunk - 1) + modulus_rows(e_ref, plane + 1, chunk - 1)
    cur = cur + pltpu.roll(jnp.where(last, before, cur), 1, 0)
    diag = KDIAG * (cur + from_below(cur))
    return 1.0 / jnp.where(diag > 0.0, diag, 1.0)


def first_kernel(
    load_ref, keep_ref, chip_ref, link_ref, dens_ref,
    v1_ref, v0_ref, e_ref, inv_ref, zs, zd, mom_ref,
    carry,
):
    first_x = lax.axis_index("space") * CX
    limit = lax.axis_size("space") * CX
    for plane in range(6):
        at = first_x - 2 + plane
        scale = jnp.where(at < limit, 1.0, 0.0).astype(F32)
        e_ref[plane, 0:ROWS] = jnp.zeros((ROWS, NZ), F32)
        for block in range(CHUNKS):
            dens = dens_ref[block, plane]
            rows = slice((block + 1) * ROWS, (block + 2) * ROWS)
            e_ref[plane, rows] = scale * (EMIN + (1.0 - EMIN) * (dens * dens * dens))
    clear_tails([zs, zd])
    clear_carry(carry)
    on_even = is_even()
    has_right, joined = 1.0 - end_flag(), has_left()
    zero = jnp.zeros((ROWS, NZ), F32)

    def start(chunk, total):
        here = rows_at(chunk)
        for plane in range(4):
            inverse = inverse_diagonal(e_ref, plane, chunk, joined if plane == 1 else 1.0)
            inv_ref[plane, here] = inverse
            for comp in range(3):
                if plane == 0:
                    load = jnp.where(on_even, link_ref[0, comp, here], chip_ref[0, comp, here])
                elif plane == 3:
                    load = has_right * jnp.where(on_even, chip_ref[1, comp, here], link_ref[1, comp, here])
                else:
                    load = load_ref[plane - 1, comp, here]
                value = load * inverse
                if plane < 3:
                    v0_ref[plane, comp, here] = value
                if plane in (1, 2):
                    total = total + load * value
                store_z_modes(zs, zd, plane, comp, here, value)
        return total

    mom0 = lax.fori_loop(0, CHUNKS, start, zero, unroll=CHUNKS // 2)

    def apply(chunk, totals):
        here = rows_at(chunk)
        odd, even = totals
        moduli = [modulus_rows(e_ref, plane, chunk) for plane in (1, 2, 3)]
        moduli[0] = moduli[0] * joined
        for plane, forces in apply_rows([(zs, zd, k) for k in range(4)], moduli, carry, chunk):
            inverse = inv_ref[plane, here]
            for comp in range(3):
                kept = keep_ref[plane - 1, comp, here] > 0.0
                before = v0_ref[plane, comp, here]
                image, value = advance(forces[comp], kept, before, inverse)
                v1_ref[plane - 1, comp, here] = value
                odd = odd + before * image
                even = even + value * image
        return odd, even

    mom1, mom2 = lax.fori_loop(0, CHUNKS, apply, (zero, zero), unroll=CHUNKS)
    mom_ref[...] = folded([mom0, mom1, mom2] + [zero] * 5)


def middle_kernel(
    v1_ref, zs0, zd0, e_ref, inv_ref, chip_ref, link_ref, keep_ref, sofar_ref,
    v2_ref, zs1, zd1, zs2, zd2, force_ref, mom_ref,
    zs, zd, zs_far, zd_far, carry,
):
    clear_tails([zs, zd, zs1, zd1, zs2, zd2, zs_far, zd_far])
    clear_carry(carry)
    has_right, on_even = 1.0 - end_flag(), is_even()
    zero = jnp.zeros((ROWS, NZ), F32)

    def right(part, comp, here):
        return has_right * jnp.where(on_even, chip_ref[part, comp, here], link_ref[part, comp, here])

    def start(chunk, done):
        here = rows_at(chunk)
        inverse = inverse_diagonal(e_ref, 4, chunk)
        for comp in range(3):
            store_z_modes(zs, zd, 0, comp, here, right(0, comp, here) * inverse)
            store_z_modes(zs1, zd1, 0, comp, here, v1_ref[0, comp, here])
            store_z_modes(zs_far, zd_far, 0, comp, here, v1_ref[1, comp, here])
        return done

    lax.fori_loop(0, CHUNKS, start, 0, unroll=CHUNKS)

    def outer(chunk, done):
        here = rows_at(chunk)
        moduli = [modulus_rows(e_ref, plane, chunk) for plane in (3, 4)]
        planes = [(zs0, zd0, 2), (zs0, zd0, 3), (zs, zd, 0)]
        for _, forces in apply_rows(planes, moduli, carry.at[0:1], chunk):
            inverse = inv_ref[3, here]
            for comp in range(3):
                kept = right(2, comp, here) > 0.0
                before = right(1, comp, here) * inverse
                _, value = advance(forces[comp], kept, before, inverse)
                store_z_modes(zs_far, zd_far, 1, comp, here, value)
        return done

    lax.fori_loop(0, CHUNKS, outer, 0, unroll=CHUNKS)

    def apply(chunk, totals):
        here = rows_at(chunk)
        odd, even = totals
        moduli = [modulus_rows(e_ref, plane, chunk) for plane in (2, 3)]
        planes = [(zs1, zd1, 0), (zs_far, zd_far, 0), (zs_far, zd_far, 1)]
        for plane, forces in apply_rows(planes, moduli, carry.at[1:3], chunk, first_edge=True):
            if plane == 0:
                for comp in range(3):
                    force_ref[comp, here] = forces[comp]
                continue
            inverse = inv_ref[2, here]
            for comp in range(3):
                kept = keep_ref[1, comp, here] > 0.0
                before = v1_ref[1, comp, here]
                image, value = advance(forces[comp], kept, before, inverse)
                v2_ref[comp, here] = value
                store_z_modes(zs2, zd2, 0, comp, here, value)
                odd = odd + before * image
                even = even + value * image
        return odd, even

    mom3, mom4 = lax.fori_loop(0, CHUNKS, apply, (zero, zero), unroll=CHUNKS)
    mom_ref[...] = sofar_ref[...] + folded([zero] * 3 + [mom3, mom4] + [zero] * 3)


def second_kernel(
    v1_left_ref, v1_ref, chip_ref, link_ref, keep_ref, e_ref, inv_ref,
    zs1, zd1, zs2_far, zd2_far, force_ref, sofar_ref,
    v2_ref, mom_ref,
    zs, zd, zs2, zd2, carry,
):
    on_even, joined = is_even(), has_left()
    clear_tails([zs, zd, zs2, zd2])
    clear_carry(carry)
    zero = jnp.zeros((ROWS, NZ), F32)

    def start(chunk, done):
        here = rows_at(chunk)
        for plane in range(2):
            for comp in range(3):
                store_z_modes(zs, zd, plane, comp, here, v1_left_ref[plane, comp, here])
        return done

    lax.fori_loop(0, CHUNKS, start, 0, unroll=CHUNKS)

    def apply(chunk, totals):
        here = rows_at(chunk)
        odd, even = totals
        moduli = [modulus_rows(e_ref, plane, chunk) for plane in (0, 1)]
        planes = [(zs, zd, 0), (zs, zd, 1), (zs1, zd1, 0)]
        for plane, forces in apply_rows(planes, moduli, carry, chunk, last_scale=joined):
            inverse = inv_ref[plane - 1, here]
            for comp in range(3):
                if plane == 1:
                    keep = jnp.where(on_even, link_ref[1, comp, here], chip_ref[1, comp, here])
                    kept, before = keep > 0.0, v1_left_ref[1, comp, here]
                    force = forces[comp]
                else:
                    kept, before = keep_ref[0, comp, here] > 0.0, v1_ref[0, comp, here]
                    force = forces[comp] + force_ref[comp, here]
                image, value = advance(force, kept, before, inverse)
                v2_ref[plane - 1, comp, here] = value
                store_z_modes(zs2, zd2, plane - 1, comp, here, value)
                if plane == 2:
                    odd = odd + before * image
                    even = even + value * image
        return odd, even

    mom3, mom4 = lax.fori_loop(0, CHUNKS, apply, (zero, zero), unroll=CHUNKS)

    def last(chunk, total):
        for plane, energy in enumerate(energies(zs2, zd2, (zs2_far, zd2_far, 0), joined, chunk)):
            total = total + modulus_rows(e_ref, 1 + plane, chunk) * energy
        return total

    mom5 = lax.fori_loop(0, CHUNKS, last, zero, unroll=CHUNKS)
    total = sofar_ref[...] + folded([zero] * 3 + [mom3, mom4, mom5] + [zero] * 2)
    for device in range(mom_ref.shape[0]):
        mom_ref[device] = total


def end_flag():
    at_end = lax.axis_index("space") == lax.axis_size("space") - 1
    return jnp.where(at_end, 1.0, 0.0).astype(F32)


def energies(zs, zd, last_plane, joined, chunk):
    low, here, high = [
        plane_modes(*where, chunk) for where in ((zs, zd, 0), (zs, zd, 1), last_plane)
    ]
    yield element_energy(element_modes(low, scaled_modes(here, joined)))
    yield element_energy(element_modes(here, high))


def energy_kernel(v0_ref, v1_left_ref, v1_ref, v2_ref, v2_far_ref, mom_ref, u_ref, out_ref, zs, zd, e_ref):
    total = mom_ref[0]
    for device in range(1, mom_ref.shape[0]):
        total = total + mom_ref[device]
    total = jnp.broadcast_to(jnp.sum(total, axis=1, keepdims=True), (8, 128))
    m0, m1, m2, m3, m4, m5 = [total[k : k + 1] for k in range(6)]
    low10 = m2 / m1
    low20 = m3 / m1
    piv1 = m3 - low10 * m2
    mix = m4 - low20 * m2
    good1 = piv1 > 1e-7 * m3
    safe1 = jnp.where(good1, piv1, 1.0)
    low21 = jnp.where(good1, mix / safe1, 0.0)
    piv2 = m5 - low20 * m3 - low21 * mix
    good2 = good1 & (piv2 > 1e-7 * m5)
    y1 = m1 - low10 * m0
    y2 = m2 - low20 * m0 - low21 * y1
    c2 = jnp.where(good2, y2 / jnp.where(good2, piv2, 1.0), 0.0)
    c1 = jnp.where(good1, y1 / safe1 - low21 * c2, 0.0)
    c0 = m0 / m1 - low10 * c1 - low20 * c2
    c0, c1, c2 = [jnp.broadcast_to(jnp.concatenate([c, c], axis=1), (ROWS, NZ)) for c in (c0, c1, c2)]

    clear_tails([zs, zd])
    for plane in range(2):
        e_ref[plane, 0:ROWS] = jnp.zeros((ROWS, NZ), F32)
        e_ref[plane, NY + ROWS : NY + 2 * ROWS] = jnp.zeros((ROWS, NZ), F32)
    v1_planes = [v1_left_ref.at[1], v1_ref.at[0], v1_ref.at[1]]
    v2_planes = [v2_ref.at[0], v2_ref.at[1], v2_far_ref]

    def combine(chunk, done):
        here = rows_at(chunk)
        for plane in range(3):
            for comp in range(3):
                value = c0 * v0_ref[plane, comp, here] + c1 * v1_planes[plane][comp, here]
                value = value + c2 * v2_planes[plane][comp, here]
                if plane > 0:
                    u_ref[comp, plane - 1, here] = value
                store_z_modes(zs, zd, plane, comp, here, value)
        return done

    lax.fori_loop(0, CHUNKS, combine, 0, unroll=CHUNKS)
    joined = has_left()

    def measure(chunk, done):
        for plane, energy in enumerate(energies(zs, zd, (zs, zd, 2), joined, chunk)):
            e_ref[plane, rows_at(chunk + 1)] = energy
        return done

    lax.fori_loop(0, CHUNKS, measure, 0, unroll=CHUNKS)
    span = ROWS + 2
    for block in range(CHUNKS):
        for plane in range(2):
            first = ROWS - 1 + block * ROWS
            out_ref[block, plane * span : (plane + 1) * span] = e_ref[plane, first : first + span]


def weigh(planes):
    near = RADIUS - 1.0
    edge = RADIUS - math.sqrt(2.0)
    beside = [from_below(p) + from_above(p) for p in planes]
    cross = []
    full = []
    for p, side in zip(planes, beside):
        up_down = p[0:ROWS] + p[2 : 2 + ROWS]
        mid, mid_side = p[1 : 1 + ROWS], side[1 : 1 + ROWS]
        cross.append(near * mid + edge * (mid_side + up_down))
        diagonal = side[0:ROWS] + side[2 : 2 + ROWS]
        full.append(RADIUS * mid + near * (mid_side + up_down) + edge * diagonal)
    return [full[k] + cross[k - 1] + cross[k + 1] for k in range(1, 1 + CX)]


def filter_kernel(energy_ref, next_ref, dens_ref, out_ref):
    space, load = lax.axis_index("space"), lax.axis_index("load")
    n_space, n_load = lax.axis_size("space"), lax.axis_size("load")
    span = ROWS + 2
    part = lambda ref, k: ref[k * span : (k + 1) * span]
    total = [part(ref, k) for ref in (energy_ref, next_ref) for k in range(2)]
    before = jnp.maximum(load - 1, 0)
    after = jnp.minimum(load + 1, n_load - 1)
    at_y = load * ROWS - 1 + row_ids((span, NZ))
    in_y = (at_y >= 0) & (at_y < n_load * ROWS)
    weighted, inside, own = [], [], []
    for plane in range(4):
        dens = jnp.concatenate(
            [
                dens_ref[before, 1 + plane][ROWS - 1 : ROWS],
                dens_ref[load, 1 + plane],
                dens_ref[after, 1 + plane][0:1],
            ],
            axis=0,
        )
        at_x = space * CX - 1 + plane
        scale = jnp.where((at_x >= 0) & (at_x < n_space * CX), 1.0, 0.0).astype(F32)
        present = scale * jnp.where(in_y, 1.0, 0.0)
        sensitivity = -PENALTY * (1.0 - EMIN) * (dens * dens) * total[plane]
        weighted.append(present * (dens * sensitivity))
        inside.append(present)
        if 1 <= plane <= CX:
            own.append(dens[1 : 1 + ROWS])
    sums, counts = weigh(weighted), weigh(inside)
    for plane in range(CX):
        out_ref[plane] = sums[plane] / (own[plane] * counts[plane])


def shifted(array, axis, distance):
    size = lax.axis_size(axis)
    return lax.ppermute(array, axis, [(i, (i + distance) % size) for i in range(size)])


def body(density, fixed_dofs, body_loads, point_nodes, point_forces):
    n_load, n_space = lax.axis_size("load"), lax.axis_size("space")
    dens_chip = swapped(density, False)
    dens_link = swapped(density, True)
    plane = (3, NY, NZ)
    by_component = jnp.swapaxes(point_forces, 0, 1)
    load, keep, to_chip, to_link = kernel_call(
        loads_kernel,
        [(2,) + plane, (2,) + plane, (3,) + plane, (3,) + plane],
        4,
        0,
        [
            pltpu.VMEM(body_loads.shape, F32),
            pltpu.VMEM(fixed_dofs.shape, jnp.int32),
            pltpu.VMEM(point_nodes.shape, jnp.int32),
            pltpu.VMEM(by_component.shape, F32),
            pltpu.SemaphoreType.DMA((4,)),
        ],
    )(*[pltpu.with_memory_space_constraint(x, pltpu.HBM) for x in (body_loads, fixed_dofs, point_nodes, by_component)])
    (dens,) = kernel_call(pack_kernel, [(n_load, 3 * CX, ROWS, NZ)], 0, 3)(
        dens_chip, density, dens_link
    )
    dens, to_chip = lax.optimization_barrier((dens, to_chip))
    chip = swapped(to_chip, False)
    link = swapped(to_link, True)
    dens = lax.all_to_all(dens, "load", 0, 0)

    padded = (NY + ROWS, NZ)
    modes = lambda planes: (planes, 3) + padded
    zed = lambda planes: pltpu.VMEM(modes(planes), F32)
    carried = lambda slots: pltpu.VMEM((slots, 3, ROWS, NZ), F32)
    v1, v0, modulus, inverse, zs0, zd0, mom = kernel_call(
        first_kernel,
        [(2,) + plane, (3,) + plane, (6,) + padded, (4, NY, NZ), modes(4), modes(4), (8, 128)],
        0,
        5,
        [carried(2)],
    )(load, keep, chip, link, dens)
    v1_left = shifted(v1, "space", 1)
    v2_far, zs1, zd1, zs2, zd2, force, mom = kernel_call(
        middle_kernel,
        [plane, modes(1), modes(1), modes(1), modes(1), plane, (8, 128)],
        0,
        9,
        [zed(1), zed(1), zed(2), zed(2), carried(3)],
    )(v1, zs0, zd0, modulus, inverse, chip, link, keep, mom)
    v2, mom = kernel_call(
        second_kernel,
        [(2,) + plane, (n_space, 8, 128)],
        0,
        13,
        [zed(2), zed(2), zed(2), zed(2), carried(2)],
    )(v1_left, v1, chip, link, keep, modulus, inverse, zs1, zd1, zs2, zd2, force, mom)
    mom = lax.all_to_all(mom, "space", 0, 0)
    span = ROWS + 2
    moved, energy = kernel_call(
        energy_kernel,
        [(3, CX, NY, NZ), (CHUNKS, 2 * span, NZ)],
        0,
        6,
        [zed(3), zed(3), pltpu.VMEM((2, NY + 2 * ROWS, NZ), F32)],
    )(v0, v1_left, v1, v2, v2_far, mom)
    energy = jnp.sum(lax.all_to_all(energy, "load", 0, 0), axis=0)
    following = shifted(energy, "space", -1)
    (filtered,) = kernel_call(filter_kernel, [(CX, ROWS, NZ)], 0, 3)(energy, following, dens)
    return (moved[None], filtered)


def solution(mesh):
    placed = (
        P("space", "load", None),
        P(None, "space", None, None),
        P("load", None, "space", None, None),
        P("load", None),
        P("load", None, None),
    )
    return jax.shard_map(
        body,
        mesh=mesh,
        in_specs=placed,
        out_specs=(P("load", None, "space", None, None), P("space", "load", None)),
        check_vma=False,
    )
```

```python
import math

import jax
import jax.numpy as jnp
from jax import lax
from jax.experimental import pallas as pl
from jax.experimental.pallas import tpu as pltpu
from jax.sharding import PartitionSpec as P

CX = 2
NY = 64
NZ = 256
ROWS = 8
CHUNKS = NY // ROWS
ZBITS = 8
EMIN = 0.001
PENALTY = 3.0
RADIUS = 1.5
POISSON = 0.3
LAME = POISSON / ((1.0 + POISSON) * (1.0 - 2.0 * POISSON))
SHEAR = 1.0 / (2.0 * (1.0 + POISSON))
KDIAG = (LAME + 4.0 * SHEAR) / 9.0
F32 = jnp.float32
VMEM_LIMIT = 16 * 1024 * 1024
PAIRS = ("ss", "sd", "ds", "dd")


def kernel_call(fn, outs, n_hbm, n_in, scratch=()):
    vmem = pl.BlockSpec(memory_space=pltpu.VMEM)
    hbm = pl.BlockSpec(memory_space=pltpu.HBM)
    return pl.pallas_call(
        fn,
        out_shape=[jax.ShapeDtypeStruct(shape, F32) for shape in outs],
        in_specs=[hbm] * n_hbm + [vmem] * n_in,
        out_specs=[vmem] * len(outs),
        scratch_shapes=list(scratch),
        compiler_params=pltpu.CompilerParams(vmem_limit_bytes=VMEM_LIMIT),
    )


def lane_ids(shape):
    return lax.broadcasted_iota(jnp.int32, shape, 1)


def row_ids(shape):
    return lax.broadcasted_iota(jnp.int32, shape, 0)


def from_above(field):
    return jnp.where(lane_ids(field.shape) == NZ - 1, 0.0, pltpu.roll(field, NZ - 1, 1))


def from_below(field):
    return jnp.where(lane_ids(field.shape) == 0, 0.0, pltpu.roll(field, 1, 1))


def rows_at(chunk):
    return pl.ds(pl.multiple_of(chunk * ROWS, ROWS), ROWS)


def store_z_modes(zs_ref, zd_ref, plane, comp, rows, field):
    up = from_above(field)
    zs_ref[plane, comp, rows] = field + up
    zd_ref[plane, comp, rows] = up - field


def y_modes(cur, nxt):
    first = row_ids(cur.shape) == 0
    up = pltpu.roll(jnp.where(first, nxt, cur), ROWS - 1, 0)
    return cur + up, up - cur


def plane_modes(zs_ref, zd_ref, plane, chunk):
    out = []
    for comp in range(3):
        here, after = rows_at(chunk), rows_at(chunk + 1)
        ss, ds = y_modes(zs_ref[plane, comp, here], zs_ref[plane, comp, after])
        sd, dd = y_modes(zd_ref[plane, comp, here], zd_ref[plane, comp, after])
        out.append({"ss": ss, "sd": sd, "ds": ds, "dd": dd})
    return out


def element_modes(low, high):
    modes = []
    for comp in range(3):
        field = {}
        for pair in PAIRS:
            field["d" + pair] = high[comp][pair] - low[comp][pair]
            if pair != "ss":
                field["s" + pair] = high[comp][pair] + low[comp][pair]
        modes.append(field)
    return modes


NORMAL = ((0, "dss"), (1, "sds"), (2, "ssd"))
SHEARS = (((0, "sds"), (1, "dss")), ((0, "ssd"), (2, "dss")), ((1, "ssd"), (2, "sds")))
BENDS = (((0, "dsd"), (1, "sdd")), ((0, "dds"), (2, "sdd")), ((1, "dds"), (2, "dsd")))
TWISTS = ((0, "sdd"), (1, "dsd"), (2, "dds"))


def element_response(modes, modulus):
    k_lame = modulus * (LAME / 16.0)
    k_two = modulus * (SHEAR / 8.0)
    k_shear = modulus * (SHEAR / 16.0)
    k_bend = modulus * (LAME / 48.0)
    k_twist = modulus * (SHEAR / 48.0)
    k_last = modulus * ((LAME + 4.0 * SHEAR) / 144.0)
    force = [{}, {}, {}]
    get = lambda key: modes[key[0]][key[1]]
    trace = k_lame * (get(NORMAL[0]) + get(NORMAL[1]) + get(NORMAL[2]))
    for comp, name in NORMAL:
        force[comp][name] = k_two * modes[comp][name] + trace
    for one, two in SHEARS:
        both = k_shear * (get(one) + get(two))
        force[one[0]][one[1]] = both
        force[two[0]][two[1]] = both
    for one, two in BENDS:
        both = k_bend * (get(one) + get(two))
        force[one[0]][one[1]] = k_shear * get(one) + both
        force[two[0]][two[1]] = k_shear * get(two) + both
    total = get(TWISTS[0]) + get(TWISTS[1]) + get(TWISTS[2])
    for comp, name in TWISTS:
        force[comp][name] = k_twist * (modes[comp][name] + total)
    for comp in range(3):
        force[comp]["ddd"] = k_last * modes[comp]["ddd"]
    return force


def element_energy(modes):
    get = lambda key: modes[key[0]][key[1]]
    square = lambda value: value * value
    normal = [get(key) for key in NORMAL]
    twist = [get(key) for key in TWISTS]
    energy = (LAME / 16.0) * square(normal[0] + normal[1] + normal[2])
    energy += (SHEAR / 8.0) * (square(normal[0]) + square(normal[1]) + square(normal[2]))
    shear = sum(square(get(one) + get(two)) for one, two in SHEARS)
    shear += sum(square(get(one)) + square(get(two)) for one, two in BENDS)
    energy += (SHEAR / 16.0) * shear
    energy += (LAME / 48.0) * sum(square(get(one) + get(two)) for one, two in BENDS)
    twisted = square(twist[0]) + square(twist[1]) + square(twist[2])
    energy += (SHEAR / 48.0) * (twisted + square(twist[0] + twist[1] + twist[2]))
    last = square(modes[0]["ddd"]) + square(modes[1]["ddd"]) + square(modes[2]["ddd"])
    return energy + ((LAME + 4.0 * SHEAR) / 144.0) * last


def split_x(force):
    low, high = [], []
    for comp in range(3):
        lo, hi = {}, {}
        for pair in PAIRS:
            diff = force[comp]["d" + pair]
            if pair == "ss":
                lo[pair], hi[pair] = -diff, diff
            else:
                mean = force[comp]["s" + pair]
                lo[pair], hi[pair] = mean - diff, mean + diff
        low.append(lo)
        high.append(hi)
    return low, high


def node_force(acc, prev):
    sides = []
    for y_mode in ("s", "d"):
        mean, diff = acc[y_mode + "s"], acc[y_mode + "d"]
        sides.append((mean - diff) + from_below(mean + diff))
    low, high = sides[0] - sides[1], sides[0] + sides[1]
    last = row_ids(low.shape) == ROWS - 1
    return low + pltpu.roll(jnp.where(last, prev, high), 1, 0), high


def apply_rows(planes, moduli, carry_ref, chunk, first_edge=False, last_scale=None):
    slot = 0

    def finish(acc):
        nonlocal slot
        forces = []
        for comp in range(3):
            force, carry = node_force(acc[comp], carry_ref[slot, comp])
            carry_ref[slot, comp] = carry
            forces.append(force)
        slot += 1
        return forces

    low = plane_modes(*planes[0], chunk)
    partial = None
    for index, modulus in enumerate(moduli):
        high = plane_modes(*planes[index + 1], chunk)
        if last_scale is not None and index + 1 == len(moduli):
            high = scaled_modes(high, last_scale)
        to_low, to_high = split_x(element_response(element_modes(low, high), modulus))
        if partial is not None:
            acc = [{p: partial[c][p] + to_low[c][p] for p in PAIRS} for c in range(3)]
            yield index, finish(acc)
        elif first_edge:
            yield index, finish(to_low)
        partial, low = to_high, high
    if last_scale is not None:
        yield len(moduli), [force * last_scale for force in finish(partial)]


def scaled_modes(modes, scale):
    return [{pair: field[pair] * scale for pair in PAIRS} for field in modes]


def has_left():
    return jnp.where(lax.axis_index("space") == 0, 0.0, 1.0).astype(F32)


def loads_kernel(
    body_hbm, fixed_hbm, node_hbm, force_hbm, load_ref, keep_ref, chip_ref, link_ref,
    body_ref, fixed_ref, node_ref, force_ref, sems,
):
    pairs = ((node_hbm, node_ref), (force_hbm, force_ref), (body_hbm, body_ref), (fixed_hbm, fixed_ref))
    copies = [pltpu.make_async_copy(src, dst, sems.at[k]) for k, (src, dst) in enumerate(pairs)]
    for copy in copies:
        copy.start()
    copies[0].wait()
    copies[1].wait()
    cells = CX * NY * NZ
    local = node_ref[...] - lax.axis_index("space") * cells
    valid = (local >= 0) & (local < cells)
    local = jnp.where(valid, local, -1)
    line = lax.shift_right_arithmetic(local, ZBITS)
    depth = lax.bitwise_and(local, NZ - 1)
    points = local.shape[1]
    on_line = row_ids((CX * NY, points)) == line
    lines = [jnp.where(on_line, force_ref[comp], 0.0) for comp in range(3)]
    at_depth = jnp.where(row_ids((NZ, points)) == depth, 1.0, 0.0)
    added = lax.dot_general(
        jnp.concatenate(lines, axis=0),
        at_depth,
        (((1,), (1,)), ((), ())),
        precision=lax.Precision.HIGHEST,
        preferred_element_type=F32,
    )
    copies[2].wait()
    copies[3].wait()
    on_even = is_even()
    for comp in range(3):
        loads, keeps = [], []
        for plane in range(CX):
            keep = 1.0 - fixed_ref[comp, plane].astype(F32)
            first = (comp * CX + plane) * NY
            loads.append(keep * (body_ref[0, comp, plane] + added[first : first + NY]))
            keeps.append(keep)
            load_ref[plane, comp] = loads[plane]
            keep_ref[plane, comp] = keep
        to_left, to_right = (loads[1], loads[0], keeps[0]), (loads[1], keeps[1], keeps[1])
        for part in range(3):
            chip_ref[part, comp] = jnp.where(on_even, to_right[part], to_left[part])
            link_ref[part, comp] = jnp.where(on_even, to_left[part], to_right[part])


def is_even():
    return lax.rem(lax.axis_index("space"), 2) == 0


def swapped(array, across):
    size = lax.axis_size("space")
    partner = lambda i: (i + (1 if (i % 2 == 0) != across else -1)) % size
    return lax.ppermute(array, "space", [(i, partner(i)) for i in range(size)])


def pack_kernel(chip_ref, own_ref, link_ref, pack_ref):
    on_even = is_even()
    for plane in range(CX):
        before = jnp.where(on_even, link_ref[plane], chip_ref[plane])
        after = jnp.where(on_even, chip_ref[plane], link_ref[plane])
        for block in range(pack_ref.shape[0]):
            pack_ref[block, plane] = before
            pack_ref[block, CX + plane] = own_ref[plane]
            pack_ref[block, 2 * CX + plane] = after


def clear_tails(refs):
    for ref in refs:
        for plane in range(ref.shape[0]):
            for comp in range(3):
                ref[plane, comp, NY : NY + ROWS] = jnp.zeros((ROWS, NZ), F32)


def clear_carry(ref):
    for plane in range(ref.shape[0]):
        for comp in range(3):
            ref[plane, comp] = jnp.zeros((ROWS, NZ), F32)


def folded(values):
    rows = [jnp.sum(v[:, :128] + v[:, 128:], axis=0, keepdims=True) for v in values]
    return jnp.concatenate(rows, axis=0)


def advance(forces, kept, before, inverse):
    image = jnp.where(kept, forces, before)
    return image, jnp.where(kept, forces * inverse, before)


def modulus_rows(e_ref, plane, chunk):
    return e_ref[plane, rows_at(chunk + 1)]


def inverse_diagonal(e_ref, plane, chunk, scale=1.0):
    last = row_ids((ROWS, NZ)) == ROWS - 1
    cur = scale * modulus_rows(e_ref, plane, chunk) + modulus_rows(e_ref, plane + 1, chunk)
    before = scale * modulus_rows(e_ref, plane, chunk - 1) + modulus_rows(e_ref, plane + 1, chunk - 1)
    cur = cur + pltpu.roll(jnp.where(last, before, cur), 1, 0)
    diag = KDIAG * (cur + from_below(cur))
    return 1.0 / jnp.where(diag > 0.0, diag, 1.0)


def first_kernel(
    load_ref, keep_ref, chip_ref, link_ref, dens_ref,
    v1_ref, v0_ref, e_ref, inv_ref, zs, zd, mom_ref,
    carry,
):
    first_x = lax.axis_index("space") * CX
    limit = lax.axis_size("space") * CX
    for plane in range(6):
        at = first_x - 2 + plane
        scale = jnp.where(at < limit, 1.0, 0.0).astype(F32)
        e_ref[plane, 0:ROWS] = jnp.zeros((ROWS, NZ), F32)
        for block in range(CHUNKS):
            dens = dens_ref[block, plane]
            rows = slice((block + 1) * ROWS, (block + 2) * ROWS)
            e_ref[plane, rows] = scale * (EMIN + (1.0 - EMIN) * (dens * dens * dens))
    clear_tails([zs, zd])
    clear_carry(carry)
    on_even = is_even()
    has_right, joined = 1.0 - end_flag(), has_left()
    zero = jnp.zeros((ROWS, NZ), F32)

    def invert(chunk, done):
        for plane in range(4):
            inverse = inverse_diagonal(e_ref, plane, chunk, joined if plane == 1 else 1.0)
            inv_ref[plane, rows_at(chunk)] = inverse
        return done

    lax.fori_loop(0, CHUNKS, invert, 0, unroll=8)

    def start(chunk, total):
        here = rows_at(chunk)
        for plane in range(4):
            inverse = inv_ref[plane, here]
            for comp in range(3):
                if plane == 0:
                    load = jnp.where(on_even, link_ref[0, comp, here], chip_ref[0, comp, here])
                elif plane == 3:
                    load = has_right * jnp.where(on_even, chip_ref[1, comp, here], link_ref[1, comp, here])
                else:
                    load = load_ref[plane - 1, comp, here]
                value = load * inverse
                if plane < 3:
                    v0_ref[plane, comp, here] = value
                if plane in (1, 2):
                    total = total + load * value
                store_z_modes(zs, zd, plane, comp, here, value)
        return total

    mom0 = lax.fori_loop(0, CHUNKS, start, zero, unroll=8)

    def apply(chunk, totals):
        here = rows_at(chunk)
        odd, even = totals
        moduli = [modulus_rows(e_ref, plane, chunk) for plane in (1, 2, 3)]
        moduli[0] = moduli[0] * joined
        for plane, forces in apply_rows([(zs, zd, k) for k in range(4)], moduli, carry, chunk):
            inverse = inv_ref[plane, here]
            for comp in range(3):
                kept = keep_ref[plane - 1, comp, here] > 0.0
                before = v0_ref[plane, comp, here]
                image, value = advance(forces[comp], kept, before, inverse)
                v1_ref[plane - 1, comp, here] = value
                odd = odd + before * image
                even = even + value * image
        return odd, even

    mom1, mom2 = lax.fori_loop(0, CHUNKS, apply, (zero, zero), unroll=CHUNKS)
    mom_ref[...] = folded([mom0, mom1, mom2] + [zero] * 5)


def middle_kernel(
    v1_ref, zs0, zd0, e_ref, inv_ref, chip_ref, link_ref, keep_ref, sofar_ref,
    v2_ref, zs1, zd1, zs2, zd2, force_ref, mom_ref,
    zs, zd, zs_far, zd_far, carry,
):
    clear_tails([zs, zd, zs1, zd1, zs2, zd2, zs_far, zd_far])
    clear_carry(carry)
    has_right, on_even = 1.0 - end_flag(), is_even()
    zero = jnp.zeros((ROWS, NZ), F32)

    def right(part, comp, here):
        return has_right * jnp.where(on_even, chip_ref[part, comp, here], link_ref[part, comp, here])

    def start(chunk, done):
        here = rows_at(chunk)
        inverse = inverse_diagonal(e_ref, 4, chunk)
        for comp in range(3):
            store_z_modes(zs, zd, 0, comp, here, right(0, comp, here) * inverse)
            store_z_modes(zs1, zd1, 0, comp, here, v1_ref[0, comp, here])
            store_z_modes(zs_far, zd_far, 0, comp, here, v1_ref[1, comp, here])
        return done

    lax.fori_loop(0, CHUNKS, start, 0, unroll=CHUNKS)

    def outer(chunk, done):
        here = rows_at(chunk)
        moduli = [modulus_rows(e_ref, plane, chunk) for plane in (3, 4)]
        planes = [(zs0, zd0, 2), (zs0, zd0, 3), (zs, zd, 0)]
        for _, forces in apply_rows(planes, moduli, carry.at[0:1], chunk):
            inverse = inv_ref[3, here]
            for comp in range(3):
                kept = right(2, comp, here) > 0.0
                before = right(1, comp, here) * inverse
                _, value = advance(forces[comp], kept, before, inverse)
                store_z_modes(zs_far, zd_far, 1, comp, here, value)
        return done

    lax.fori_loop(0, CHUNKS, outer, 0, unroll=CHUNKS)

    def apply(chunk, totals):
        here = rows_at(chunk)
        odd, even = totals
        moduli = [modulus_rows(e_ref, plane, chunk) for plane in (2, 3)]
        planes = [(zs1, zd1, 0), (zs_far, zd_far, 0), (zs_far, zd_far, 1)]
        for plane, forces in apply_rows(planes, moduli, carry.at[1:3], chunk, first_edge=True):
            if plane == 0:
                for comp in range(3):
                    force_ref[comp, here] = forces[comp]
                continue
            inverse = inv_ref[2, here]
            for comp in range(3):
                kept = keep_ref[1, comp, here] > 0.0
                before = v1_ref[1, comp, here]
                image, value = advance(forces[comp], kept, before, inverse)
                v2_ref[comp, here] = value
                store_z_modes(zs2, zd2, 0, comp, here, value)
                odd = odd + before * image
                even = even + value * image
        return odd, even

    mom3, mom4 = lax.fori_loop(0, CHUNKS, apply, (zero, zero), unroll=CHUNKS)
    mom_ref[...] = sofar_ref[...] + folded([zero] * 3 + [mom3, mom4] + [zero] * 3)


def second_kernel(
    v1_left_ref, v1_ref, chip_ref, link_ref, keep_ref, e_ref, inv_ref,
    zs1, zd1, zs2_far, zd2_far, force_ref, sofar_ref,
    v2_ref, mom_ref,
    zs, zd, zs2, zd2, carry,
):
    on_even, joined = is_even(), has_left()
    clear_tails([zs, zd, zs2, zd2])
    clear_carry(carry)
    zero = jnp.zeros((ROWS, NZ), F32)

    def start(chunk, done):
        here = rows_at(chunk)
        for plane in range(2):
            for comp in range(3):
                store_z_modes(zs, zd, plane, comp, here, v1_left_ref[plane, comp, here])
        return done

    lax.fori_loop(0, CHUNKS, start, 0, unroll=CHUNKS)

    def apply(chunk, totals):
        here = rows_at(chunk)
        odd, even = totals
        moduli = [modulus_rows(e_ref, plane, chunk) for plane in (0, 1)]
        planes = [(zs, zd, 0), (zs, zd, 1), (zs1, zd1, 0)]
        for plane, forces in apply_rows(planes, moduli, carry, chunk, last_scale=joined):
            inverse = inv_ref[plane - 1, here]
            for comp in range(3):
                if plane == 1:
                    keep = jnp.where(on_even, link_ref[1, comp, here], chip_ref[1, comp, here])
                    kept, before = keep > 0.0, v1_left_ref[1, comp, here]
                    force = forces[comp]
                else:
                    kept, before = keep_ref[0, comp, here] > 0.0, v1_ref[0, comp, here]
                    force = forces[comp] + force_ref[comp, here]
                image, value = advance(force, kept, before, inverse)
                v2_ref[plane - 1, comp, here] = value
                store_z_modes(zs2, zd2, plane - 1, comp, here, value)
                if plane == 2:
                    odd = odd + before * image
                    even = even + value * image
        return odd, even

    mom3, mom4 = lax.fori_loop(0, CHUNKS, apply, (zero, zero), unroll=CHUNKS)

    def last(chunk, total):
        for plane, energy in enumerate(energies(zs2, zd2, (zs2_far, zd2_far, 0), joined, chunk)):
            total = total + modulus_rows(e_ref, 1 + plane, chunk) * energy
        return total

    mom5 = lax.fori_loop(0, CHUNKS, last, zero, unroll=CHUNKS)
    total = sofar_ref[...] + folded([zero] * 3 + [mom3, mom4, mom5] + [zero] * 2)
    for device in range(mom_ref.shape[0]):
        mom_ref[device] = total


def end_flag():
    at_end = lax.axis_index("space") == lax.axis_size("space") - 1
    return jnp.where(at_end, 1.0, 0.0).astype(F32)


def energies(zs, zd, last_plane, joined, chunk):
    low, here, high = [
        plane_modes(*where, chunk) for where in ((zs, zd, 0), (zs, zd, 1), last_plane)
    ]
    yield element_energy(element_modes(low, scaled_modes(here, joined)))
    yield element_energy(element_modes(here, high))


def energy_kernel(v0_ref, v1_left_ref, v1_ref, v2_ref, v2_far_ref, mom_ref, u_ref, out_ref, zs, zd, e_ref):
    total = mom_ref[0]
    for device in range(1, mom_ref.shape[0]):
        total = total + mom_ref[device]
    total = jnp.broadcast_to(jnp.sum(total, axis=1, keepdims=True), (8, 128))
    m0, m1, m2, m3, m4, m5 = [total[k : k + 1] for k in range(6)]
    low10 = m2 / m1
    low20 = m3 / m1
    piv1 = m3 - low10 * m2
    mix = m4 - low20 * m2
    good1 = piv1 > 1e-7 * m3
    safe1 = jnp.where(good1, piv1, 1.0)
    low21 = jnp.where(good1, mix / safe1, 0.0)
    piv2 = m5 - low20 * m3 - low21 * mix
    good2 = good1 & (piv2 > 1e-7 * m5)
    y1 = m1 - low10 * m0
    y2 = m2 - low20 * m0 - low21 * y1
    c2 = jnp.where(good2, y2 / jnp.where(good2, piv2, 1.0), 0.0)
    c1 = jnp.where(good1, y1 / safe1 - low21 * c2, 0.0)
    c0 = m0 / m1 - low10 * c1 - low20 * c2
    c0, c1, c2 = [jnp.broadcast_to(jnp.concatenate([c, c], axis=1), (ROWS, NZ)) for c in (c0, c1, c2)]

    clear_tails([zs, zd])
    for plane in range(2):
        e_ref[plane, 0:ROWS] = jnp.zeros((ROWS, NZ), F32)
        e_ref[plane, NY + ROWS : NY + 2 * ROWS] = jnp.zeros((ROWS, NZ), F32)
    v1_planes = [v1_left_ref.at[1], v1_ref.at[0], v1_ref.at[1]]
    v2_planes = [v2_ref.at[0], v2_ref.at[1], v2_far_ref]

    def combine(chunk, done):
        here = rows_at(chunk)
        for plane in range(3):
            for comp in range(3):
                value = c0 * v0_ref[plane, comp, here] + c1 * v1_planes[plane][comp, here]
                value = value + c2 * v2_planes[plane][comp, here]
                if plane > 0:
                    u_ref[comp, plane - 1, here] = value
                store_z_modes(zs, zd, plane, comp, here, value)
        return done

    lax.fori_loop(0, CHUNKS, combine, 0, unroll=CHUNKS)
    joined = has_left()

    def measure(chunk, done):
        for plane, energy in enumerate(energies(zs, zd, (zs, zd, 2), joined, chunk)):
            e_ref[plane, rows_at(chunk + 1)] = energy
        return done

    lax.fori_loop(0, CHUNKS, measure, 0, unroll=CHUNKS)
    span = ROWS + 2
    for block in range(CHUNKS):
        for plane in range(2):
            first = ROWS - 1 + block * ROWS
            out_ref[block, plane * span : (plane + 1) * span] = e_ref[plane, first : first + span]


def weigh(planes):
    near = RADIUS - 1.0
    edge = RADIUS - math.sqrt(2.0)
    beside = [from_below(p) + from_above(p) for p in planes]
    cross = []
    full = []
    for p, side in zip(planes, beside):
        up_down = p[0:ROWS] + p[2 : 2 + ROWS]
        mid, mid_side = p[1 : 1 + ROWS], side[1 : 1 + ROWS]
        cross.append(near * mid + edge * (mid_side + up_down))
        diagonal = side[0:ROWS] + side[2 : 2 + ROWS]
        full.append(RADIUS * mid + near * (mid_side + up_down) + edge * diagonal)
    return [full[k] + cross[k - 1] + cross[k + 1] for k in range(1, 1 + CX)]


def filter_kernel(energy_ref, next_ref, dens_ref, out_ref):
    space, load = lax.axis_index("space"), lax.axis_index("load")
    n_space, n_load = lax.axis_size("space"), lax.axis_size("load")
    span = ROWS + 2
    part = lambda ref, k: ref[k * span : (k + 1) * span]
    total = [part(ref, k) for ref in (energy_ref, next_ref) for k in range(2)]
    before = jnp.maximum(load - 1, 0)
    after = jnp.minimum(load + 1, n_load - 1)
    at_y = load * ROWS - 1 + row_ids((span, NZ))
    in_y = (at_y >= 0) & (at_y < n_load * ROWS)
    weighted, inside, own = [], [], []
    for plane in range(4):
        dens = jnp.concatenate(
            [
                dens_ref[before, 1 + plane][ROWS - 1 : ROWS],
                dens_ref[load, 1 + plane],
                dens_ref[after, 1 + plane][0:1],
            ],
            axis=0,
        )
        at_x = space * CX - 1 + plane
        scale = jnp.where((at_x >= 0) & (at_x < n_space * CX), 1.0, 0.0).astype(F32)
        present = scale * jnp.where(in_y, 1.0, 0.0)
        sensitivity = -PENALTY * (1.0 - EMIN) * (dens * dens) * total[plane]
        weighted.append(present * (dens * sensitivity))
        inside.append(present)
        if 1 <= plane <= CX:
            own.append(dens[1 : 1 + ROWS])
    sums, counts = weigh(weighted), weigh(inside)
    for plane in range(CX):
        out_ref[plane] = sums[plane] / (own[plane] * counts[plane])


def shifted(array, axis, distance):
    size = lax.axis_size(axis)
    return lax.ppermute(array, axis, [(i, (i + distance) % size) for i in range(size)])


def body(density, fixed_dofs, body_loads, point_nodes, point_forces):
    n_load, n_space = lax.axis_size("load"), lax.axis_size("space")
    dens_chip = swapped(density, False)
    dens_link = swapped(density, True)
    plane = (3, NY, NZ)
    by_component = jnp.swapaxes(point_forces, 0, 1)
    load, keep, to_chip, to_link = kernel_call(
        loads_kernel,
        [(2,) + plane, (2,) + plane, (3,) + plane, (3,) + plane],
        4,
        0,
        [
            pltpu.VMEM(body_loads.shape, F32),
            pltpu.VMEM(fixed_dofs.shape, jnp.int32),
            pltpu.VMEM(point_nodes.shape, jnp.int32),
            pltpu.VMEM(by_component.shape, F32),
            pltpu.SemaphoreType.DMA((4,)),
        ],
    )(*[pltpu.with_memory_space_constraint(x, pltpu.HBM) for x in (body_loads, fixed_dofs, point_nodes, by_component)])
    (dens,) = kernel_call(pack_kernel, [(n_load, 3 * CX, ROWS, NZ)], 0, 3)(
        dens_chip, density, dens_link
    )
    dens, to_chip = lax.optimization_barrier((dens, to_chip))
    chip = swapped(to_chip, False)
    link = swapped(to_link, True)
    dens = lax.all_to_all(dens, "load", 0, 0)

    padded = (NY + ROWS, NZ)
    modes = lambda planes: (planes, 3) + padded
    zed = lambda planes: pltpu.VMEM(modes(planes), F32)
    carried = lambda slots: pltpu.VMEM((slots, 3, ROWS, NZ), F32)
    v1, v0, modulus, inverse, zs0, zd0, mom = kernel_call(
        first_kernel,
        [(2,) + plane, (3,) + plane, (6,) + padded, (4, NY, NZ), modes(4), modes(4), (8, 128)],
        0,
        5,
        [carried(2)],
    )(load, keep, chip, link, dens)
    v1_left = shifted(v1, "space", 1)
    v2_far, zs1, zd1, zs2, zd2, force, mom = kernel_call(
        middle_kernel,
        [plane, modes(1), modes(1), modes(1), modes(1), plane, (8, 128)],
        0,
        9,
        [zed(1), zed(1), zed(2), zed(2), carried(3)],
    )(v1, zs0, zd0, modulus, inverse, chip, link, keep, mom)
    v2, mom = kernel_call(
        second_kernel,
        [(2,) + plane, (n_space, 8, 128)],
        0,
        13,
        [zed(2), zed(2), zed(2), zed(2), carried(2)],
    )(v1_left, v1, chip, link, keep, modulus, inverse, zs1, zd1, zs2, zd2, force, mom)
    mom = lax.all_to_all(mom, "space", 0, 0)
    span = ROWS + 2
    moved, energy = kernel_call(
        energy_kernel,
        [(3, CX, NY, NZ), (CHUNKS, 2 * span, NZ)],
        0,
        6,
        [zed(3), zed(3), pltpu.VMEM((2, NY + 2 * ROWS, NZ), F32)],
    )(v0, v1_left, v1, v2, v2_far, mom)
    energy = jnp.sum(lax.all_to_all(energy, "load", 0, 0), axis=0)
    following = shifted(energy, "space", -1)
    (filtered,) = kernel_call(filter_kernel, [(CX, ROWS, NZ)], 0, 3)(energy, following, dens)
    return (moved[None], filtered)


def solution(mesh):
    placed = (
        P("space", "load", None),
        P(None, "space", None, None),
        P("load", None, "space", None, None),
        P("load", None),
        P("load", None, None),
    )
    return jax.shard_map(
        body,
        mesh=mesh,
        in_specs=placed,
        out_specs=(P("load", None, "space", None, None), P("space", "load", None)),
        check_vma=False,
    )
```
